512 devices in a mesh: space: 128 (over x, z, core), col: 4 (over y).
Axes of the slice: x: 4, y: 4, z: 16, core: 2. Of those that a mesh axis runs over, the one named last changes fastest.
Arguments:
- panel: float32 [128, 983040], P(None, ('space', 'col')), may hold values from -6 to 1008
- trailing: float32 [256, 983040], P('col', 'space'), may hold values from -6 to 6
Outputs:
- upper_factor: float32 [128, 128], replicated
- updated: float32 [256, 983040], P('col', 'space')
The draws below stay inside these ranges and needn't reach their ends.
All inputs are finite; a program needn't handle non-finite values.
Results may differ from the reference program's by a relative error of at most 0.00007.
Values sent between devices are 32-bit elements; how exact they have to be, the bound alone decides.
A program may use at most 64 MiB of HBM per device.

```python
import math
import jax
import jax.numpy as jnp
from jax import lax

B = 128
TRAIL = 256
ROWS_DEV = 7680
ROWS = 983040


def common_field(key, growth, mode_size):
    keys = jax.random.split(key, 4)
    position = jnp.arange(ROWS, dtype=jnp.float32) / ROWS
    gauss = jax.random.normal(keys[0], (B, ROWS), jnp.float32)
    noise = gauss
    row_scale = jnp.sqrt(1.0 + growth * position)
    modes = jax.random.normal(keys[2], (3, ROWS), jnp.float32)
    amounts = jax.random.uniform(keys[3], (B, 3), jnp.float32, -1.0, 1.0) * mode_size
    values = noise * row_scale[None, :]
    values = values + amounts[:, 0:1] * modes[0:1, :]
    values = values + amounts[:, 1:2] * modes[1:2, :]
    values = values + amounts[:, 2:3] * modes[2:3, :]
    return jnp.clip(values, -6.0, 6.0)


def draw_panel(key, part):
    values = common_field(key, 2.0, 0.3)
    key = jax.random.fold_in(key, 11)
    keys = jax.random.split(key, 2)
    space_count = ROWS // ROWS_DEV
    ceiling = float(min(ROWS_DEV, 2 * space_count + ROWS_DEV // 4, 6 * space_count + ROWS_DEV // 32))
    lift = jax.random.uniform(keys[0], (B,), jnp.float32, 0.5, 1.0) * ceiling
    top_member = jax.random.randint(keys[1], (), 0, B)
    members_line = jnp.arange(B, dtype=jnp.int32)
    lift = jnp.where(members_line == top_member, ceiling, lift)
    columns = jnp.arange(ROWS, dtype=jnp.int32)[None, :]
    members = members_line[:, None]
    values = jnp.where(columns == members, lift[:, None], values)
    return values.astype(jnp.float32)


def draw_trailing(key, part):
    shared = common_field(key, 2.0, 0.3)
    amp_low, amp_high = (0.3, 0.7)
    key = jax.random.fold_in(key, 23)
    keys = jax.random.split(key, 7)
    fresh = jax.random.normal(keys[0], (TRAIL, ROWS), jnp.float32)
    amplitude = jax.random.uniform(keys[1], (TRAIL, 1), jnp.float32, amp_low, amp_high)
    coefficient = jax.random.uniform(keys[2], (TRAIL, 4), jnp.float32, -0.6, 0.6)
    owners = jnp.arange(TRAIL, dtype=jnp.int32) % B
    total = fresh
    for member in range(4):
        order = jax.random.permutation(keys[3 + member], B).astype(jnp.int32)
        chosen = order[owners]
        total = total + amplitude * coefficient[:, member:member + 1] * shared[chosen]
    return jnp.clip(total, -6.0, 6.0).astype(jnp.float32)


def setup_inputs(seed: int = 0) -> dict:
    streams_of = jax.random.split(jax.random.key(seed), 3)
    panel = draw_panel(jax.random.fold_in(streams_of[2], 71), 0)
    trailing = draw_trailing(jax.random.fold_in(streams_of[2], 71), 0)
    return {"panel": panel, "trailing": trailing}


highest = lax.Precision.HIGHEST

def reference(panel, trailing):
    gram = jnp.dot(panel, panel.T, precision=highest)
    lower_factor = jnp.linalg.cholesky(gram)
    scaled = jax.scipy.linalg.solve_triangular(lower_factor, panel, lower=True)
    identity = jnp.eye(B, dtype=jnp.float32)
    basis = scaled.at[:, :B].add(identity)
    kernel_matrix = identity + scaled[:, :B].T
    coupling = jnp.dot(basis, trailing.T, precision=highest)
    weights = jnp.linalg.solve(kernel_matrix, coupling)
    updated = trailing - jnp.dot(weights.T, basis, precision=highest)
    upper_factor = -lower_factor.T / math.sqrt(ROWS)
    return (upper_factor, updated)
```

```python
import functools
import math

import jax
import jax.numpy as jnp
from jax import lax
from jax.experimental import pallas as pl
from jax.experimental.pallas import tpu as pltpu
from jax.sharding import PartitionSpec as P

F32 = jnp.float32
BF16 = jnp.bfloat16
HIGHEST = lax.Precision.HIGHEST
MESH = pl.DeviceIdType.MESH
NX, NZ, NCORE, NY = 4, 16, 2, 4
PLANE = NX * NY * NCORE
PAIRS = NX * NCORE
BLK = 8


def split2(x):
    high = x.astype(BF16)
    low = (x - high.astype(F32)).astype(BF16)
    return high, low


def split3(x):
    high = x.astype(BF16).astype(F32)
    rest = x - high
    mid = rest.astype(BF16).astype(F32)
    return high, mid, rest - mid


def stacks(a, b):
    ah, am, al = split3(a)
    bh, bm, bl = split3(b)
    left = jnp.concatenate([ah, ah, ah, am, am, al], axis=0).astype(BF16)
    right = jnp.concatenate([bh, bm, bl, bh, bm, bh], axis=0).astype(BF16)
    return left, right


def dot_tn(a, b):
    return lax.dot_general(a, b, (((0,), (0,)), ((), ())), preferred_element_type=F32)


def dot_nt(a, b):
    return lax.dot_general(a, b, (((1,), (1,)), ((), ())), preferred_element_type=F32)


def recip(x):
    y = pl.reciprocal(x, approx=True)
    return y * (2.0 - x * y)


def lane_splat(x, lane):
    return jnp.take_along_axis(x, jnp.full(x.shape, lane, jnp.int32), axis=1)


def merge(rows, row8):
    out = rows[0]
    for i in range(1, len(rows)):
        out = jnp.where(row8 == i, rows[i], out)
    return out


def block_rows(ref, base):
    width = ref.shape[1]
    return [jnp.broadcast_to(ref[pl.ds(base + i, 1), :], (BLK, width)) for i in range(BLK)]


def chol_step(k, work, upper):
    width = work.shape[1]
    row8 = lax.broadcasted_iota(jnp.int32, (BLK, width), 0)
    lane8 = lax.broadcasted_iota(jnp.int32, (BLK, width), 1)
    base = pl.multiple_of(k * BLK, BLK)
    rows = block_rows(work, base)
    s = {(i, j): lane_splat(rows[i], base + j) for i in range(BLK) for j in range(i, BLK)}
    for j in range(BLK):
        inv = recip(s[j, j])
        for i in range(j + 1, BLK):
            factor = s[j, i] * inv
            for l in range(i, BLK):
                s[i, l] = s[i, l] - factor * s[j, l]
            rows[i] = rows[i] - factor * rows[j]
    pivots = merge([s[j, j] for j in range(BLK)], row8)
    block = merge(rows, row8) * lax.rsqrt(pivots)
    block = jnp.where(lane8 >= row8 + base, block, 0.0)
    upper[pl.ds(base, BLK), :] = block
    left, right = stacks(block, block)
    work[...] -= dot_tn(left, right)


def inverse_step(k, mat, mat_t):
    width = mat.shape[1]
    row8 = lax.broadcasted_iota(jnp.int32, (BLK, width), 0)
    lane8 = lax.broadcasted_iota(jnp.int32, (BLK, width), 1)
    base = pl.multiple_of(k * BLK, BLK)
    rows = block_rows(mat, base)
    cols = mat_t[pl.ds(base, BLK), :]
    s = {(i, j): lane_splat(rows[i], base + j) for i in range(BLK) for j in range(BLK)}
    for j in range(BLK):
        inv = recip(s[j, j])
        at = lane8 == base + j
        scaled = jnp.where(at, 1.0, rows[j]) * inv
        for l in range(j + 1, BLK):
            s[j, l] = s[j, l] * inv
        for i in range(BLK):
            if i == j:
                continue
            for l in range(j + 1, BLK):
                s[i, l] = s[i, l] - s[i, j] * s[j, l]
            rows[i] = jnp.where(at, 0.0, rows[i]) - s[i, j] * scaled
        rows[j] = scaled
    block = merge(rows, row8)
    inside = (lane8 >= base) & (lane8 < base + BLK)
    cols = jnp.where(inside, jnp.where(lane8 == row8 + base, -1.0, 0.0), cols)
    left, right = stacks(cols, block)
    row_id = lax.broadcasted_iota(jnp.int32, (width, width), 0)
    lane_id = lax.broadcasted_iota(jnp.int32, (width, width), 1)
    row_out = (row_id < base) | (row_id >= base + BLK)
    lane_out = (lane_id < base) | (lane_id >= base + BLK)
    keep = row_out & lane_out
    mat[...] = jnp.where(keep, mat[...], 0.0) - dot_tn(left, right)
    mat_t[...] = jnp.where(keep, mat_t[...], 0.0) - dot_tn(right, left)


def main_kernel(p_hbm, t_hbm, gat_out, upper, zt,
                gat, tv, g_loc, zr, pr, gf, p1t, p1f, m_loc, mr, mz, zsum, work, work_t,
                gp_send, gp_recv, loc, out_sem, st_send, st_recv):
    width, part = p_hbm.shape
    half = width // 2
    space = lax.axis_index("space")
    y = lax.axis_index("col")
    core = space % NCORE
    z = (space // NCORE) % NZ
    x = space // (NCORE * NZ)
    pair = x * NCORE + core
    plane = pair * NY + y
    right, left, far = (y + 1) % NY, (y + NY - 1) % NY, (y + 2) % NY

    def at_z(zz):
        return (x * (NZ * NCORE) + zz * NCORE + core, y)

    def at_plane(q):
        px = q // (NCORE * NY)
        pc = (q // NY) % NCORE
        return (px * (NZ * NCORE) + z * NCORE + pc, q % NY)

    def at_pair(q):
        return ((q // NCORE) * (NZ * NCORE) + z * NCORE + q % NCORE, y)

    def loop(low, high, body):
        lax.fori_loop(low, high, lambda i, c: (body(i), c)[1], 0)

    def send(src, dst, stage, device):
        pltpu.make_async_remote_copy(
            src_ref=src, dst_ref=dst, send_sem=st_send.at[stage], recv_sem=st_recv.at[stage],
            device_id=device, device_id_type=MESH).start()

    def settle(ref, sem):
        pltpu.make_async_copy(ref, ref, sem).wait()

    def rows8(i):
        return pl.ds(pl.multiple_of(i * BLK, BLK), BLK)

    barrier = pltpu.get_barrier_semaphore()

    def greet(device):
        pl.semaphore_signal(barrier, inc=1, device_id=device, device_id_type=MESH)

    own = pltpu.make_async_copy(p_hbm, gat.at[y], loc.at[0])
    own.start()
    loads = [pltpu.make_async_copy(t_hbm.at[:, pl.ds(c * part, part)], tv.at[c], loc.at[1 + c])
             for c in range(NY)]
    for load in loads:
        load.start()
    loop(1, PLANE, lambda d: greet(at_plane((plane + d) % PLANE)))
    loop(1, NZ, lambda d: greet(at_z((z + d) % NZ)))
    pl.semaphore_wait(barrier, PLANE + NZ - 2)

    first, second = pl.ds(0, half), pl.ds(half, half)

    def gather_copy(src, dst, index, target):
        return pltpu.make_async_remote_copy(
            src_ref=src, dst_ref=dst, send_sem=gp_send.at[index], recv_sem=gp_recv.at[index],
            device_id=(space, target), device_id_type=MESH)

    ra = gather_copy(p_hbm.at[first], gat.at[y, first], 0, right)
    lb = gather_copy(p_hbm.at[second], gat.at[y, second], 1, left)
    rb = gather_copy(p_hbm.at[second], gat.at[y, second], 2, right)
    la = gather_copy(p_hbm.at[first], gat.at[y, first], 3, left)
    for copy in (ra, lb, rb, la):
        copy.start()
    own.wait()
    high, low = split2(gat[y])
    both = dot_nt(high, jnp.concatenate([high, low], axis=0))
    cross = both[:, width:]
    g_loc[...] = both[:, :width] + cross + cross.T

    loop(1, NZ, lambda d: send(g_loc.at[rows8((z + d) % NZ)], zr.at[d - 1], 0, at_z((z + d) % NZ)))

    @pl.when((plane == 0) & (z == 0))
    def _():
        loop(1, NZ, lambda d: send(gat.at[0, rows8(d), pl.ds(0, width)], p1t, 3, at_z(d)))
        p1t[...] = gat[0, 0:BLK, 0:width]

    settle(zr, st_recv.at[0])
    total = g_loc[rows8(z), :]
    for d in range(NZ - 1):
        total = total + zr[d]
    pr[plane] = total
    loop(1, PLANE, lambda d: send(pr.at[plane], pr.at[plane], 1, at_plane((plane + d) % PLANE)))

    @pl.when((plane == 0) & (z > 0))
    def _():
        settle(p1t, st_recv.at[3])

    @pl.when(plane == 0)
    def _():
        loop(1, PLANE, lambda d: send(p1t, p1t, 4, at_plane(d)))

    settle(pr.at[pl.ds(0, PLANE - 1)], st_recv.at[1])
    total = pr[0]
    for q in range(1, PLANE):
        total = total + pr[q]
    gf[rows8(z), :] = total
    loop(1, NZ, lambda d: send(gf.at[rows8(z)], gf.at[rows8(z)], 2, at_z((z + d) % NZ)))

    @pl.when(plane > 0)
    def _():
        settle(p1t, st_recv.at[4])

    p1f[rows8(z), :] = p1t[...]
    loop(1, NZ, lambda d: send(p1f.at[rows8(z)], p1f.at[rows8(z)], 5, at_z((z + d) % NZ)))

    settle(gf.at[pl.ds(0, (NZ - 1) * BLK)], st_recv.at[2])
    work[...] = gf[...]
    ra.wait_recv()
    fa = gather_copy(gat.at[left, first], gat.at[left, first], 4, right)
    fa.start()
    lb.wait_recv()
    fb = gather_copy(gat.at[right, second], gat.at[right, second], 5, left)
    fb.start()
    loop(0, width // BLK, lambda k: chol_step(k, work, upper))

    settle(p1f.at[pl.ds(0, (NZ - 1) * BLK)], st_recv.at[5])
    work[...] = gf[...] + jnp.dot(p1f[...], upper[...], precision=HIGHEST, preferred_element_type=F32)
    work_t[...] = work[...].T
    loop(0, width // BLK, lambda k: inverse_step(k, work, work_t))

    for load in loads:
        load.wait()

    def products(c):
        ph, pl_ = split2(gat[c])
        th, tl = split2(tv[c])
        four = dot_nt(jnp.concatenate([th, tl], axis=0), jnp.concatenate([ph, pl_], axis=0))
        rows = th.shape[0]
        return (four[:rows, :width] + four[rows:, :width]) + (four[:rows, width:] + four[rows:, width:])

    def put_out(c, index):
        copy = pltpu.make_async_copy(gat.at[c], gat_out.at[c], out_sem.at[index])
        copy.start()
        return copy

    m_loc[...] = products(y)
    outs = [put_out(y, 0)]

    @pl.when(space == 0)
    def _():
        m_loc[...] += jnp.dot(tv[0, :, 0:width], upper[...], precision=HIGHEST,
                              preferred_element_type=F32)

    rb.wait_recv()
    m_loc[...] += products(left)
    outs.append(put_out(left, 1))
    la.wait_recv()
    m_loc[...] += products(right)
    outs.append(put_out(right, 2))
    fa.wait_recv()
    fb.wait_recv()
    m_loc[...] += products(far)
    outs.append(put_out(far, 3))

    loop(1, PAIRS, lambda d: send(m_loc.at[rows8((pair + d) % PAIRS)], mr.at[d - 1], 6,
                                  at_pair((pair + d) % PAIRS)))
    settle(mr, st_recv.at[6])
    total = m_loc[rows8(pair), :]
    for d in range(PAIRS - 1):
        total = total + mr[d]
    mz[z] = total
    loop(1, NZ, lambda d: send(mz.at[z], mz.at[z], 7, at_z((z + d) % NZ)))
    settle(mz.at[pl.ds(0, NZ - 1)], st_recv.at[7])
    total = mz[0]
    for q in range(1, NZ):
        total = total + mz[q]
    zsum[rows8(pair), :] = jnp.dot(total, work[...], precision=HIGHEST, preferred_element_type=F32)
    loop(1, PAIRS, lambda d: send(zsum.at[rows8(pair)], zsum.at[rows8(pair)], 8,
                                  at_pair((pair + d) % PAIRS)))
    settle(zsum.at[pl.ds(0, (PAIRS - 1) * BLK)], st_recv.at[8])
    zt[...] = zsum[...]

    for copy in (ra, lb, rb, la, fa, fb):
        copy.wait_send()
    for copy in outs:
        copy.wait()
    settle(zr, st_send.at[0])
    settle(pr.at[pl.ds(0, PLANE - 1)], st_send.at[1])
    settle(gf.at[pl.ds(0, (NZ - 1) * BLK)], st_send.at[2])

    @pl.when((plane == 0) & (z == 0))
    def _():
        settle(gf.at[pl.ds(0, (NZ - 1) * BLK)], st_send.at[3])

    @pl.when(plane == 0)
    def _():
        settle(pr.at[pl.ds(0, PLANE - 1)], st_send.at[4])

    settle(gf.at[pl.ds(0, (NZ - 1) * BLK)], st_send.at[5])
    settle(mr, st_send.at[6])
    settle(mz.at[pl.ds(0, NZ - 1)], st_send.at[7])
    settle(mr, st_send.at[8])


def update_kernel(scale, p_ref, t_ref, zt_ref, upper_ref, up_ref, out_ref):
    zt = zt_ref[...]
    rows = zt.shape[0]
    width = zt.shape[1]
    zh, zl = split2(zt)
    ph, pl_ = split2(p_ref[0])
    double = jnp.dot(jnp.concatenate([zh, zl], axis=0), ph, preferred_element_type=F32)
    cross = jnp.dot(zh, pl_, preferred_element_type=F32)
    out_ref[...] = t_ref[...] - (double[:rows] + (double[rows:] + cross))

    @pl.when(pl.program_id(0) == 0)
    def _():
        up_ref[...] = upper_ref[...] * scale

    @pl.when((pl.program_id(0) == 0) & (lax.axis_index("space") == 0))
    def _():
        out_ref[:, 0:width] -= lax.dot_general(
            zt, upper_ref[...], (((1,), (1,)), ((), ())), precision=HIGHEST,
            preferred_element_type=F32)


def per_device(panel, trailing):
    width, part = panel.shape
    rows, block = trailing.shape
    rows_total = block * lax.axis_size("space")
    vmem = pl.BlockSpec(memory_space=pltpu.VMEM)
    hbm = pl.BlockSpec(memory_space=pl.ANY)

    def buf(*shape):
        return pltpu.VMEM(shape, F32)

    gat, upper, zt = pl.pallas_call(
        main_kernel,
        out_shape=(
            jax.ShapeDtypeStruct((NY, width, part), F32),
            jax.ShapeDtypeStruct((width, width), F32),
            jax.ShapeDtypeStruct((rows, width), F32),
        ),
        in_specs=[hbm, hbm],
        out_specs=(hbm, vmem, vmem),
        scratch_shapes=[
            buf(NY, width, part),
            buf(NY, rows, part),
            buf(width, width),
            buf(NZ - 1, BLK, width),
            buf(PLANE, BLK, width),
            buf(width, width),
            buf(BLK, width),
            buf(width, width),
            buf(rows, width),
            buf(PAIRS - 1, BLK, width),
            buf(NZ, BLK, width),
            buf(rows, width),
            buf(width, width),
            buf(width, width),
            pltpu.SemaphoreType.DMA((6,)),
            pltpu.SemaphoreType.DMA((6,)),
            pltpu.SemaphoreType.DMA((1 + NY,)),
            pltpu.SemaphoreType.DMA((NY,)),
            pltpu.SemaphoreType.DMA((9,)),
            pltpu.SemaphoreType.DMA((9,)),
        ],
        compiler_params=pltpu.CompilerParams(
            collective_id=0, has_side_effects=True, vmem_limit_bytes=40 * 2**20),
        name="reduce_factor",
    )(panel, trailing)

    upper_factor, updated = pl.pallas_call(
        functools.partial(update_kernel, -1.0 / math.sqrt(rows_total)),
        grid=(NY,),
        out_shape=(
            jax.ShapeDtypeStruct((width, width), F32),
            jax.ShapeDtypeStruct((rows, block), F32),
        ),
        in_specs=[
            pl.BlockSpec((1, width, part), lambda i: (i, 0, 0)),
            pl.BlockSpec((rows, part), lambda i: (0, i)),
            pl.BlockSpec((rows, width), lambda i: (0, 0)),
            pl.BlockSpec((width, width), lambda i: (0, 0)),
        ],
        out_specs=(
            pl.BlockSpec((width, width), lambda i: (0, 0)),
            pl.BlockSpec((rows, part), lambda i: (0, i)),
        ),
        compiler_params=pltpu.CompilerParams(vmem_limit_bytes=40 * 2**20),
        name="apply_update",
    )(gat, trailing, zt, upper)
    return (upper_factor, updated)


def solution(mesh):
    return jax.shard_map(
        per_device,
        mesh=mesh,
        in_specs=(P(None, ("space", "col")), P("col", "space")),
        out_specs=(P(), P("col", "space")),
        check_vma=False,
    )
```

```python
import functools
import math

import jax
import jax.numpy as jnp
from jax import lax
from jax.experimental import pallas as pl
from jax.experimental.pallas import tpu as pltpu
from jax.sharding import PartitionSpec as P

F32 = jnp.float32
BF16 = jnp.bfloat16
HIGHEST = lax.Precision.HIGHEST
MESH = pl.DeviceIdType.MESH
NX, NZ, NCORE, NY = 4, 16, 2, 4
PLANE = NX * NY * NCORE
PAIRS = NX * NCORE
BLK = 8
PIECE = 16


def split2(x):
    high = x.astype(BF16)
    low = (x - high.astype(F32)).astype(BF16)
    return high, low


def split3(x):
    high = x.astype(BF16).astype(F32)
    rest = x - high
    mid = rest.astype(BF16).astype(F32)
    return high, mid, rest - mid


def stacks(a, b):
    ah, am, al = split3(a)
    bh, bm, bl = split3(b)
    left = jnp.concatenate([ah, ah, ah, am, am, al], axis=0).astype(BF16)
    right = jnp.concatenate([bh, bm, bl, bh, bm, bh], axis=0).astype(BF16)
    return left, right


def dot_tn(a, b):
    return lax.dot_general(a, b, (((0,), (0,)), ((), ())), preferred_element_type=F32)


def dot_nt(a, b):
    return lax.dot_general(a, b, (((1,), (1,)), ((), ())), preferred_element_type=F32)


def recip(x):
    y = pl.reciprocal(x, approx=True)
    return y * (2.0 - x * y)


def lane_splat(x, lane):
    return jnp.take_along_axis(x, jnp.full(x.shape, lane, jnp.int32), axis=1)


def merge(rows, row8):
    out = rows[0]
    for i in range(1, len(rows)):
        out = jnp.where(row8 == i, rows[i], out)
    return out


def block_rows(ref, base):
    width = ref.shape[1]
    return [jnp.broadcast_to(ref[pl.ds(base + i, 1), :], (BLK, width)) for i in range(BLK)]


def chol_step(k, work, upper):
    width = work.shape[1]
    row8 = lax.broadcasted_iota(jnp.int32, (BLK, width), 0)
    lane8 = lax.broadcasted_iota(jnp.int32, (BLK, width), 1)
    base = pl.multiple_of(k * BLK, BLK)
    rows = block_rows(work, base)
    s = {(i, j): lane_splat(rows[i], base + j) for i in range(BLK) for j in range(i, BLK)}
    for j in range(BLK):
        inv = recip(s[j, j])
        for i in range(j + 1, BLK):
            factor = s[j, i] * inv
            for l in range(i, BLK):
                s[i, l] = s[i, l] - factor * s[j, l]
            rows[i] = rows[i] - factor * rows[j]
    pivots = merge([s[j, j] for j in range(BLK)], row8)
    block = merge(rows, row8) * lax.rsqrt(pivots)
    block = jnp.where(lane8 >= row8 + base, block, 0.0)
    upper[pl.ds(base, BLK), :] = block
    left, right = stacks(block, block)
    work[...] -= dot_tn(left, right)


def inverse_step(k, mat, mat_t):
    width = mat.shape[1]
    row8 = lax.broadcasted_iota(jnp.int32, (BLK, width), 0)
    lane8 = lax.broadcasted_iota(jnp.int32, (BLK, width), 1)
    base = pl.multiple_of(k * BLK, BLK)
    rows = block_rows(mat, base)
    cols = mat_t[pl.ds(base, BLK), :]
    s = {(i, j): lane_splat(rows[i], base + j) for i in range(BLK) for j in range(BLK)}
    for j in range(BLK):
        inv = recip(s[j, j])
        at = lane8 == base + j
        scaled = jnp.where(at, 1.0, rows[j]) * inv
        for l in range(j + 1, BLK):
            s[j, l] = s[j, l] * inv
        for i in range(BLK):
            if i == j:
                continue
            for l in range(j + 1, BLK):
                s[i, l] = s[i, l] - s[i, j] * s[j, l]
            rows[i] = jnp.where(at, 0.0, rows[i]) - s[i, j] * scaled
        rows[j] = scaled
    block = merge(rows, row8)
    inside = (lane8 >= base) & (lane8 < base + BLK)
    cols = jnp.where(inside, jnp.where(lane8 == row8 + base, -1.0, 0.0), cols)
    left, right = stacks(cols, block)
    row_id = lax.broadcasted_iota(jnp.int32, (width, width), 0)
    lane_id = lax.broadcasted_iota(jnp.int32, (width, width), 1)
    row_out = (row_id < base) | (row_id >= base + BLK)
    lane_out = (lane_id < base) | (lane_id >= base + BLK)
    keep = row_out & lane_out
    mat[...] = jnp.where(keep, mat[...], 0.0) - dot_tn(left, right)
    mat_t[...] = jnp.where(keep, mat_t[...], 0.0) - dot_tn(right, left)


def main_kernel(p_hbm, t_hbm, gat_out, upper, zt,
                gat, tv, g_loc, pr, gz, gf, p1s, p1f, m_loc, mr, mz, zsum, work, work_t,
                gp_send, gp_recv, loc, out_sem, st_send, st_recv):
    width, part = p_hbm.shape
    half = width // 2
    space = lax.axis_index("space")
    y = lax.axis_index("col")
    core = space % NCORE
    z = (space // NCORE) % NZ
    x = space // (NCORE * NZ)
    pair = x * NCORE + core
    plane = pair * NY + y
    right, left, far = (y + 1) % NY, (y + NY - 1) % NY, (y + 2) % NY
    root = (space == 0) & (y == 0)

    def at_z(zz):
        return (x * (NZ * NCORE) + zz * NCORE + core, y)

    def at_plane(q):
        px = q // (NCORE * NY)
        pc = (q // NY) % NCORE
        return (px * (NZ * NCORE) + z * NCORE + pc, q % NY)

    def at_pair(q):
        return ((q // NCORE) * (NZ * NCORE) + z * NCORE + q % NCORE, y)

    def loop(low, high, body):
        lax.fori_loop(low, high, lambda i, c: (body(i), c)[1], 0)

    def send(src, dst, stage, device):
        pltpu.make_async_remote_copy(
            src_ref=src, dst_ref=dst, send_sem=st_send.at[stage], recv_sem=st_recv.at[stage],
            device_id=device, device_id_type=MESH).start()

    def settle(ref, sem):
        pltpu.make_async_copy(ref, ref, sem).wait()

    def rows_of(i, size):
        return pl.ds(pl.multiple_of(i * size, size), size)

    barrier = pltpu.get_barrier_semaphore()

    def greet(device):
        pl.semaphore_signal(barrier, inc=1, device_id=device, device_id_type=MESH)

    own = pltpu.make_async_copy(p_hbm, gat.at[y], loc.at[0])
    own.start()
    loop(1, NZ, lambda d: greet(at_z((z + d) % NZ)))
    loop(1, PLANE, lambda d: greet(at_plane((plane + d) % PLANE)))
    own.wait()
    loads = [pltpu.make_async_copy(t_hbm.at[:, pl.ds(c * part, part)], tv.at[c], loc.at[1 + c])
             for c in range(NY)]
    for load in loads:
        load.start()
    high, low = split2(gat[y])
    both = dot_nt(high, jnp.concatenate([high, low], axis=0))
    cross = both[:, width:]
    g_loc[...] = both[:, :width] + cross + cross.T
    pl.semaphore_wait(barrier, PLANE + NZ - 2)

    def scatter(d):
        q = (plane + d) % PLANE
        send(g_loc.at[rows_of(q // NY, PIECE)], pr.at[plane], 0, at_plane(q))

    loop(1, PLANE, scatter)

    @pl.when(root)
    def _():
        loop(1, PLANE, lambda q: send(gat.at[0, rows_of(q // NY, PIECE), pl.ds(0, width)], p1s, 3,
                                      at_plane(q)))
        p1s[...] = gat[0, 0:PIECE, 0:width]

    first, second = pl.ds(0, half), pl.ds(half, half)

    def gather_copy(src, dst, index, target):
        return pltpu.make_async_remote_copy(
            src_ref=src, dst_ref=dst, send_sem=gp_send.at[index], recv_sem=gp_recv.at[index],
            device_id=(space, target), device_id_type=MESH)

    ra = gather_copy(p_hbm.at[first], gat.at[y, first], 0, right)
    lb = gather_copy(p_hbm.at[second], gat.at[y, second], 1, left)
    rb = gather_copy(p_hbm.at[second], gat.at[y, second], 2, right)
    la = gather_copy(p_hbm.at[first], gat.at[y, first], 3, left)
    for copy in (ra, lb, rb, la):
        copy.start()

    pr[plane] = g_loc[rows_of(pair, PIECE), :]
    settle(pr.at[pl.ds(0, PLANE - 1)], st_recv.at[0])
    total = pr[0]
    for q in range(1, PLANE):
        total = total + pr[q]
    gz[z] = total
    loop(1, NZ, lambda d: send(gz.at[z], gz.at[z], 1, at_z((z + d) % NZ)))

    @pl.when((z == 0) & (plane > 0))
    def _():
        settle(p1s, st_recv.at[3])

    @pl.when(z == 0)
    def _():
        loop(1, NZ, lambda d: send(p1s, p1s, 4, at_z(d)))

    for load in loads:
        load.wait()

    def products(c):
        ph, pl_ = split2(gat[c])
        th, tl = split2(tv[c])
        four = dot_nt(jnp.concatenate([th, tl], axis=0), jnp.concatenate([ph, pl_], axis=0))
        rows = th.shape[0]
        return (four[:rows, :width] + four[rows:, :width]) + (four[:rows, width:] + four[rows:, width:])

    def put_out(c, index):
        copy = pltpu.make_async_copy(gat.at[c], gat_out.at[c], out_sem.at[index])
        copy.start()
        return copy

    m_loc[...] = products(y)
    outs = [put_out(y, 0)]

    settle(gz.at[pl.ds(0, NZ - 1)], st_recv.at[1])
    total = gz[0]
    for q in range(1, NZ):
        total = total + gz[q]
    mine = rows_of(pair, PIECE)
    gf[mine, :] = total
    loop(1, PAIRS, lambda d: send(gf.at[mine], gf.at[mine], 2, at_pair((pair + d) % PAIRS)))

    @pl.when(z > 0)
    def _():
        settle(p1s, st_recv.at[4])

    p1f[mine, :] = p1s[...]
    loop(1, PAIRS, lambda d: send(p1f.at[mine], p1f.at[mine], 5, at_pair((pair + d) % PAIRS)))

    ra.wait_recv()
    fa = gather_copy(gat.at[left, first], gat.at[left, first], 4, right)
    fa.start()
    lb.wait_recv()
    fb = gather_copy(gat.at[right, second], gat.at[right, second], 5, left)
    fb.start()

    others = pl.ds(0, (PAIRS - 1) * PIECE)
    settle(gf.at[others], st_recv.at[2])
    work[...] = gf[...]
    loop(0, width // BLK, lambda k: chol_step(k, work, upper))
    settle(p1f.at[others], st_recv.at[5])
    work[...] = gf[...] + jnp.dot(p1f[...], upper[...], precision=HIGHEST, preferred_element_type=F32)
    work_t[...] = work[...].T
    loop(0, width // BLK, lambda k: inverse_step(k, work, work_t))

    @pl.when(space == 0)
    def _():
        m_loc[...] += jnp.dot(tv[0, :, 0:width], upper[...], precision=HIGHEST,
                              preferred_element_type=F32)

    rb.wait_recv()
    m_loc[...] += products(left)
    outs.append(put_out(left, 1))
    la.wait_recv()
    m_loc[...] += products(right)
    outs.append(put_out(right, 2))
    fa.wait_recv()
    fb.wait_recv()
    m_loc[...] += products(far)
    outs.append(put_out(far, 3))

    loop(1, PAIRS, lambda d: send(m_loc.at[rows_of((pair + d) % PAIRS, BLK)], mr.at[d - 1], 6,
                                  at_pair((pair + d) % PAIRS)))
    settle(mr, st_recv.at[6])
    tile = rows_of(pair, BLK)
    total = m_loc[tile, :]
    for d in range(PAIRS - 1):
        total = total + mr[d]
    mz[z] = total
    loop(1, NZ, lambda d: send(mz.at[z], mz.at[z], 7, at_z((z + d) % NZ)))
    settle(mz.at[pl.ds(0, NZ - 1)], st_recv.at[7])
    total = mz[0]
    for q in range(1, NZ):
        total = total + mz[q]
    zsum[tile, :] = jnp.dot(total, work[...], precision=HIGHEST, preferred_element_type=F32)
    loop(1, PAIRS, lambda d: send(zsum.at[tile], zsum.at[tile], 8, at_pair((pair + d) % PAIRS)))
    settle(zsum.at[pl.ds(0, (PAIRS - 1) * BLK)], st_recv.at[8])
    zt[...] = zsum[...]

    for copy in (ra, lb, rb, la, fa, fb):
        copy.wait_send()
    for copy in outs:
        copy.wait()
    settle(pr.at[pl.ds(0, PLANE - 1)], st_send.at[0])
    settle(gz.at[pl.ds(0, NZ - 1)], st_send.at[1])
    settle(gf.at[others], st_send.at[2])

    @pl.when(root)
    def _():
        settle(pr.at[pl.ds(0, PLANE - 1)], st_send.at[3])

    @pl.when(z == 0)
    def _():
        settle(gz.at[pl.ds(0, NZ - 1)], st_send.at[4])

    settle(gf.at[others], st_send.at[5])
    settle(mr, st_send.at[6])
    settle(mz.at[pl.ds(0, NZ - 1)], st_send.at[7])
    settle(mr, st_send.at[8])


def update_kernel(scale, p_ref, t_ref, zt_ref, upper_ref, up_ref, out_ref):
    zt = zt_ref[...]
    rows = zt.shape[0]
    width = zt.shape[1]
    zh, zl = split2(zt)
    ph, pl_ = split2(p_ref[0])
    double = jnp.dot(jnp.concatenate([zh, zl], axis=0), ph, preferred_element_type=F32)
    cross = jnp.dot(zh, pl_, preferred_element_type=F32)
    out_ref[...] = t_ref[...] - (double[:rows] + (double[rows:] + cross))

    @pl.when(pl.program_id(0) == 0)
    def _():
        up_ref[...] = upper_ref[...] * scale

    @pl.when((pl.program_id(0) == 0) & (lax.axis_index("space") == 0))
    def _():
        out_ref[:, 0:width] -= lax.dot_general(
            zt, upper_ref[...], (((1,), (1,)), ((), ())), precision=HIGHEST,
            preferred_element_type=F32)


def per_device(panel, trailing):
    width, part = panel.shape
    rows, block = trailing.shape
    rows_total = block * lax.axis_size("space")
    vmem = pl.BlockSpec(memory_space=pltpu.VMEM)
    hbm = pl.BlockSpec(memory_space=pltpu.HBM)
    anywhere = pl.BlockSpec(memory_space=pl.ANY)

    def buf(*shape):
        return pltpu.VMEM(shape, F32)

    gat, upper, zt = pl.pallas_call(
        main_kernel,
        out_shape=(
            jax.ShapeDtypeStruct((NY, width, part), F32),
            jax.ShapeDtypeStruct((width, width), F32),
            jax.ShapeDtypeStruct((rows, width), F32),
        ),
        in_specs=[hbm, hbm],
        out_specs=(anywhere, vmem, vmem),
        scratch_shapes=[
            buf(NY, width, part),
            buf(NY, rows, part),
            buf(width, width),
            buf(PLANE, PIECE, width),
            buf(NZ, PIECE, width),
            buf(width, width),
            buf(PIECE, width),
            buf(width, width),
            buf(rows, width),
            buf(PAIRS - 1, BLK, width),
            buf(NZ, BLK, width),
            buf(rows, width),
            buf(width, width),
            buf(width, width),
            pltpu.SemaphoreType.DMA((6,)),
            pltpu.SemaphoreType.DMA((6,)),
            pltpu.SemaphoreType.DMA((1 + NY,)),
            pltpu.SemaphoreType.DMA((NY,)),
            pltpu.SemaphoreType.DMA((9,)),
            pltpu.SemaphoreType.DMA((9,)),
        ],
        compiler_params=pltpu.CompilerParams(
            collective_id=0, has_side_effects=True, vmem_limit_bytes=40 * 2**20),
        name="reduce_factor",
    )(pltpu.with_memory_space_constraint(panel, pltpu.HBM),
      pltpu.with_memory_space_constraint(trailing, pltpu.HBM))

    upper_factor, updated = pl.pallas_call(
        functools.partial(update_kernel, -1.0 / math.sqrt(rows_total)),
        grid=(NY,),
        out_shape=(
            jax.ShapeDtypeStruct((width, width), F32),
            jax.ShapeDtypeStruct((rows, block), F32),
        ),
        in_specs=[
            pl.BlockSpec((1, width, part), lambda i: (i, 0, 0)),
            pl.BlockSpec((rows, part), lambda i: (0, i)),
            pl.BlockSpec((rows, width), lambda i: (0, 0)),
            pl.BlockSpec((width, width), lambda i: (0, 0)),
        ],
        out_specs=(
            pl.BlockSpec((width, width), lambda i: (0, 0)),
            pl.BlockSpec((rows, part), lambda i: (0, i)),
        ),
        compiler_params=pltpu.CompilerParams(vmem_limit_bytes=40 * 2**20),
        name="apply_update",
    )(gat, trailing, zt, upper)
    return (upper_factor, updated)


def solution(mesh):
    return jax.shard_map(
        per_device,
        mesh=mesh,
        in_specs=(P(None, ("space", "col")), P("col", "space")),
        out_specs=(P(), P("col", "space")),
        check_vma=False,
    )
```

```python
import functools
import math

import jax
import jax.numpy as jnp
from jax import lax
from jax.experimental import pallas as pl
from jax.experimental.pallas import tpu as pltpu
from jax.sharding import PartitionSpec as P

F32 = jnp.float32
BF16 = jnp.bfloat16
HIGHEST = lax.Precision.HIGHEST
MESH = pl.DeviceIdType.MESH
NX, NZ, NCORE, NY = 4, 16, 2, 4
PLANE = NX * NY * NCORE
PAIRS = NX * NCORE
BLK = 8
PIECE = 16


def split2(x):
    high = x.astype(BF16)
    low = (x - high.astype(F32)).astype(BF16)
    return high, low


def split3(x):
    high = x.astype(BF16).astype(F32)
    rest = x - high
    mid = rest.astype(BF16).astype(F32)
    return high, mid, rest - mid


def stacks(a, b):
    ah, am, al = split3(a)
    bh, bm, bl = split3(b)
    left = jnp.concatenate([ah, ah, ah, am, am, al], axis=0).astype(BF16)
    right = jnp.concatenate([bh, bm, bl, bh, bm, bh], axis=0).astype(BF16)
    return left, right


def dot_tn(a, b):
    return lax.dot_general(a, b, (((0,), (0,)), ((), ())), preferred_element_type=F32)


def dot_nt(a, b):
    return lax.dot_general(a, b, (((1,), (1,)), ((), ())), preferred_element_type=F32)


def recip(x):
    y = pl.reciprocal(x, approx=True)
    return y * (2.0 - x * y)


def lane_splat(x, lane):
    return jnp.take_along_axis(x, jnp.full(x.shape, lane, jnp.int32), axis=1)


def merge(rows, row8):
    out = rows[0]
    for i in range(1, len(rows)):
        out = jnp.where(row8 == i, rows[i], out)
    return out


def block_rows(ref, base):
    width = ref.shape[1]
    return [jnp.broadcast_to(ref[pl.ds(base + i, 1), :], (BLK, width)) for i in range(BLK)]


def chol_step(k, work, upper):
    width = work.shape[1]
    row8 = lax.broadcasted_iota(jnp.int32, (BLK, width), 0)
    lane8 = lax.broadcasted_iota(jnp.int32, (BLK, width), 1)
    base = pl.multiple_of(k * BLK, BLK)
    rows = block_rows(work, base)
    s = {(i, j): lane_splat(rows[i], base + j) for i in range(BLK) for j in range(i, BLK)}
    for j in range(BLK):
        inv = recip(s[j, j])
        for i in range(j + 1, BLK):
            factor = s[j, i] * inv
            for l in range(i, BLK):
                s[i, l] = s[i, l] - factor * s[j, l]
            rows[i] = rows[i] - factor * rows[j]
    pivots = merge([s[j, j] for j in range(BLK)], row8)
    block = merge(rows, row8) * lax.rsqrt(pivots)
    block = jnp.where(lane8 >= row8 + base, block, 0.0)
    upper[pl.ds(base, BLK), :] = block
    left, right = stacks(block, block)
    work[...] -= dot_tn(left, right)


def inverse_step(k, mat, mat_t):
    width = mat.shape[1]
    row8 = lax.broadcasted_iota(jnp.int32, (BLK, width), 0)
    lane8 = lax.broadcasted_iota(jnp.int32, (BLK, width), 1)
    base = pl.multiple_of(k * BLK, BLK)
    rows = block_rows(mat, base)
    cols = mat_t[pl.ds(base, BLK), :]
    s = {(i, j): lane_splat(rows[i], base + j) for i in range(BLK) for j in range(BLK)}
    for j in range(BLK):
        inv = recip(s[j, j])
        at = lane8 == base + j
        scaled = jnp.where(at, 1.0, rows[j]) * inv
        for l in range(j + 1, BLK):
            s[j, l] = s[j, l] * inv
        for i in range(BLK):
            if i == j:
                continue
            for l in range(j + 1, BLK):
                s[i, l] = s[i, l] - s[i, j] * s[j, l]
            rows[i] = jnp.where(at, 0.0, rows[i]) - s[i, j] * scaled
        rows[j] = scaled
    block = merge(rows, row8)
    inside = (lane8 >= base) & (lane8 < base + BLK)
    cols = jnp.where(inside, jnp.where(lane8 == row8 + base, -1.0, 0.0), cols)
    left, right = stacks(cols, block)
    row_id = lax.broadcasted_iota(jnp.int32, (width, width), 0)
    lane_id = lax.broadcasted_iota(jnp.int32, (width, width), 1)
    row_out = (row_id < base) | (row_id >= base + BLK)
    lane_out = (lane_id < base) | (lane_id >= base + BLK)
    keep = row_out & lane_out
    mat[...] = jnp.where(keep, mat[...], 0.0) - dot_tn(left, right)
    mat_t[...] = jnp.where(keep, mat_t[...], 0.0) - dot_tn(right, left)


def main_kernel(p_hbm, t_hbm, gat_out, upper, zt,
                gat, tv, g_loc, pr, gz, gf, p1s, p1f, m_loc, mr, mz, zsum, work, work_t,
                gp_send, gp_recv, loc, out_sem, st_send, st_recv, ready):
    width, part = p_hbm.shape
    half = width // 2
    space = lax.axis_index("space")
    y = lax.axis_index("col")
    core = space % NCORE
    z = (space // NCORE) % NZ
    x = space // (NCORE * NZ)
    pair = x * NCORE + core
    plane = pair * NY + y
    right, left, far = (y + 1) % NY, (y + NY - 1) % NY, (y + 2) % NY
    root = (space == 0) & (y == 0)

    def at_z(zz):
        return (x * (NZ * NCORE) + zz * NCORE + core, y)

    def at_plane(q):
        px = q // (NCORE * NY)
        pc = (q // NY) % NCORE
        return (px * (NZ * NCORE) + z * NCORE + pc, q % NY)

    def at_pair(q):
        return ((q // NCORE) * (NZ * NCORE) + z * NCORE + q % NCORE, y)

    def loop(low, high, body):
        lax.fori_loop(low, high, lambda i, c: (body(i), c)[1], 0)

    def send(src, dst, stage, device):
        pltpu.make_async_remote_copy(
            src_ref=src, dst_ref=dst, send_sem=st_send.at[stage], recv_sem=st_recv.at[stage],
            device_id=device, device_id_type=MESH).start()

    def settle(ref, sem):
        pltpu.make_async_copy(ref, ref, sem).wait()

    def rows_of(i, size):
        return pl.ds(pl.multiple_of(i * size, size), size)

    barrier = pltpu.get_barrier_semaphore()

    def greet(device):
        pl.semaphore_signal(barrier, inc=1, device_id=device, device_id_type=MESH)

    own = pltpu.make_async_copy(p_hbm, gat.at[y], loc.at[0])
    own.start()
    greet(at_z((z + 1) % NZ))
    greet(at_z((z + NZ - 1) % NZ))
    loop(1, PLANE, lambda d: greet(at_plane((plane + d) % PLANE)))
    own.wait()
    high, low = split2(gat[y])
    both = dot_nt(high, jnp.concatenate([high, low], axis=0))
    cross = both[:, width:]
    g_loc[...] = both[:, :width] + cross + cross.T
    pl.semaphore_wait(barrier, PLANE + 1)

    def announce(level, step):
        for zz in ((z + step) % NZ, (z + NZ - step) % NZ):
            pl.semaphore_signal(ready.at[level], inc=1, device_id=at_z(zz), device_id_type=MESH)

    announce(0, 1)

    def gather_copy(src, dst, index, target):
        return pltpu.make_async_remote_copy(
            src_ref=src, dst_ref=dst, send_sem=gp_send.at[index], recv_sem=gp_recv.at[index],
            device_id=(space, target), device_id_type=MESH)

    def share(start, size, index, target):
        rows = pl.ds(start, size)
        copy = gather_copy(p_hbm.at[rows], gat.at[y, rows], index, target)
        copy.start()
        return copy

    head = 8
    first, second = pl.ds(0, half), pl.ds(half, half)
    ra0 = share(0, head, 6, right)
    lb0 = share(half, head, 7, left)

    def scatter(d):
        q = (plane + d) % PLANE
        send(g_loc.at[rows_of(q // NY, PIECE)], pr.at[plane], 0, at_plane(q))

    loop(1, PLANE, scatter)

    @pl.when(root)
    def _():
        loop(1, PLANE, lambda q: send(gat.at[0, rows_of(q // NY, PIECE), pl.ds(0, width)], p1s, 3,
                                      at_plane(q)))
        p1s[...] = gat[0, 0:PIECE, 0:width]

    ra = share(head, half - head, 0, right)
    lb = share(half + head, half - head, 1, left)
    rb = share(half, half, 2, right)
    la = share(0, half, 3, left)
    loads = [pltpu.make_async_copy(t_hbm.at[:, pl.ds(c * part, part)], tv.at[c], loc.at[1 + c])
             for c in range(NY)]
    for load in loads:
        load.start()
    pl.semaphore_wait(ready.at[0], 2)
    announce(1, 2)
    pr[plane] = g_loc[rows_of(pair, PIECE), :]
    pl.semaphore_wait(ready.at[1], 2)
    announce(2, 4)
    settle(pr.at[pl.ds(0, PLANE - 1)], st_recv.at[0])
    total = pr[0]
    for q in range(1, PLANE):
        total = total + pr[q]
    gz[z] = total
    pl.semaphore_wait(ready.at[2], 2)
    loop(1, NZ, lambda d: send(gz.at[z], gz.at[z], 1, at_z((z + d) % NZ)))

    @pl.when((z == 0) & (plane > 0))
    def _():
        settle(p1s, st_recv.at[3])

    @pl.when(z == 0)
    def _():
        loop(1, NZ, lambda d: send(p1s, p1s, 4, at_z(d)))

    for load in loads:
        load.wait()

    def products(c):
        ph, pl_ = split2(gat[c])
        th, tl = split2(tv[c])
        four = dot_nt(jnp.concatenate([th, tl], axis=0), jnp.concatenate([ph, pl_], axis=0))
        rows = th.shape[0]
        return (four[:rows, :width] + four[rows:, :width]) + (four[:rows, width:] + four[rows:, width:])

    def put_out(c, index):
        copy = pltpu.make_async_copy(gat.at[c], gat_out.at[c], out_sem.at[index])
        copy.start()
        return copy

    m_loc[...] = products(y)
    outs = [put_out(y, 0)]

    ra0.wait_recv()
    ra.wait_recv()
    fa = gather_copy(gat.at[left, first], gat.at[left, first], 4, right)
    fa.start()
    lb0.wait_recv()
    lb.wait_recv()
    fb = gather_copy(gat.at[right, second], gat.at[right, second], 5, left)
    fb.start()

    settle(gz.at[pl.ds(0, NZ - 1)], st_recv.at[1])
    total = gz[0]
    for q in range(1, NZ):
        total = total + gz[q]
    mine = rows_of(pair, PIECE)
    gf[mine, :] = total
    loop(1, PAIRS, lambda d: send(gf.at[mine], gf.at[mine], 2, at_pair((pair + d) % PAIRS)))

    @pl.when(z > 0)
    def _():
        settle(p1s, st_recv.at[4])

    p1f[mine, :] = p1s[...]
    loop(1, PAIRS, lambda d: send(p1f.at[mine], p1f.at[mine], 5, at_pair((pair + d) % PAIRS)))

    others = pl.ds(0, (PAIRS - 1) * PIECE)
    settle(gf.at[others], st_recv.at[2])
    work[...] = gf[...]
    loop(0, width // BLK, lambda k: chol_step(k, work, upper))
    rb.wait_recv()
    m_loc[...] += products(left)
    outs.append(put_out(left, 1))
    la.wait_recv()
    m_loc[...] += products(right)
    outs.append(put_out(right, 2))
    settle(p1f.at[others], st_recv.at[5])
    work[...] = gf[...] + jnp.dot(p1f[...], upper[...], precision=HIGHEST, preferred_element_type=F32)
    work_t[...] = work[...].T
    loop(0, width // BLK, lambda k: inverse_step(k, work, work_t))

    @pl.when(space == 0)
    def _():
        m_loc[...] += jnp.dot(tv[0, :, 0:width], upper[...], precision=HIGHEST,
                              preferred_element_type=F32)

    fa.wait_recv()
    fb.wait_recv()
    m_loc[...] += products(far)
    outs.append(put_out(far, 3))

    loop(1, PAIRS, lambda d: send(m_loc.at[rows_of((pair + d) % PAIRS, BLK)], mr.at[d - 1], 6,
                                  at_pair((pair + d) % PAIRS)))
    settle(mr, st_recv.at[6])
    tile = rows_of(pair, BLK)
    total = m_loc[tile, :]
    for d in range(PAIRS - 1):
        total = total + mr[d]
    mz[z] = total
    loop(1, NZ, lambda d: send(mz.at[z], mz.at[z], 7, at_z((z + d) % NZ)))
    settle(mz.at[pl.ds(0, NZ - 1)], st_recv.at[7])
    total = mz[0]
    for q in range(1, NZ):
        total = total + mz[q]
    zsum[tile, :] = jnp.dot(total, work[...], precision=HIGHEST, preferred_element_type=F32)
    loop(1, PAIRS, lambda d: send(zsum.at[tile], zsum.at[tile], 8, at_pair((pair + d) % PAIRS)))
    settle(zsum.at[pl.ds(0, (PAIRS - 1) * BLK)], st_recv.at[8])
    zt[...] = zsum[...]

    for copy in (ra0, lb0, ra, lb, rb, la, fa, fb):
        copy.wait_send()
    for copy in outs:
        copy.wait()
    settle(pr.at[pl.ds(0, PLANE - 1)], st_send.at[0])
    settle(gz.at[pl.ds(0, NZ - 1)], st_send.at[1])
    settle(gf.at[others], st_send.at[2])

    @pl.when(root)
    def _():
        settle(pr.at[pl.ds(0, PLANE - 1)], st_send.at[3])

    @pl.when(z == 0)
    def _():
        settle(gz.at[pl.ds(0, NZ - 1)], st_send.at[4])

    settle(gf.at[others], st_send.at[5])
    settle(mr, st_send.at[6])
    settle(mz.at[pl.ds(0, NZ - 1)], st_send.at[7])
    settle(mr, st_send.at[8])


def update_kernel(scale, p_ref, t_ref, zt_ref, upper_ref, up_ref, out_ref, new, out_sem):
    zt = zt_ref[...]
    rows, width = zt.shape
    part = p_ref.shape[2]
    zh, zl = split2(zt)
    pair = jnp.concatenate([zh, zl], axis=0)
    copies = []
    for c in range(NY):
        cols = pl.ds(c * part, part)
        ph, pl_ = split2(p_ref[c])
        double = jnp.dot(pair, ph, preferred_element_type=F32)
        cross = jnp.dot(zh, pl_, preferred_element_type=F32)
        new[c] = t_ref[:, cols] - (double[:rows] + (double[rows:] + cross))
        if c == 0:
            @pl.when(lax.axis_index("space") == 0)
            def _():
                new[0, :, 0:width] -= lax.dot_general(
                    zt, upper_ref[...], (((1,), (1,)), ((), ())), precision=HIGHEST,
                    preferred_element_type=F32)
        copy = pltpu.make_async_copy(new.at[c], out_ref.at[:, cols], out_sem.at[c])
        copy.start()
        copies.append(copy)
    up_ref[...] = upper_ref[...] * scale
    for copy in copies:
        copy.wait()


def per_device(panel, trailing):
    width, part = panel.shape
    rows, block = trailing.shape
    rows_total = block * lax.axis_size("space")
    vmem = pl.BlockSpec(memory_space=pltpu.VMEM)
    hbm = pl.BlockSpec(memory_space=pltpu.HBM)
    anywhere = pl.BlockSpec(memory_space=pl.ANY)

    def buf(*shape):
        return pltpu.VMEM(shape, F32)

    gat, upper, zt = pl.pallas_call(
        main_kernel,
        out_shape=(
            jax.ShapeDtypeStruct((NY, width, part), F32),
            jax.ShapeDtypeStruct((width, width), F32),
            jax.ShapeDtypeStruct((rows, width), F32),
        ),
        in_specs=[hbm, hbm],
        out_specs=(anywhere, vmem, vmem),
        scratch_shapes=[
            buf(NY, width, part),
            buf(NY, rows, part),
            buf(width, width),
            buf(PLANE, PIECE, width),
            buf(NZ, PIECE, width),
            buf(width, width),
            buf(PIECE, width),
            buf(width, width),
            buf(rows, width),
            buf(PAIRS - 1, BLK, width),
            buf(NZ, BLK, width),
            buf(rows, width),
            buf(width, width),
            buf(width, width),
            pltpu.SemaphoreType.DMA((8,)),
            pltpu.SemaphoreType.DMA((8,)),
            pltpu.SemaphoreType.DMA((1 + NY,)),
            pltpu.SemaphoreType.DMA((NY,)),
            pltpu.SemaphoreType.DMA((9,)),
            pltpu.SemaphoreType.DMA((9,)),
            pltpu.SemaphoreType.REGULAR((3,)),
        ],
        compiler_params=pltpu.CompilerParams(
            collective_id=0, has_side_effects=True, vmem_limit_bytes=40 * 2**20),
        name="reduce_factor",
    )(pltpu.with_memory_space_constraint(panel, pltpu.HBM),
      pltpu.with_memory_space_constraint(trailing, pltpu.HBM))

    upper_factor, updated = pl.pallas_call(
        functools.partial(update_kernel, -1.0 / math.sqrt(rows_total)),
        out_shape=(
            jax.ShapeDtypeStruct((width, width), F32),
            jax.ShapeDtypeStruct((rows, block), F32),
        ),
        in_specs=[vmem] * 4,
        out_specs=(vmem, hbm),
        scratch_shapes=[buf(NY, rows, part), pltpu.SemaphoreType.DMA((NY,))],
        compiler_params=pltpu.CompilerParams(vmem_limit_bytes=40 * 2**20),
        name="apply_update",
    )(gat, trailing, zt, upper)
    return (upper_factor, updated)


def solution(mesh):
    return jax.shard_map(
        per_device,
        mesh=mesh,
        in_specs=(P(None, ("space", "col")), P("col", "space")),
        out_specs=(P(), P("col", "space")),
        check_vma=False,
    )
```

```python
import functools
import math

import jax
import jax.numpy as jnp
from jax import lax
from jax.experimental import pallas as pl
from jax.experimental.pallas import tpu as pltpu
from jax.sharding import PartitionSpec as P

F32 = jnp.float32
BF16 = jnp.bfloat16
HIGHEST = lax.Precision.HIGHEST
MESH = pl.DeviceIdType.MESH
NX, NZ, NCORE, NY = 4, 16, 2, 4
PAIRS = NX * NCORE
BLK = 8
PIECE = 16


def split2(x):
    high = x.astype(BF16)
    low = (x - high.astype(F32)).astype(BF16)
    return high, low


def split3(x):
    high = x.astype(BF16).astype(F32)
    rest = x - high
    mid = rest.astype(BF16).astype(F32)
    return high, mid, rest - mid


def stacks(a, b):
    ah, am, al = split3(a)
    bh, bm, bl = split3(b)
    left = jnp.concatenate([ah, ah, ah, am, am, al], axis=0).astype(BF16)
    right = jnp.concatenate([bh, bm, bl, bh, bm, bh], axis=0).astype(BF16)
    return left, right


def dot_tn(a, b):
    return lax.dot_general(a, b, (((0,), (0,)), ((), ())), preferred_element_type=F32)


def dot_nt(a, b):
    return lax.dot_general(a, b, (((1,), (1,)), ((), ())), preferred_element_type=F32)


def recip(x):
    y = pl.reciprocal(x, approx=True)
    return y * (2.0 - x * y)


def lane_splat(x, lane):
    return jnp.take_along_axis(x, jnp.full(x.shape, lane, jnp.int32), axis=1)


def merge(rows, row8):
    out = rows[0]
    for i in range(1, len(rows)):
        out = jnp.where(row8 == i, rows[i], out)
    return out


def block_rows(ref, base):
    width = ref.shape[1]
    return [jnp.broadcast_to(ref[pl.ds(base + i, 1), :], (BLK, width)) for i in range(BLK)]


def chol_step(k, work, upper):
    width = work.shape[1]
    row8 = lax.broadcasted_iota(jnp.int32, (BLK, width), 0)
    lane8 = lax.broadcasted_iota(jnp.int32, (BLK, width), 1)
    base = pl.multiple_of(k * BLK, BLK)
    rows = block_rows(work, base)
    s = {(i, j): lane_splat(rows[i], base + j) for i in range(BLK) for j in range(i, BLK)}
    for j in range(BLK):
        inv = recip(s[j, j])
        for i in range(j + 1, BLK):
            factor = s[j, i] * inv
            for l in range(i, BLK):
                s[i, l] = s[i, l] - factor * s[j, l]
            rows[i] = rows[i] - factor * rows[j]
    pivots = merge([s[j, j] for j in range(BLK)], row8)
    block = merge(rows, row8) * lax.rsqrt(pivots)
    block = jnp.where(lane8 >= row8 + base, block, 0.0)
    upper[pl.ds(base, BLK), :] = block
    left, right = stacks(block, block)
    work[...] -= dot_tn(left, right)


def inverse_step(k, mat, mat_t):
    width = mat.shape[1]
    row8 = lax.broadcasted_iota(jnp.int32, (BLK, width), 0)
    lane8 = lax.broadcasted_iota(jnp.int32, (BLK, width), 1)
    base = pl.multiple_of(k * BLK, BLK)
    rows = block_rows(mat, base)
    cols = mat_t[pl.ds(base, BLK), :]
    s = {(i, j): lane_splat(rows[i], base + j) for i in range(BLK) for j in range(BLK)}
    for j in range(BLK):
        inv = recip(s[j, j])
        at = lane8 == base + j
        scaled = jnp.where(at, 1.0, rows[j]) * inv
        for l in range(j + 1, BLK):
            s[j, l] = s[j, l] * inv
        for i in range(BLK):
            if i == j:
                continue
            for l in range(j + 1, BLK):
                s[i, l] = s[i, l] - s[i, j] * s[j, l]
            rows[i] = jnp.where(at, 0.0, rows[i]) - s[i, j] * scaled
        rows[j] = scaled
    block = merge(rows, row8)
    inside = (lane8 >= base) & (lane8 < base + BLK)
    cols = jnp.where(inside, jnp.where(lane8 == row8 + base, -1.0, 0.0), cols)
    left, right = stacks(cols, block)
    row_id = lax.broadcasted_iota(jnp.int32, (width, width), 0)
    lane_id = lax.broadcasted_iota(jnp.int32, (width, width), 1)
    row_out = (row_id < base) | (row_id >= base + BLK)
    lane_out = (lane_id < base) | (lane_id >= base + BLK)
    keep = row_out & lane_out
    mat[...] = jnp.where(keep, mat[...], 0.0) - dot_tn(left, right)
    mat_t[...] = jnp.where(keep, mat_t[...], 0.0) - dot_tn(right, left)


def main_kernel(p_hbm, t_hbm, gat_out, upper, zt,
                gat, tv, g_loc, pr, yr, gz, gf, p1w, p1s, p1f, m_loc, mr, mz, zsum, work, work_t,
                gp_send, gp_recv, loc, out_sem, st_send, st_recv, p1_send, ready):
    width, part = p_hbm.shape
    half = width // 2
    space = lax.axis_index("space")
    y = lax.axis_index("col")
    core = space % NCORE
    z = (space // NCORE) % NZ
    x = space // (NCORE * NZ)
    pair = x * NCORE + core
    right, left, far = (y + 1) % NY, (y + NY - 1) % NY, (y + 2) % NY
    root = (space == 0) & (y == 0)

    def at_z(zz):
        return (x * (NZ * NCORE) + zz * NCORE + core, y)

    def at_y(yy):
        return (space, yy)

    def at_pair(q):
        return ((q // NCORE) * (NZ * NCORE) + z * NCORE + q % NCORE, y)

    def loop(low, high, body):
        lax.fori_loop(low, high, lambda i, c: (body(i), c)[1], 0)

    def send(src, dst, stage, device):
        pltpu.make_async_remote_copy(
            src_ref=src, dst_ref=dst, send_sem=st_send.at[stage], recv_sem=st_recv.at[stage],
            device_id=device, device_id_type=MESH).start()

    def settle(ref, sem):
        pltpu.make_async_copy(ref, ref, sem).wait()

    def rows_of(i, size):
        return pl.ds(pl.multiple_of(i * size, size), size)

    barrier = pltpu.get_barrier_semaphore()

    def greet(device):
        pl.semaphore_signal(barrier, inc=1, device_id=device, device_id_type=MESH)

    own = pltpu.make_async_copy(p_hbm, gat.at[y], loc.at[0])
    own.start()
    greet(at_z((z + 1) % NZ))
    greet(at_z((z + NZ - 1) % NZ))
    loop(1, NY, lambda d: greet(at_y((y + d) % NY)))
    loop(1, PAIRS, lambda d: greet(at_pair((pair + d) % PAIRS)))
    own.wait()
    high, low = split2(gat[y])
    both = dot_nt(high, jnp.concatenate([high, low], axis=0))
    cross = both[:, width:]
    g_loc[...] = both[:, :width] + cross + cross.T
    pl.semaphore_wait(barrier, PAIRS + NY)

    def announce(level, step):
        for zz in ((z + step) % NZ, (z + NZ - step) % NZ):
            pl.semaphore_signal(ready.at[level], inc=1, device_id=at_z(zz), device_id_type=MESH)

    announce(0, 1)

    def gather_copy(src, dst, index, target):
        return pltpu.make_async_remote_copy(
            src_ref=src, dst_ref=dst, send_sem=gp_send.at[index], recv_sem=gp_recv.at[index],
            device_id=(space, target), device_id_type=MESH)

    def share(start, size, index, target):
        rows = pl.ds(start, size)
        copy = gather_copy(p_hbm.at[rows], gat.at[y, rows], index, target)
        copy.start()
        return copy

    loop(1, PAIRS, lambda d: send(g_loc.at[rows_of((pair + d) % PAIRS, PIECE)], pr.at[d - 1], 0,
                                  at_pair((pair + d) % PAIRS)))
    head = 24
    first, second = pl.ds(0, half), pl.ds(half, half)
    ra0 = share(0, head, 6, right)
    lb0 = share(half, head, 7, left)
    pl.semaphore_wait(ready.at[0], 2)
    announce(1, 2)

    @pl.when(root)
    def _():
        for d in range(1, NY):
            pltpu.make_async_remote_copy(
                src_ref=gat.at[0, :, pl.ds(0, width)], dst_ref=p1w, send_sem=p1_send.at[d - 1],
                recv_sem=st_recv.at[3], device_id=at_y(d), device_id_type=MESH).start()
        p1w[...] = gat[0, :, 0:width]

    settle(pr, st_recv.at[0])
    total = g_loc[rows_of(pair, PIECE), :]
    for d in range(PAIRS - 1):
        total = total + pr[d]
    yr[y] = total
    loop(1, NY, lambda d: send(yr.at[y], yr.at[y], 10, at_y((y + d) % NY)))
    ra = share(head, half - head, 0, right)
    lb = share(half + head, half - head, 1, left)
    rb = share(half, half, 2, right)
    la = share(0, half, 3, left)
    loads = [pltpu.make_async_copy(t_hbm.at[:, pl.ds(c * part, part)], tv.at[c], loc.at[1 + c])
             for c in range(NY)]
    for load in loads:
        load.start()
    pl.semaphore_wait(ready.at[1], 2)
    announce(2, 4)
    settle(yr.at[pl.ds(0, NY - 1)], st_recv.at[10])
    total = yr[0]
    for q in range(1, NY):
        total = total + yr[q]
    gz[z] = total
    pl.semaphore_wait(ready.at[2], 2)
    loop(1, NZ, lambda d: send(gz.at[z], gz.at[z], 1, at_z((z + d) % NZ)))

    @pl.when((space == 0) & (y > 0))
    def _():
        settle(p1w, st_recv.at[3])

    @pl.when(space == 0)
    def _():
        loop(1, PAIRS, lambda q: send(p1w.at[rows_of(q, PIECE)], p1s, 4, at_pair(q)))
        p1s[...] = p1w[0:PIECE, :]

    @pl.when((z == 0) & (pair > 0))
    def _():
        settle(p1s, st_recv.at[4])

    @pl.when(z == 0)
    def _():
        loop(1, NZ, lambda d: send(p1s, p1s, 5, at_z(d)))

    for load in loads:
        load.wait()

    def products(c):
        ph, pl_ = split2(gat[c])
        th, tl = split2(tv[c])
        four = dot_nt(jnp.concatenate([th, tl], axis=0), jnp.concatenate([ph, pl_], axis=0))
        rows = th.shape[0]
        return (four[:rows, :width] + four[rows:, :width]) + (four[:rows, width:] + four[rows:, width:])

    def put_out(c, index):
        copy = pltpu.make_async_copy(gat.at[c], gat_out.at[c], out_sem.at[index])
        copy.start()
        return copy

    m_loc[...] = products(y)
    outs = [put_out(y, 0)]

    ra0.wait_recv()
    ra.wait_recv()
    fa = gather_copy(gat.at[left, first], gat.at[left, first], 4, right)
    fa.start()
    lb0.wait_recv()
    lb.wait_recv()
    fb = gather_copy(gat.at[right, second], gat.at[right, second], 5, left)
    fb.start()

    settle(gz.at[pl.ds(0, NZ - 1)], st_recv.at[1])
    total = gz[0]
    for q in range(1, NZ):
        total = total + gz[q]
    mine = rows_of(pair, PIECE)
    gf[mine, :] = total
    loop(1, PAIRS, lambda d: send(gf.at[mine], gf.at[mine], 2, at_pair((pair + d) % PAIRS)))

    @pl.when(z > 0)
    def _():
        settle(p1s, st_recv.at[5])

    p1f[mine, :] = p1s[...]
    loop(1, PAIRS, lambda d: send(p1f.at[mine], p1f.at[mine], 6, at_pair((pair + d) % PAIRS)))

    others = pl.ds(0, (PAIRS - 1) * PIECE)
    settle(gf.at[others], st_recv.at[2])
    work[...] = gf[...]
    loop(0, width // BLK, lambda k: chol_step(k, work, upper))
    rb.wait_recv()
    m_loc[...] += products(left)
    outs.append(put_out(left, 1))
    la.wait_recv()
    m_loc[...] += products(right)
    outs.append(put_out(right, 2))
    settle(p1f.at[others], st_recv.at[6])
    work[...] = gf[...] + jnp.dot(p1f[...], upper[...], precision=HIGHEST, preferred_element_type=F32)
    work_t[...] = work[...].T
    loop(0, width // BLK, lambda k: inverse_step(k, work, work_t))

    @pl.when(space == 0)
    def _():
        m_loc[...] += jnp.dot(tv[0, :, 0:width], upper[...], precision=HIGHEST,
                              preferred_element_type=F32)

    fa.wait_recv()
    fb.wait_recv()
    m_loc[...] += products(far)
    outs.append(put_out(far, 3))

    loop(1, PAIRS, lambda d: send(m_loc.at[rows_of((pair + d) % PAIRS, BLK)], mr.at[d - 1], 7,
                                  at_pair((pair + d) % PAIRS)))
    settle(mr, st_recv.at[7])
    tile = rows_of(pair, BLK)
    total = m_loc[tile, :]
    for d in range(PAIRS - 1):
        total = total + mr[d]
    mz[z] = total
    loop(1, NZ, lambda d: send(mz.at[z], mz.at[z], 8, at_z((z + d) % NZ)))
    settle(mz.at[pl.ds(0, NZ - 1)], st_recv.at[8])
    total = mz[0]
    for q in range(1, NZ):
        total = total + mz[q]
    zsum[tile, :] = jnp.dot(total, work[...], precision=HIGHEST, preferred_element_type=F32)
    loop(1, PAIRS, lambda d: send(zsum.at[tile], zsum.at[tile], 9, at_pair((pair + d) % PAIRS)))
    settle(zsum.at[pl.ds(0, (PAIRS - 1) * BLK)], st_recv.at[9])
    zt[...] = zsum[...]

    for copy in (ra0, lb0, ra, lb, rb, la, fa, fb):
        copy.wait_send()
    for copy in outs:
        copy.wait()
    settle(pr, st_send.at[0])
    settle(gz.at[pl.ds(0, NZ - 1)], st_send.at[1])
    settle(gf.at[others], st_send.at[2])

    @pl.when(root)
    def _():
        for d in range(1, NY):
            settle(p1w, p1_send.at[d - 1])

    @pl.when(space == 0)
    def _():
        settle(gf.at[others], st_send.at[4])

    @pl.when(z == 0)
    def _():
        settle(gz.at[pl.ds(0, NZ - 1)], st_send.at[5])

    settle(gf.at[others], st_send.at[6])
    settle(mr, st_send.at[7])
    settle(mz.at[pl.ds(0, NZ - 1)], st_send.at[8])
    settle(mr, st_send.at[9])
    settle(yr.at[pl.ds(0, NY - 1)], st_send.at[10])


def update_kernel(scale, p_ref, t_ref, zt_ref, upper_ref, up_ref, out_ref, new, out_sem):
    zt = zt_ref[...]
    rows, width = zt.shape
    part = p_ref.shape[2]
    zh, zl = split2(zt)
    pair = jnp.concatenate([zh, zl], axis=0)
    copies = []
    for c in range(NY):
        cols = pl.ds(c * part, part)
        ph, pl_ = split2(p_ref[c])
        double = jnp.dot(pair, ph, preferred_element_type=F32)
        cross = jnp.dot(zh, pl_, preferred_element_type=F32)
        new[c] = t_ref[:, cols] - (double[:rows] + (double[rows:] + cross))
        if c == 0:
            @pl.when(lax.axis_index("space") == 0)
            def _():
                new[0, :, 0:width] -= lax.dot_general(
                    zt, upper_ref[...], (((1,), (1,)), ((), ())), precision=HIGHEST,
                    preferred_element_type=F32)
        copy = pltpu.make_async_copy(new.at[c], out_ref.at[:, cols], out_sem.at[c])
        copy.start()
        copies.append(copy)
    up_ref[...] = upper_ref[...] * scale
    for copy in copies:
        copy.wait()


def per_device(panel, trailing):
    width, part = panel.shape
    rows, block = trailing.shape
    rows_total = block * lax.axis_size("space")
    vmem = pl.BlockSpec(memory_space=pltpu.VMEM)
    hbm = pl.BlockSpec(memory_space=pltpu.HBM)
    anywhere = pl.BlockSpec(memory_space=pl.ANY)

    def buf(*shape):
        return pltpu.VMEM(shape, F32)

    gat, upper, zt = pl.pallas_call(
        main_kernel,
        out_shape=(
            jax.ShapeDtypeStruct((NY, width, part), F32),
            jax.ShapeDtypeStruct((width, width), F32),
            jax.ShapeDtypeStruct((rows, width), F32),
        ),
        in_specs=[hbm, hbm],
        out_specs=(anywhere, vmem, vmem),
        scratch_shapes=[
            buf(NY, width, part),
            buf(NY, rows, part),
            buf(width, width),
            buf(PAIRS - 1, PIECE, width),
            buf(NY, PIECE, width),
            buf(NZ, PIECE, width),
            buf(width, width),
            buf(width, width),
            buf(PIECE, width),
            buf(width, width),
            buf(rows, width),
            buf(PAIRS - 1, BLK, width),
            buf(NZ, BLK, width),
            buf(rows, width),
            buf(width, width),
            buf(width, width),
            pltpu.SemaphoreType.DMA((8,)),
            pltpu.SemaphoreType.DMA((8,)),
            pltpu.SemaphoreType.DMA((1 + NY,)),
            pltpu.SemaphoreType.DMA((NY,)),
            pltpu.SemaphoreType.DMA((11,)),
            pltpu.SemaphoreType.DMA((11,)),
            pltpu.SemaphoreType.DMA((NY - 1,)),
            pltpu.SemaphoreType.REGULAR((3,)),
        ],
        compiler_params=pltpu.CompilerParams(
            collective_id=0, has_side_effects=True, vmem_limit_bytes=40 * 2**20),
        name="reduce_factor",
    )(pltpu.with_memory_space_constraint(panel, pltpu.HBM),
      pltpu.with_memory_space_constraint(trailing, pltpu.HBM))

    upper_factor, updated = pl.pallas_call(
        functools.partial(update_kernel, -1.0 / math.sqrt(rows_total)),
        out_shape=(
            jax.ShapeDtypeStruct((width, width), F32),
            jax.ShapeDtypeStruct((rows, block), F32),
        ),
        in_specs=[vmem] * 4,
        out_specs=(vmem, hbm),
        scratch_shapes=[buf(NY, rows, part), pltpu.SemaphoreType.DMA((NY,))],
        compiler_params=pltpu.CompilerParams(vmem_limit_bytes=40 * 2**20),
        name="apply_update",
    )(gat, trailing, zt, upper)
    return (upper_factor, updated)


def solution(mesh):
    return jax.shard_map(
        per_device,
        mesh=mesh,
        in_specs=(P(None, ("space", "col")), P("col", "space")),
        out_specs=(P(), P("col", "space")),
        check_vma=False,
    )
```

```python
import functools
import math

import jax
import jax.numpy as jnp
from jax import lax
from jax.experimental import pallas as pl
from jax.experimental.pallas import tpu as pltpu
from jax.sharding import PartitionSpec as P

F32 = jnp.float32
BF16 = jnp.bfloat16
HIGHEST = lax.Precision.HIGHEST
MESH = pl.DeviceIdType.MESH
NX, NZ, NCORE, NY = 4, 16, 2, 4
PAIRS = NX * NCORE
BLK = 8
LANES = 128
PIECE = 16
EARLY = 10
PLANE = PAIRS * NY


def split2(x):
    high = x.astype(BF16)
    low = (x - high.astype(F32)).astype(BF16)
    return high, low


def split3(x):
    high = x.astype(BF16).astype(F32)
    rest = x - high
    mid = rest.astype(BF16).astype(F32)
    return high, mid, rest - mid


def stacks(a, b):
    ah, am, al = split3(a)
    bh, bm, bl = split3(b)
    left = jnp.concatenate([ah, ah, ah, am, am, al], axis=0).astype(BF16)
    right = jnp.concatenate([bh, bm, bl, bh, bm, bh], axis=0).astype(BF16)
    return left, right


def dot_tn(a, b):
    return lax.dot_general(a, b, (((0,), (0,)), ((), ())), preferred_element_type=F32)


def dot_nt(a, b):
    return lax.dot_general(a, b, (((1,), (1,)), ((), ())), preferred_element_type=F32)


def recip(x):
    y = pl.reciprocal(x, approx=True)
    return y * (2.0 - x * y)


def lane_splat(x, lane):
    return jnp.take_along_axis(x, jnp.full(x.shape, lane, jnp.int32), axis=1)


def merge(rows, row8):
    out = rows[0]
    for i in range(1, len(rows)):
        out = jnp.where(row8 == i, rows[i], out)
    return out


def block_rows(ref, base):
    width = ref.shape[1]
    return [jnp.broadcast_to(ref[pl.ds(base + i, 1), :], (BLK, width)) for i in range(BLK)]


def chol_step(k, work, upper):
    width = work.shape[1]
    row8 = lax.broadcasted_iota(jnp.int32, (BLK, width), 0)
    lane8 = lax.broadcasted_iota(jnp.int32, (BLK, width), 1)
    base = pl.multiple_of(k * BLK, BLK)
    rows = block_rows(work, base)
    s = {(i, j): lane_splat(rows[i], base + j) for i in range(BLK) for j in range(i, BLK)}
    for j in range(BLK):
        inv = recip(s[j, j])
        for i in range(j + 1, BLK):
            factor = s[j, i] * inv
            for l in range(i, BLK):
                s[i, l] = s[i, l] - factor * s[j, l]
            rows[i] = rows[i] - factor * rows[j]
    pivots = merge([s[j, j] for j in range(BLK)], row8)
    block = merge(rows, row8) * lax.rsqrt(pivots)
    block = jnp.where(lane8 >= row8 + base, block, 0.0)
    upper[pl.ds(base, BLK), :] = block
    left, right = stacks(block, block)
    work[...] -= dot_tn(left, right)


def inverse_step(k, mat, mat_t):
    width = mat.shape[1]
    row8 = lax.broadcasted_iota(jnp.int32, (BLK, width), 0)
    lane8 = lax.broadcasted_iota(jnp.int32, (BLK, width), 1)
    base = pl.multiple_of(k * BLK, BLK)
    rows = block_rows(mat, base)
    cols = mat_t[pl.ds(base, BLK), :]
    s = {(i, j): lane_splat(rows[i], base + j) for i in range(BLK) for j in range(BLK)}
    for j in range(BLK):
        inv = recip(s[j, j])
        at = lane8 == base + j
        scaled = jnp.where(at, 1.0, rows[j]) * inv
        for l in range(j + 1, BLK):
            s[j, l] = s[j, l] * inv
        for i in range(BLK):
            if i == j:
                continue
            for l in range(j + 1, BLK):
                s[i, l] = s[i, l] - s[i, j] * s[j, l]
            rows[i] = jnp.where(at, 0.0, rows[i]) - s[i, j] * scaled
        rows[j] = scaled
    block = merge(rows, row8)
    inside = (lane8 >= base) & (lane8 < base + BLK)
    cols = jnp.where(inside, jnp.where(lane8 == row8 + base, -1.0, 0.0), cols)
    left, right = stacks(cols, block)
    row_id = lax.broadcasted_iota(jnp.int32, (width, width), 0)
    lane_id = lax.broadcasted_iota(jnp.int32, (width, width), 1)
    row_out = (row_id < base) | (row_id >= base + BLK)
    lane_out = (lane_id < base) | (lane_id >= base + BLK)
    keep = row_out & lane_out
    mat[...] = jnp.where(keep, mat[...], 0.0) - dot_tn(left, right)
    mat_t[...] = jnp.where(keep, mat_t[...], 0.0) - dot_tn(right, left)


def main_kernel(p_hbm, t_hbm, gat_out, upper, zt,
                gat, tv, tb, g_loc, pr, yr, gz, gf, p1w, p1s, p1f, m_loc, pm, mz, zsum, work, work_t,
                gp_send, gp_recv, loc, out_sem, st_send, st_recv, p1_send, ready):
    width, part = p_hbm.shape
    half = width // 2
    rows = t_hbm.shape[0]
    tail = tb.shape[2]
    main = part - tail
    space = lax.axis_index("space")
    y = lax.axis_index("col")
    core = space % NCORE
    z = (space // NCORE) % NZ
    x = space // (NCORE * NZ)
    pair = x * NCORE + core
    plane = pair * NY + y
    right, left, far = (y + 1) % NY, (y + NY - 1) % NY, (y + 2) % NY
    root = (space == 0) & (y == 0)

    def at_z(zz):
        return (x * (NZ * NCORE) + zz * NCORE + core, y)

    def at_plane(q):
        return at_pair(q // NY)[0], q % NY

    def at_y(yy):
        return (space, yy)

    def at_pair(q):
        return ((q // NCORE) * (NZ * NCORE) + z * NCORE + q % NCORE, y)

    def loop(low, high, body):
        lax.fori_loop(low, high, lambda i, c: (body(i), c)[1], 0)

    def send(src, dst, stage, device):
        pltpu.make_async_remote_copy(
            src_ref=src, dst_ref=dst, send_sem=st_send.at[stage], recv_sem=st_recv.at[stage],
            device_id=device, device_id_type=MESH).start()

    def settle(ref, sem):
        pltpu.make_async_copy(ref, ref, sem).wait()

    def rows_of(i, size):
        return pl.ds(pl.multiple_of(i * size, size), size)

    barrier = pltpu.get_barrier_semaphore()

    def greet(device):
        pl.semaphore_signal(barrier, inc=1, device_id=device, device_id_type=MESH)

    own = pltpu.make_async_copy(p_hbm, gat.at[y], loc.at[0])
    own.start()
    greet(at_z((z + 1) % NZ))
    greet(at_z((z + NZ - 1) % NZ))
    loop(1, NY, lambda d: greet(at_y((y + d) % NY)))
    loop(1, PAIRS, lambda d: greet(at_pair((pair + d) % PAIRS)))
    own.wait()
    high, low = split2(gat[y])
    both = dot_nt(high, jnp.concatenate([high, low], axis=0))
    cross = both[:, width:]
    g_loc[...] = both[:, :width] + cross + cross.T
    pl.semaphore_wait(barrier, PAIRS + NY)

    def announce(level, step):
        for zz in ((z + step) % NZ, (z + NZ - step) % NZ):
            pl.semaphore_signal(ready.at[level], inc=1, device_id=at_z(zz), device_id_type=MESH)

    announce(0, 1)

    def gather_copy(src, dst, index, target):
        return pltpu.make_async_remote_copy(
            src_ref=src, dst_ref=dst, send_sem=gp_send.at[index], recv_sem=gp_recv.at[index],
            device_id=(space, target), device_id_type=MESH)

    def share(start, size, cols, index, target):
        lines = pl.ds(start, size)
        copy = gather_copy(p_hbm.at[lines, cols], gat.at[y, lines, cols], index, target)
        copy.start()
        return copy

    def forward(block, lines, cols, index, target):
        ref = gat.at[block, lines, cols]
        copy = gather_copy(ref, ref, index, target)
        copy.start()
        return copy

    loop(1, PAIRS, lambda d: send(g_loc.at[rows_of((pair + d) % PAIRS, PIECE)], pr.at[d - 1], 0,
                                  at_pair((pair + d) % PAIRS)))
    head = 32
    first, second = pl.ds(0, half), pl.ds(half, half)
    cols_a, cols_b = pl.ds(0, main), pl.ds(main, tail)
    ra0 = share(0, head, cols_a, 6, right)
    lb0 = share(half, head, cols_a, 7, left)
    pl.semaphore_wait(ready.at[0], 2)
    announce(1, 2)

    @pl.when(root)
    def _():
        for d in range(1, NY):
            pltpu.make_async_remote_copy(
                src_ref=gat.at[0, :, pl.ds(0, width)], dst_ref=p1w, send_sem=p1_send.at[d - 1],
                recv_sem=st_recv.at[3], device_id=at_y(d), device_id_type=MESH).start()
        p1w[...] = gat[0, :, 0:width]

    settle(pr, st_recv.at[0])
    total = g_loc[rows_of(pair, PIECE), :]
    for d in range(PAIRS - 1):
        total = total + pr[d]
    yr[y] = total
    loop(1, NY, lambda d: send(yr.at[y], yr.at[y], 10, at_y((y + d) % NY)))
    ra = share(head, half - head, cols_a, 0, right)
    lb = share(half + head, half - head, cols_a, 1, left)
    rb = share(half, half, cols_a, 2, right)
    la = share(0, half, cols_a, 3, left)
    swaps = []
    for index, target in ((8, right), (9, left), (10, far)):
        cols = pl.ds(pl.multiple_of(target * part + main, LANES), tail)
        swaps.append(gather_copy(t_hbm.at[:, cols], tb.at[y], index, target))
        swaps[-1].start()
    loads = [pltpu.make_async_copy(t_hbm.at[:, pl.ds(c * part, part)], tv.at[c], loc.at[1 + c])
             for c in range(NY)]
    for load in loads:
        load.start()
    pl.semaphore_wait(ready.at[1], 2)
    announce(2, 4)
    settle(yr.at[pl.ds(0, NY - 1)], st_recv.at[10])
    total = yr[0]
    for q in range(1, NY):
        total = total + yr[q]
    gz[z] = total
    pl.semaphore_wait(ready.at[2], 2)
    loop(1, NZ, lambda d: send(gz.at[z], gz.at[z], 1, at_z((z + d) % NZ)))

    @pl.when((space == 0) & (y > 0))
    def _():
        settle(p1w, st_recv.at[3])

    @pl.when(space == 0)
    def _():
        loop(1, PAIRS, lambda q: send(p1w.at[rows_of(q, PIECE)], p1s, 4, at_pair(q)))
        p1s[...] = p1w[0:PIECE, :]

    @pl.when((z == 0) & (pair > 0))
    def _():
        settle(p1s, st_recv.at[4])

    @pl.when(z == 0)
    def _():
        loop(1, NZ, lambda d: send(p1s, p1s, 5, at_z(d)))

    for load in loads:
        load.wait()

    def products(trail, block):
        ph, pl_ = split2(block)
        th, tl = split2(trail)
        four = dot_nt(jnp.concatenate([th, tl], axis=0), jnp.concatenate([ph, pl_], axis=0))
        n = th.shape[0]
        return (four[:n, :width] + four[n:, :width]) + (four[:n, width:] + four[n:, width:])

    outs = []

    def put_out(c, cols):
        copy = pltpu.make_async_copy(gat.at[c, :, cols], gat_out.at[c, :, cols],
                                     out_sem.at[len(outs)])
        copy.start()
        outs.append(copy)

    def add_main(c):
        m_loc[0] += products(tv[c, :, 0:main], gat[c, :, 0:main])
        put_out(c, cols_a)

    m_loc[0] = products(tv[y], gat[y])
    put_out(y, pl.ds(0, part))

    ra0.wait_recv()
    ra.wait_recv()
    fa = forward(left, first, cols_a, 4, right)
    lb0.wait_recv()
    lb.wait_recv()
    fb = forward(right, second, cols_a, 5, left)

    settle(gz.at[pl.ds(0, NZ - 1)], st_recv.at[1])
    total = gz[0]
    for q in range(1, NZ):
        total = total + gz[q]
    mine = rows_of(pair, PIECE)
    gf[mine, :] = total
    loop(1, PAIRS, lambda d: send(gf.at[mine], gf.at[mine], 2, at_pair((pair + d) % PAIRS)))

    @pl.when(z > 0)
    def _():
        settle(p1s, st_recv.at[5])

    p1f[mine, :] = p1s[...]
    loop(1, PAIRS, lambda d: send(p1f.at[mine], p1f.at[mine], 6, at_pair((pair + d) % PAIRS)))

    others = pl.ds(0, (PAIRS - 1) * PIECE)
    settle(gf.at[others], st_recv.at[2])
    work[...] = gf[...]
    loop(0, width // BLK, lambda k: chol_step(k, work, upper))
    rb.wait_recv()
    add_main(left)
    la.wait_recv()
    add_main(right)
    settle(p1f.at[others], st_recv.at[6])
    work[...] = gf[...] + jnp.dot(p1f[...], upper[...], precision=HIGHEST, preferred_element_type=F32)
    work_t[...] = work[...].T
    loop(0, EARLY, lambda k: inverse_step(k, work, work_t))

    @pl.when(space == 0)
    def _():
        m_loc[0] += jnp.dot(tv[0, :, 0:width], upper[...], precision=HIGHEST,
                            preferred_element_type=F32)

    for swap in swaps:
        swap.wait_recv()
    others_t = jnp.concatenate([tb[right], tb[far], tb[left]], axis=0)
    swapped = products(others_t, gat[y, :, main:part])
    for r in range(1, NY):
        m_loc[r] = swapped[(r - 1) * rows:r * rows, :]
    fa.wait_recv()
    fb.wait_recv()
    add_main(far)

    def scatter(d):
        q = (plane + d) % PLANE
        ahead = (q % NY - y + NY) % NY
        send(m_loc.at[ahead, rows_of(q // NY, BLK)], pm.at[d - 1], 7, at_plane(q))

    loop(1, PLANE, scatter)
    ra_b = share(0, half, cols_b, 11, right)
    lb_b = share(half, half, cols_b, 12, left)
    rb_b = share(half, half, cols_b, 13, right)
    la_b = share(0, half, cols_b, 14, left)
    loop(EARLY, width // BLK, lambda k: inverse_step(k, work, work_t))
    settle(pm, st_recv.at[7])
    tile = rows_of(pair, BLK)
    total = m_loc[0, tile, :]
    for d in range(PLANE - 1):
        total = total + pm[d]
    mz[z] = total
    loop(1, NZ, lambda d: send(mz.at[z], mz.at[z], 8, at_z((z + d) % NZ)))
    ra_b.wait_recv()
    fa_b = forward(left, first, cols_b, 15, right)
    lb_b.wait_recv()
    fb_b = forward(right, second, cols_b, 16, left)
    settle(mz.at[pl.ds(0, NZ - 1)], st_recv.at[8])
    total = mz[0]
    for q in range(1, NZ):
        total = total + mz[q]
    zsum[tile, :] = jnp.dot(total, work[...], precision=HIGHEST, preferred_element_type=F32)
    loop(1, PAIRS, lambda d: send(zsum.at[tile], zsum.at[tile], 9, at_pair((pair + d) % PAIRS)))
    settle(zsum.at[pl.ds(0, (PAIRS - 1) * BLK)], st_recv.at[9])
    zt[...] = zsum[...]
    rb_b.wait_recv()
    put_out(left, cols_b)
    la_b.wait_recv()
    put_out(right, cols_b)
    fa_b.wait_recv()
    fb_b.wait_recv()
    put_out(far, cols_b)

    for copy in (ra0, lb0, ra, lb, rb, la, fa, fb, *swaps, ra_b, lb_b, rb_b, la_b, fa_b, fb_b):
        copy.wait_send()
    for copy in outs:
        copy.wait()
    settle(pr, st_send.at[0])
    settle(gz.at[pl.ds(0, NZ - 1)], st_send.at[1])
    settle(gf.at[others], st_send.at[2])

    @pl.when(root)
    def _():
        for d in range(1, NY):
            settle(p1w, p1_send.at[d - 1])

    @pl.when(space == 0)
    def _():
        settle(gf.at[others], st_send.at[4])

    @pl.when(z == 0)
    def _():
        settle(gz.at[pl.ds(0, NZ - 1)], st_send.at[5])

    settle(gf.at[others], st_send.at[6])
    settle(pm, st_send.at[7])
    settle(mz.at[pl.ds(0, NZ - 1)], st_send.at[8])
    settle(zsum.at[pl.ds(0, (PAIRS - 1) * BLK)], st_send.at[9])
    settle(yr.at[pl.ds(0, NY - 1)], st_send.at[10])


def update_kernel(scale, p_ref, t_ref, zt_ref, upper_ref, up_ref, out_ref, new, out_sem):
    zt = zt_ref[...]
    rows, width = zt.shape
    part = p_ref.shape[2]
    zh, zl = split2(zt)
    pair = jnp.concatenate([zh, zl], axis=0)
    copies = []
    for c in range(NY):
        cols = pl.ds(c * part, part)
        ph, pl_ = split2(p_ref[c])
        double = jnp.dot(pair, ph, preferred_element_type=F32)
        cross = jnp.dot(zh, pl_, preferred_element_type=F32)
        new[c] = t_ref[:, cols] - (double[:rows] + (double[rows:] + cross))
        if c == 0:
            @pl.when(lax.axis_index("space") == 0)
            def _():
                new[0, :, 0:width] -= lax.dot_general(
                    zt, upper_ref[...], (((1,), (1,)), ((), ())), precision=HIGHEST,
                    preferred_element_type=F32)
        copy = pltpu.make_async_copy(new.at[c], out_ref.at[:, cols], out_sem.at[c])
        copy.start()
        copies.append(copy)
    up_ref[...] = upper_ref[...] * scale
    for copy in copies:
        copy.wait()


def per_device(panel, trailing):
    width, part = panel.shape
    rows, block = trailing.shape
    tail = part // LANES * 2 // 5 * LANES
    rows_total = block * lax.axis_size("space")
    vmem = pl.BlockSpec(memory_space=pltpu.VMEM)
    hbm = pl.BlockSpec(memory_space=pltpu.HBM)
    anywhere = pl.BlockSpec(memory_space=pl.ANY)

    def buf(*shape):
        return pltpu.VMEM(shape, F32)

    gat, upper, zt = pl.pallas_call(
        main_kernel,
        out_shape=(
            jax.ShapeDtypeStruct((NY, width, part), F32),
            jax.ShapeDtypeStruct((width, width), F32),
            jax.ShapeDtypeStruct((rows, width), F32),
        ),
        in_specs=[hbm, hbm],
        out_specs=(anywhere, vmem, vmem),
        scratch_shapes=[
            buf(NY, width, part),
            buf(NY, rows, part),
            buf(NY, rows, tail),
            buf(width, width),
            buf(PAIRS - 1, PIECE, width),
            buf(NY, PIECE, width),
            buf(NZ, PIECE, width),
            buf(width, width),
            buf(width, width),
            buf(PIECE, width),
            buf(width, width),
            buf(NY, rows, width),
            buf(PLANE - 1, BLK, width),
            buf(NZ, BLK, width),
            buf(rows, width),
            buf(width, width),
            buf(width, width),
            pltpu.SemaphoreType.DMA((17,)),
            pltpu.SemaphoreType.DMA((17,)),
            pltpu.SemaphoreType.DMA((1 + NY,)),
            pltpu.SemaphoreType.DMA((2 * NY - 1,)),
            pltpu.SemaphoreType.DMA((11,)),
            pltpu.SemaphoreType.DMA((11,)),
            pltpu.SemaphoreType.DMA((NY - 1,)),
            pltpu.SemaphoreType.REGULAR((3,)),
        ],
        compiler_params=pltpu.CompilerParams(
            collective_id=0, has_side_effects=True, vmem_limit_bytes=40 * 2**20),
        name="reduce_factor",
    )(pltpu.with_memory_space_constraint(panel, pltpu.HBM),
      pltpu.with_memory_space_constraint(trailing, pltpu.HBM))

    upper_factor, updated = pl.pallas_call(
        functools.partial(update_kernel, -1.0 / math.sqrt(rows_total)),
        out_shape=(
            jax.ShapeDtypeStruct((width, width), F32),
            jax.ShapeDtypeStruct((rows, block), F32),
        ),
        in_specs=[vmem] * 4,
        out_specs=(vmem, hbm),
        scratch_shapes=[buf(NY, rows, part), pltpu.SemaphoreType.DMA((NY,))],
        compiler_params=pltpu.CompilerParams(vmem_limit_bytes=40 * 2**20),
        name="apply_update",
    )(gat, trailing, zt, upper)
    return (upper_factor, updated)


def solution(mesh):
    return jax.shard_map(
        per_device,
        mesh=mesh,
        in_specs=(P(None, ("space", "col")), P("col", "space")),
        out_specs=(P(), P("col", "space")),
        check_vma=False,
    )
```

```python
import functools
import math

import jax
import jax.numpy as jnp
from jax import lax
from jax.experimental import pallas as pl
from jax.experimental.pallas import tpu as pltpu
from jax.sharding import PartitionSpec as P

F32 = jnp.float32
BF16 = jnp.bfloat16
HIGHEST = lax.Precision.HIGHEST
MESH = pl.DeviceIdType.MESH
NX, NZ, NCORE, NY = 4, 16, 2, 4
PAIRS = NX * NCORE
BLK = 8
LANES = 128
PIECE = 16
EARLY, MIDDLE = 5, 12
PLANE = PAIRS * NY


def split2(x):
    high = x.astype(BF16)
    low = (x - high.astype(F32)).astype(BF16)
    return high, low


def split3(x):
    high = x.astype(BF16).astype(F32)
    rest = x - high
    mid = rest.astype(BF16).astype(F32)
    return high, mid, rest - mid


def stacks(a, b):
    ah, am, al = split3(a)
    bh, bm, bl = split3(b)
    left = jnp.concatenate([ah, ah, ah, am, am, al], axis=0).astype(BF16)
    right = jnp.concatenate([bh, bm, bl, bh, bm, bh], axis=0).astype(BF16)
    return left, right


def dot_tn(a, b):
    return lax.dot_general(a, b, (((0,), (0,)), ((), ())), preferred_element_type=F32)


def dot_nt(a, b):
    return lax.dot_general(a, b, (((1,), (1,)), ((), ())), preferred_element_type=F32)


def recip(x):
    y = pl.reciprocal(x, approx=True)
    return y * (2.0 - x * y)


def lane_splat(x, lane):
    return jnp.take_along_axis(x, jnp.full(x.shape, lane, jnp.int32), axis=1)


def merge(rows, row8):
    out = rows[0]
    for i in range(1, len(rows)):
        out = jnp.where(row8 == i, rows[i], out)
    return out


def block_rows(ref, base):
    width = ref.shape[1]
    return [jnp.broadcast_to(ref[pl.ds(base + i, 1), :], (BLK, width)) for i in range(BLK)]


def chol_step(k, work, upper):
    width = work.shape[1]
    row8 = lax.broadcasted_iota(jnp.int32, (BLK, width), 0)
    lane8 = lax.broadcasted_iota(jnp.int32, (BLK, width), 1)
    base = pl.multiple_of(k * BLK, BLK)
    rows = block_rows(work, base)
    s = {(i, j): lane_splat(rows[i], base + j) for i in range(BLK) for j in range(i, BLK)}
    for j in range(BLK):
        inv = recip(s[j, j])
        for i in range(j + 1, BLK):
            factor = s[j, i] * inv
            for l in range(i, BLK):
                s[i, l] = s[i, l] - factor * s[j, l]
            rows[i] = rows[i] - factor * rows[j]
    pivots = merge([s[j, j] for j in range(BLK)], row8)
    block = merge(rows, row8) * lax.rsqrt(pivots)
    block = jnp.where(lane8 >= row8 + base, block, 0.0)
    upper[pl.ds(base, BLK), :] = block
    left, right = stacks(block, block)
    work[...] -= dot_tn(left, right)


def inverse_step(k, mat, mat_t):
    width = mat.shape[1]
    row8 = lax.broadcasted_iota(jnp.int32, (BLK, width), 0)
    lane8 = lax.broadcasted_iota(jnp.int32, (BLK, width), 1)
    base = pl.multiple_of(k * BLK, BLK)
    rows = block_rows(mat, base)
    cols = mat_t[pl.ds(base, BLK), :]
    s = {(i, j): lane_splat(rows[i], base + j) for i in range(BLK) for j in range(BLK)}
    for j in range(BLK):
        inv = recip(s[j, j])
        at = lane8 == base + j
        scaled = jnp.where(at, 1.0, rows[j]) * inv
        for l in range(j + 1, BLK):
            s[j, l] = s[j, l] * inv
        for i in range(BLK):
            if i == j:
                continue
            for l in range(j + 1, BLK):
                s[i, l] = s[i, l] - s[i, j] * s[j, l]
            rows[i] = jnp.where(at, 0.0, rows[i]) - s[i, j] * scaled
        rows[j] = scaled
    block = merge(rows, row8)
    inside = (lane8 >= base) & (lane8 < base + BLK)
    cols = jnp.where(inside, jnp.where(lane8 == row8 + base, -1.0, 0.0), cols)
    left, right = stacks(cols, block)
    row_id = lax.broadcasted_iota(jnp.int32, (width, width), 0)
    lane_id = lax.broadcasted_iota(jnp.int32, (width, width), 1)
    row_out = (row_id < base) | (row_id >= base + BLK)
    lane_out = (lane_id < base) | (lane_id >= base + BLK)
    keep = row_out & lane_out
    mat[...] = jnp.where(keep, mat[...], 0.0) - dot_tn(left, right)
    mat_t[...] = jnp.where(keep, mat_t[...], 0.0) - dot_tn(right, left)


def main_kernel(p_hbm, t_hbm, gat_out, upper, zt,
                gat, tv, tb, g_loc, pr, yr, gz, gf, p1w, p1s, p1f, m_loc, pm, mz, zsum, work, work_t,
                gp_send, gp_recv, loc, out_sem, st_send, st_recv, p1_send, ready):
    width, part = p_hbm.shape
    half = width // 2
    rows = t_hbm.shape[0]
    tail = tb.shape[2]
    main = part - tail
    space = lax.axis_index("space")
    y = lax.axis_index("col")
    core = space % NCORE
    z = (space // NCORE) % NZ
    x = space // (NCORE * NZ)
    pair = x * NCORE + core
    right, left, far = (y + 1) % NY, (y + NY - 1) % NY, (y + 2) % NY
    root = (space == 0) & (y == 0)

    z_order = sorted(range(1, NZ), key=lambda d: -min(d, NZ - d))
    plane_order = sorted(
        ((dx, dc, dy) for dx in range(NX) for dc in range(NCORE) for dy in range(NY)),
        key=lambda d: -(min(d[0], NX - d[0]) + d[1] + min(d[2], NY - d[2])))[:-1]
    pair_order = [(dx, dc) for dx, dc, dy in plane_order if dy == 0]

    def pair_at(dx, dc):
        return ((x + dx) % NX) * NCORE + (core + dc) % NCORE

    def to_pairs(src, dst, stage):
        for n, (dx, dc) in enumerate(pair_order):
            q = pair_at(dx, dc)
            send(src(q), dst(n), stage, at_pair(q))

    def to_z(ref, stage):
        for d in z_order:
            send(ref, ref, stage, at_z((z + d) % NZ))

    def at_z(zz):
        return (x * (NZ * NCORE) + zz * NCORE + core, y)

    def at_y(yy):
        return (space, yy)

    def at_pair(q):
        return ((q // NCORE) * (NZ * NCORE) + z * NCORE + q % NCORE, y)

    def loop(low, high, body):
        lax.fori_loop(low, high, lambda i, c: (body(i), c)[1], 0)

    def send(src, dst, stage, device):
        pltpu.make_async_remote_copy(
            src_ref=src, dst_ref=dst, send_sem=st_send.at[stage], recv_sem=st_recv.at[stage],
            device_id=device, device_id_type=MESH).start()

    def settle(ref, sem):
        pltpu.make_async_copy(ref, ref, sem).wait()

    def rows_of(i, size):
        return pl.ds(pl.multiple_of(i * size, size), size)

    barrier = pltpu.get_barrier_semaphore()

    def greet(device):
        pl.semaphore_signal(barrier, inc=1, device_id=device, device_id_type=MESH)

    own = pltpu.make_async_copy(p_hbm, gat.at[y], loc.at[0])
    own.start()
    greet(at_z((z + 1) % NZ))
    greet(at_z((z + NZ - 1) % NZ))
    loop(1, NY, lambda d: greet(at_y((y + d) % NY)))
    loop(1, PAIRS, lambda d: greet(at_pair((pair + d) % PAIRS)))
    pl.semaphore_wait(barrier, PAIRS + NY)

    def announce(level, step):
        for zz in ((z + step) % NZ, (z + NZ - step) % NZ):
            pl.semaphore_signal(ready.at[level], inc=1, device_id=at_z(zz), device_id_type=MESH)

    announce(0, 1)

    def gather_copy(src, dst, index, target):
        return pltpu.make_async_remote_copy(
            src_ref=src, dst_ref=dst, send_sem=gp_send.at[index], recv_sem=gp_recv.at[index],
            device_id=(space, target), device_id_type=MESH)

    def share(start, size, cols, index, target):
        lines = pl.ds(start, size)
        copy = gather_copy(p_hbm.at[lines, cols], gat.at[y, lines, cols], index, target)
        copy.start()
        return copy

    def forward(block, lines, cols, index, target):
        ref = gat.at[block, lines, cols]
        copy = gather_copy(ref, ref, index, target)
        copy.start()
        return copy

    head = 48
    first, second = pl.ds(0, half), pl.ds(half, half)
    cols_a, cols_b = pl.ds(0, main), pl.ds(main, tail)
    ra0 = share(0, head, cols_a, 6, right)
    lb0 = share(half, head, cols_a, 7, left)
    own.wait()
    high, low = split2(gat[y])
    both = dot_nt(high, jnp.concatenate([high, low], axis=0))
    cross = both[:, width:]
    g_loc[...] = both[:, :width] + cross + cross.T
    to_pairs(lambda q: g_loc.at[rows_of(q, PIECE)], lambda n: pr.at[n], 0)
    pl.semaphore_wait(ready.at[0], 2)
    announce(1, 2)

    @pl.when(root)
    def _():
        for d in range(1, NY):
            pltpu.make_async_remote_copy(
                src_ref=gat.at[0, :, pl.ds(0, width)], dst_ref=p1w, send_sem=p1_send.at[d - 1],
                recv_sem=st_recv.at[3], device_id=at_y(d), device_id_type=MESH).start()
        p1w[...] = gat[0, :, 0:width]

    settle(pr, st_recv.at[0])
    total = g_loc[rows_of(pair, PIECE), :]
    for d in range(PAIRS - 1):
        total = total + pr[d]
    yr[y] = total
    loop(1, NY, lambda d: send(yr.at[y], yr.at[y], 10, at_y((y + d) % NY)))
    ra = share(head, half - head, cols_a, 0, right)
    lb = share(half + head, half - head, cols_a, 1, left)
    rb = share(half, half, cols_a, 2, right)
    la = share(0, half, cols_a, 3, left)
    swaps = []
    for index, target in ((8, right), (9, left), (10, far)):
        cols = pl.ds(pl.multiple_of(target * part + main, LANES), tail)
        swaps.append(gather_copy(t_hbm.at[:, cols], tb.at[y], index, target))
        swaps[-1].start()
    loads = [pltpu.make_async_copy(t_hbm.at[:, pl.ds(c * part, part)], tv.at[c], loc.at[1 + c])
             for c in range(NY)]
    for load in loads:
        load.start()
    pl.semaphore_wait(ready.at[1], 2)
    announce(2, 4)
    settle(yr.at[pl.ds(0, NY - 1)], st_recv.at[10])
    total = yr[0]
    for q in range(1, NY):
        total = total + yr[q]
    gz[z] = total
    pl.semaphore_wait(ready.at[2], 2)
    to_z(gz.at[z], 1)

    @pl.when((space == 0) & (y > 0))
    def _():
        settle(p1w, st_recv.at[3])

    @pl.when(space == 0)
    def _():
        loop(1, PAIRS, lambda q: send(p1w.at[rows_of(q, PIECE)], p1s, 4, at_pair(q)))
        p1s[...] = p1w[0:PIECE, :]

    @pl.when((z == 0) & (pair > 0))
    def _():
        settle(p1s, st_recv.at[4])

    @pl.when(z == 0)
    def _():
        loop(1, NZ, lambda d: send(p1s, p1s, 5, at_z(d)))

    for load in loads:
        load.wait()

    def products(trail, block):
        ph, pl_ = split2(block)
        th, tl = split2(trail)
        four = dot_nt(jnp.concatenate([th, tl], axis=0), jnp.concatenate([ph, pl_], axis=0))
        n = th.shape[0]
        return (four[:n, :width] + four[n:, :width]) + (four[:n, width:] + four[n:, width:])

    outs = []

    def put_out(c, cols):
        copy = pltpu.make_async_copy(gat.at[c, :, cols], gat_out.at[c, :, cols],
                                     out_sem.at[len(outs)])
        copy.start()
        outs.append(copy)

    def add_main(c):
        m_loc[0] += products(tv[c, :, 0:main], gat[c, :, 0:main])
        put_out(c, cols_a)

    m_loc[0] = products(tv[y], gat[y])
    put_out(y, pl.ds(0, part))

    ra0.wait_recv()
    ra.wait_recv()
    fa = forward(left, first, cols_a, 4, right)
    lb0.wait_recv()
    lb.wait_recv()
    fb = forward(right, second, cols_a, 5, left)

    settle(gz.at[pl.ds(0, NZ - 1)], st_recv.at[1])
    total = gz[0]
    for q in range(1, NZ):
        total = total + gz[q]
    mine = rows_of(pair, PIECE)
    gf[mine, :] = total
    to_pairs(lambda q: gf.at[mine], lambda n: gf.at[mine], 2)

    @pl.when(z > 0)
    def _():
        settle(p1s, st_recv.at[5])

    p1f[mine, :] = p1s[...]
    to_pairs(lambda q: p1f.at[mine], lambda n: p1f.at[mine], 6)

    others = pl.ds(0, (PAIRS - 1) * PIECE)
    settle(gf.at[others], st_recv.at[2])
    work[...] = gf[...]
    loop(0, width // BLK, lambda k: chol_step(k, work, upper))
    rb.wait_recv()
    add_main(left)
    la.wait_recv()
    add_main(right)
    settle(p1f.at[others], st_recv.at[6])
    work[...] = gf[...] + jnp.dot(p1f[...], upper[...], precision=HIGHEST, preferred_element_type=F32)
    work_t[...] = work[...].T
    loop(0, EARLY, lambda k: inverse_step(k, work, work_t))

    @pl.when(space == 0)
    def _():
        m_loc[0] += jnp.dot(tv[0, :, 0:width], upper[...], precision=HIGHEST,
                            preferred_element_type=F32)

    for swap in swaps:
        swap.wait_recv()
    others_t = jnp.concatenate([tb[right], tb[far], tb[left]], axis=0)
    swapped = products(others_t, gat[y, :, main:part])
    for r in range(1, NY):
        m_loc[r] = swapped[(r - 1) * rows:r * rows, :]
    fa.wait_recv()
    fb.wait_recv()
    add_main(far)

    for n, (dx, dc, dy) in enumerate(plane_order):
        q = pair_at(dx, dc)
        send(m_loc.at[dy, rows_of(q, BLK)], pm.at[n], 7, (at_pair(q)[0], (y + dy) % NY))
    ra_b = share(0, half, cols_b, 11, right)
    lb_b = share(half, half, cols_b, 12, left)
    rb_b = share(half, half, cols_b, 13, right)
    la_b = share(0, half, cols_b, 14, left)
    loop(EARLY, MIDDLE, lambda k: inverse_step(k, work, work_t))
    settle(pm, st_recv.at[7])
    tile = rows_of(pair, BLK)
    total = m_loc[0, tile, :]
    for d in range(PLANE - 1):
        total = total + pm[d]
    mz[z] = total
    to_z(mz.at[z], 8)
    loop(MIDDLE, width // BLK, lambda k: inverse_step(k, work, work_t))
    ra_b.wait_recv()
    fa_b = forward(left, first, cols_b, 15, right)
    lb_b.wait_recv()
    fb_b = forward(right, second, cols_b, 16, left)
    settle(mz.at[pl.ds(0, NZ - 1)], st_recv.at[8])
    total = mz[0]
    for q in range(1, NZ):
        total = total + mz[q]
    zsum[tile, :] = jnp.dot(total, work[...], precision=HIGHEST, preferred_element_type=F32)
    to_pairs(lambda q: zsum.at[tile], lambda n: zsum.at[tile], 9)
    rb_b.wait_recv()
    put_out(left, cols_b)
    la_b.wait_recv()
    put_out(right, cols_b)
    fa_b.wait_recv()
    fb_b.wait_recv()
    put_out(far, cols_b)
    settle(zsum.at[pl.ds(0, (PAIRS - 1) * BLK)], st_recv.at[9])
    zt[...] = zsum[...]

    for copy in (ra0, lb0, ra, lb, rb, la, fa, fb, *swaps, ra_b, lb_b, rb_b, la_b, fa_b, fb_b):
        copy.wait_send()
    for copy in outs:
        copy.wait()
    settle(pr, st_send.at[0])
    settle(gz.at[pl.ds(0, NZ - 1)], st_send.at[1])
    settle(gf.at[others], st_send.at[2])

    @pl.when(root)
    def _():
        for d in range(1, NY):
            settle(p1w, p1_send.at[d - 1])

    @pl.when(space == 0)
    def _():
        settle(gf.at[others], st_send.at[4])

    @pl.when(z == 0)
    def _():
        settle(gz.at[pl.ds(0, NZ - 1)], st_send.at[5])

    settle(gf.at[others], st_send.at[6])
    settle(pm, st_send.at[7])
    settle(mz.at[pl.ds(0, NZ - 1)], st_send.at[8])
    settle(zsum.at[pl.ds(0, (PAIRS - 1) * BLK)], st_send.at[9])
    settle(yr.at[pl.ds(0, NY - 1)], st_send.at[10])


def update_kernel(scale, p_ref, t_ref, zt_ref, upper_ref, up_ref, out_ref, new, out_sem):
    zt = zt_ref[...]
    rows, width = zt.shape
    part = p_ref.shape[2]
    zh, zl = split2(zt)
    quad = jnp.concatenate([jnp.concatenate([zh, zh], axis=1),
                            jnp.concatenate([zl, zl], axis=1)], axis=0)
    copies = []
    for c in range(NY):
        cols = pl.ds(c * part, part)
        ph, pl_ = split2(p_ref[c])
        both = jnp.dot(quad, jnp.concatenate([ph, pl_], axis=0), preferred_element_type=F32)
        new[c] = t_ref[:, cols] - (both[:rows] + both[rows:])
        if c == 0:
            @pl.when(lax.axis_index("space") == 0)
            def _():
                new[0, :, 0:width] -= lax.dot_general(
                    zt, upper_ref[...], (((1,), (1,)), ((), ())), precision=HIGHEST,
                    preferred_element_type=F32)
        copy = pltpu.make_async_copy(new.at[c], out_ref.at[:, cols], out_sem.at[c])
        copy.start()
        copies.append(copy)
    up_ref[...] = upper_ref[...] * scale
    for copy in copies:
        copy.wait()


def per_device(panel, trailing):
    width, part = panel.shape
    rows, block = trailing.shape
    tail = part // LANES * 2 // 5 * LANES
    rows_total = block * lax.axis_size("space")
    vmem = pl.BlockSpec(memory_space=pltpu.VMEM)
    hbm = pl.BlockSpec(memory_space=pltpu.HBM)
    anywhere = pl.BlockSpec(memory_space=pl.ANY)

    def buf(*shape):
        return pltpu.VMEM(shape, F32)

    gat, upper, zt = pl.pallas_call(
        main_kernel,
        out_shape=(
            jax.ShapeDtypeStruct((NY, width, part), F32),
            jax.ShapeDtypeStruct((width, width), F32),
            jax.ShapeDtypeStruct((rows, width), F32),
        ),
        in_specs=[hbm, hbm],
        out_specs=(anywhere, vmem, vmem),
        scratch_shapes=[
            buf(NY, width, part),
            buf(NY, rows, part),
            buf(NY, rows, tail),
            buf(width, width),
            buf(PAIRS - 1, PIECE, width),
            buf(NY, PIECE, width),
            buf(NZ, PIECE, width),
            buf(width, width),
            buf(width, width),
            buf(PIECE, width),
            buf(width, width),
            buf(NY, rows, width),
            buf(PLANE - 1, BLK, width),
            buf(NZ, BLK, width),
            buf(rows, width),
            buf(width, width),
            buf(width, width),
            pltpu.SemaphoreType.DMA((17,)),
            pltpu.SemaphoreType.DMA((17,)),
            pltpu.SemaphoreType.DMA((1 + NY,)),
            pltpu.SemaphoreType.DMA((2 * NY - 1,)),
            pltpu.SemaphoreType.DMA((11,)),
            pltpu.SemaphoreType.DMA((11,)),
            pltpu.SemaphoreType.DMA((NY - 1,)),
            pltpu.SemaphoreType.REGULAR((3,)),
        ],
        compiler_params=pltpu.CompilerParams(
            collective_id=0, has_side_effects=True, vmem_limit_bytes=40 * 2**20),
        name="reduce_factor",
    )(pltpu.with_memory_space_constraint(panel, pltpu.HBM),
      pltpu.with_memory_space_constraint(trailing, pltpu.HBM))

    upper_factor, updated = pl.pallas_call(
        functools.partial(update_kernel, -1.0 / math.sqrt(rows_total)),
        out_shape=(
            jax.ShapeDtypeStruct((width, width), F32),
            jax.ShapeDtypeStruct((rows, block), F32),
        ),
        in_specs=[vmem] * 4,
        out_specs=(vmem, hbm),
        scratch_shapes=[buf(NY, rows, part), pltpu.SemaphoreType.DMA((NY,))],
        compiler_params=pltpu.CompilerParams(vmem_limit_bytes=40 * 2**20),
        name="apply_update",
    )(gat, trailing, zt, upper)
    return (upper_factor, updated)


def solution(mesh):
    return jax.shard_map(
        per_device,
        mesh=mesh,
        in_specs=(P(None, ("space", "col")), P("col", "space")),
        out_specs=(P(), P("col", "space")),
        check_vma=False,
    )
```

```python
import functools
import math

import jax
import jax.numpy as jnp
from jax import lax
from jax.experimental import pallas as pl
from jax.experimental.pallas import tpu as pltpu
from jax.sharding import PartitionSpec as P

F32 = jnp.float32
BF16 = jnp.bfloat16
HIGHEST = lax.Precision.HIGHEST
MESH = pl.DeviceIdType.MESH
NX, NZ, NCORE, NY = 4, 16, 2, 4
PAIRS = NX * NCORE
BLK = 8
LANES = 128
PIECE = 16
EARLY, MIDDLE = 5, 12
PLANE = PAIRS * NY


def split2(x):
    high = x.astype(BF16)
    low = (x - high.astype(F32)).astype(BF16)
    return high, low


def split3(x):
    high = x.astype(BF16).astype(F32)
    rest = x - high
    mid = rest.astype(BF16).astype(F32)
    return high, mid, rest - mid


def stacks(a, b):
    ah, am, al = split3(a)
    bh, bm, bl = split3(b)
    left = jnp.concatenate([ah, ah, ah, am, am, al], axis=0).astype(BF16)
    right = jnp.concatenate([bh, bm, bl, bh, bm, bh], axis=0).astype(BF16)
    return left, right


def dot_tn(a, b):
    return lax.dot_general(a, b, (((0,), (0,)), ((), ())), preferred_element_type=F32)


def dot_nt(a, b):
    return lax.dot_general(a, b, (((1,), (1,)), ((), ())), preferred_element_type=F32)


def recip(x):
    y = pl.reciprocal(x, approx=True)
    return y * (2.0 - x * y)


def lane_splat(x, lane):
    return jnp.take_along_axis(x, jnp.full(x.shape, lane, jnp.int32), axis=1)


def merge(rows, row8):
    out = rows[0]
    for i in range(1, len(rows)):
        out = jnp.where(row8 == i, rows[i], out)
    return out


def block_rows(ref, base):
    width = ref.shape[1]
    return [jnp.broadcast_to(ref[pl.ds(base + i, 1), :], (BLK, width)) for i in range(BLK)]


def chol_step(k, work, upper):
    width = work.shape[1]
    row8 = lax.broadcasted_iota(jnp.int32, (BLK, width), 0)
    lane8 = lax.broadcasted_iota(jnp.int32, (BLK, width), 1)
    base = pl.multiple_of(k * BLK, BLK)
    rows = block_rows(work, base)
    s = {(i, j): lane_splat(rows[i], base + j) for i in range(BLK) for j in range(i, BLK)}
    for j in range(BLK):
        inv = recip(s[j, j])
        for i in range(j + 1, BLK):
            factor = s[j, i] * inv
            for l in range(i, BLK):
                s[i, l] = s[i, l] - factor * s[j, l]
            rows[i] = rows[i] - factor * rows[j]
    pivots = merge([s[j, j] for j in range(BLK)], row8)
    block = merge(rows, row8) * lax.rsqrt(pivots)
    block = jnp.where(lane8 >= row8 + base, block, 0.0)
    upper[pl.ds(base, BLK), :] = block
    left, right = stacks(block, block)
    work[...] -= dot_tn(left, right)


def inverse_step(k, mat, mat_t):
    width = mat.shape[1]
    row8 = lax.broadcasted_iota(jnp.int32, (BLK, width), 0)
    lane8 = lax.broadcasted_iota(jnp.int32, (BLK, width), 1)
    base = pl.multiple_of(k * BLK, BLK)
    rows = block_rows(mat, base)
    cols = mat_t[pl.ds(base, BLK), :]
    s = {(i, j): lane_splat(rows[i], base + j) for i in range(BLK) for j in range(BLK)}
    for j in range(BLK):
        inv = recip(s[j, j])
        at = lane8 == base + j
        scaled = jnp.where(at, 1.0, rows[j]) * inv
        for l in range(j + 1, BLK):
            s[j, l] = s[j, l] * inv
        for i in range(BLK):
            if i == j:
                continue
            for l in range(j + 1, BLK):
                s[i, l] = s[i, l] - s[i, j] * s[j, l]
            rows[i] = jnp.where(at, 0.0, rows[i]) - s[i, j] * scaled
        rows[j] = scaled
    block = merge(rows, row8)
    inside = (lane8 >= base) & (lane8 < base + BLK)
    cols = jnp.where(inside, jnp.where(lane8 == row8 + base, -1.0, 0.0), cols)
    left, right = stacks(cols, block)
    row_id = lax.broadcasted_iota(jnp.int32, (width, width), 0)
    lane_id = lax.broadcasted_iota(jnp.int32, (width, width), 1)
    row_out = (row_id < base) | (row_id >= base + BLK)
    lane_out = (lane_id < base) | (lane_id >= base + BLK)
    keep = row_out & lane_out
    mat[...] = jnp.where(keep, mat[...], 0.0) - dot_tn(left, right)
    mat_t[...] = jnp.where(keep, mat_t[...], 0.0) - dot_tn(right, left)


def main_kernel(p_hbm, t_hbm, gat_out, upper, zt,
                gat, tv, tb, g_loc, pr, yr, gz, gf, p1w, p1s, p1f, m_loc, pm, mz, zsum, work, work_t,
                gp_send, gp_recv, loc, out_sem, st_send, st_recv, p1_send, ready):
    width, part = p_hbm.shape
    half = width // 2
    rows = t_hbm.shape[0]
    tail = tb.shape[2]
    main = part - tail
    space = lax.axis_index("space")
    y = lax.axis_index("col")
    core = space % NCORE
    z = (space // NCORE) % NZ
    x = space // (NCORE * NZ)
    pair = x * NCORE + core
    right, left, far = (y + 1) % NY, (y + NY - 1) % NY, (y + 2) % NY
    root = (space == 0) & (y == 0)

    z_order = sorted(range(1, NZ), key=lambda d: -min(d, NZ - d))
    plane_order = sorted(
        ((dx, dc, dy) for dx in range(NX) for dc in range(NCORE) for dy in range(NY)),
        key=lambda d: -(min(d[0], NX - d[0]) + d[1] + min(d[2], NY - d[2])))[:-1]
    pair_order = [(dx, dc) for dx, dc, dy in plane_order if dy == 0]

    def pair_at(dx, dc):
        return ((x + dx) % NX) * NCORE + (core + dc) % NCORE

    def to_pairs(src, dst, stage):
        for n, (dx, dc) in enumerate(pair_order):
            q = pair_at(dx, dc)
            send(src(q), dst(n), stage, at_pair(q))

    def to_z(ref, stage):
        for d in z_order:
            send(ref, ref, stage, at_z((z + d) % NZ))

    def at_z(zz):
        return (x * (NZ * NCORE) + zz * NCORE + core, y)

    def at_y(yy):
        return (space, yy)

    def at_pair(q):
        return ((q // NCORE) * (NZ * NCORE) + z * NCORE + q % NCORE, y)

    def loop(low, high, body):
        lax.fori_loop(low, high, lambda i, c: (body(i), c)[1], 0)

    def send(src, dst, stage, device):
        pltpu.make_async_remote_copy(
            src_ref=src, dst_ref=dst, send_sem=st_send.at[stage], recv_sem=st_recv.at[stage],
            device_id=device, device_id_type=MESH).start()

    def settle(ref, sem):
        pltpu.make_async_copy(ref, ref, sem).wait()

    def rows_of(i, size):
        return pl.ds(pl.multiple_of(i * size, size), size)

    barrier = pltpu.get_barrier_semaphore()

    def greet(device):
        pl.semaphore_signal(barrier, inc=1, device_id=device, device_id_type=MESH)

    own = pltpu.make_async_copy(p_hbm, gat.at[y], loc.at[0])
    own.start()
    greet(at_z((z + 1) % NZ))
    greet(at_z((z + NZ - 1) % NZ))
    for step in (1, NY - 1):
        greet(at_y((y + step) % NY))
    near = [(0, 1), (1, 0), (NX - 1, 0), (1, 1), (NX - 1, 1)]
    for dx, dc in near:
        greet(at_pair(pair_at(dx, dc)))
    pl.semaphore_wait(barrier, 4 + len(near))

    def announce(level, one, other):
        for device in (one, other):
            pl.semaphore_signal(ready.at[level], inc=1, device_id=device, device_id_type=MESH)

    def announce_z(level, step):
        announce(level, at_z((z + step) % NZ), at_z((z + NZ - step) % NZ))

    announce(3, at_pair(pair_at(1, 0)), at_pair(pair_at(NX - 1, 0)))
    announce(4, at_y(right), at_y(left))
    announce_z(0, 1)

    def gather_copy(src, dst, index, target):
        return pltpu.make_async_remote_copy(
            src_ref=src, dst_ref=dst, send_sem=gp_send.at[index], recv_sem=gp_recv.at[index],
            device_id=(space, target), device_id_type=MESH)

    def share(start, size, cols, index, target):
        lines = pl.ds(start, size)
        copy = gather_copy(p_hbm.at[lines, cols], gat.at[y, lines, cols], index, target)
        copy.start()
        return copy

    def forward(block, lines, cols, index, target):
        ref = gat.at[block, lines, cols]
        copy = gather_copy(ref, ref, index, target)
        copy.start()
        return copy

    head = 48
    first, second = pl.ds(0, half), pl.ds(half, half)
    cols_a, cols_b = pl.ds(0, main), pl.ds(main, tail)
    ra0 = share(0, head, cols_a, 6, right)
    lb0 = share(half, head, cols_a, 7, left)
    own.wait()
    high, low = split2(gat[y])
    both = dot_nt(high, jnp.concatenate([high, low], axis=0))
    cross = both[:, width:]
    g_loc[...] = both[:, :width] + cross + cross.T
    pl.semaphore_wait(ready.at[3], 2)
    to_pairs(lambda q: g_loc.at[rows_of(q, PIECE)], lambda n: pr.at[n], 0)
    pl.semaphore_wait(ready.at[0], 2)
    announce_z(1, 2)
    pl.semaphore_wait(ready.at[4], 2)

    @pl.when(root)
    def _():
        for d in range(1, NY):
            pltpu.make_async_remote_copy(
                src_ref=gat.at[0, :, pl.ds(0, width)], dst_ref=p1w, send_sem=p1_send.at[d - 1],
                recv_sem=st_recv.at[3], device_id=at_y(d), device_id_type=MESH).start()
        p1w[...] = gat[0, :, 0:width]

    settle(pr, st_recv.at[0])
    total = g_loc[rows_of(pair, PIECE), :]
    for d in range(PAIRS - 1):
        total = total + pr[d]
    yr[y] = total
    loop(1, NY, lambda d: send(yr.at[y], yr.at[y], 10, at_y((y + d) % NY)))
    ra = share(head, half - head, cols_a, 0, right)
    lb = share(half + head, half - head, cols_a, 1, left)
    rb = share(half, half, cols_a, 2, right)
    la = share(0, half, cols_a, 3, left)
    swaps = []
    for index, target in ((8, right), (9, left), (10, far)):
        cols = pl.ds(pl.multiple_of(target * part + main, LANES), tail)
        swaps.append(gather_copy(t_hbm.at[:, cols], tb.at[y], index, target))
        swaps[-1].start()
    loads = [pltpu.make_async_copy(t_hbm.at[:, pl.ds(c * part, part)], tv.at[c], loc.at[1 + c])
             for c in range(NY)]
    for load in loads:
        load.start()
    pl.semaphore_wait(ready.at[1], 2)
    announce_z(2, 4)
    settle(yr.at[pl.ds(0, NY - 1)], st_recv.at[10])
    total = yr[0]
    for q in range(1, NY):
        total = total + yr[q]
    gz[z] = total
    pl.semaphore_wait(ready.at[2], 2)
    to_z(gz.at[z], 1)

    @pl.when((space == 0) & (y > 0))
    def _():
        settle(p1w, st_recv.at[3])

    @pl.when(space == 0)
    def _():
        loop(1, PAIRS, lambda q: send(p1w.at[rows_of(q, PIECE)], p1s, 4, at_pair(q)))
        p1s[...] = p1w[0:PIECE, :]

    @pl.when((z == 0) & (pair > 0))
    def _():
        settle(p1s, st_recv.at[4])

    @pl.when(z == 0)
    def _():
        loop(1, NZ, lambda d: send(p1s, p1s, 5, at_z(d)))

    for load in loads:
        load.wait()

    def products(trail, block):
        ph, pl_ = split2(block)
        th, tl = split2(trail)
        four = dot_nt(jnp.concatenate([th, tl], axis=0), jnp.concatenate([ph, pl_], axis=0))
        n = th.shape[0]
        return (four[:n, :width] + four[n:, :width]) + (four[:n, width:] + four[n:, width:])

    outs = []

    def put_out(c, cols):
        copy = pltpu.make_async_copy(gat.at[c, :, cols], gat_out.at[c, :, cols],
                                     out_sem.at[len(outs)])
        copy.start()
        outs.append(copy)

    def add_main(c):
        m_loc[0] += products(tv[c, :, 0:main], gat[c, :, 0:main])
        put_out(c, cols_a)

    m_loc[0] = products(tv[y], gat[y])
    put_out(y, pl.ds(0, part))

    ra0.wait_recv()
    ra.wait_recv()
    fa = forward(left, first, cols_a, 4, right)
    lb0.wait_recv()
    lb.wait_recv()
    fb = forward(right, second, cols_a, 5, left)
    fill = 32
    ra_b0 = share(0, fill, cols_b, 17, right)
    lb_b0 = share(half, fill, cols_b, 18, left)

    settle(gz.at[pl.ds(0, NZ - 1)], st_recv.at[1])
    total = gz[0]
    for q in range(1, NZ):
        total = total + gz[q]
    mine = rows_of(pair, PIECE)
    gf[mine, :] = total
    to_pairs(lambda q: gf.at[mine], lambda n: gf.at[mine], 2)

    @pl.when(z > 0)
    def _():
        settle(p1s, st_recv.at[5])

    p1f[mine, :] = p1s[...]
    to_pairs(lambda q: p1f.at[mine], lambda n: p1f.at[mine], 6)

    others = pl.ds(0, (PAIRS - 1) * PIECE)
    settle(gf.at[others], st_recv.at[2])
    work[...] = gf[...]
    loop(0, width // BLK, lambda k: chol_step(k, work, upper))
    rb.wait_recv()
    add_main(left)
    la.wait_recv()
    add_main(right)
    settle(p1f.at[others], st_recv.at[6])
    work[...] = gf[...] + jnp.dot(p1f[...], upper[...], precision=HIGHEST, preferred_element_type=F32)
    work_t[...] = work[...].T
    loop(0, EARLY, lambda k: inverse_step(k, work, work_t))

    @pl.when(space == 0)
    def _():
        m_loc[0] += jnp.dot(tv[0, :, 0:width], upper[...], precision=HIGHEST,
                            preferred_element_type=F32)

    for swap in swaps:
        swap.wait_recv()
    others_t = jnp.concatenate([tb[right], tb[far], tb[left]], axis=0)
    swapped = products(others_t, gat[y, :, main:part])
    for r in range(1, NY):
        m_loc[r] = swapped[(r - 1) * rows:r * rows, :]
    fa.wait_recv()
    fb.wait_recv()
    add_main(far)

    for n, (dx, dc, dy) in enumerate(plane_order):
        q = pair_at(dx, dc)
        send(m_loc.at[dy, rows_of(q, BLK)], pm.at[n], 7, (at_pair(q)[0], (y + dy) % NY))
    ra_b = share(fill, half - fill, cols_b, 11, right)
    lb_b = share(half + fill, half - fill, cols_b, 12, left)
    rb_b = share(half, half, cols_b, 13, right)
    la_b = share(0, half, cols_b, 14, left)
    loop(EARLY, MIDDLE, lambda k: inverse_step(k, work, work_t))
    settle(pm, st_recv.at[7])
    tile = rows_of(pair, BLK)
    total = m_loc[0, tile, :]
    for d in range(PLANE - 1):
        total = total + pm[d]
    mz[z] = total
    to_z(mz.at[z], 8)
    loop(MIDDLE, width // BLK, lambda k: inverse_step(k, work, work_t))
    ra_b0.wait_recv()
    ra_b.wait_recv()
    fa_b = forward(left, first, cols_b, 15, right)
    lb_b0.wait_recv()
    lb_b.wait_recv()
    fb_b = forward(right, second, cols_b, 16, left)
    settle(mz.at[pl.ds(0, NZ - 1)], st_recv.at[8])
    total = mz[0]
    for q in range(1, NZ):
        total = total + mz[q]
    zsum[tile, :] = jnp.dot(total, work[...], precision=HIGHEST, preferred_element_type=F32)
    to_pairs(lambda q: zsum.at[tile], lambda n: zsum.at[tile], 9)
    rb_b.wait_recv()
    put_out(left, cols_b)
    la_b.wait_recv()
    put_out(right, cols_b)
    fa_b.wait_recv()
    fb_b.wait_recv()
    put_out(far, cols_b)
    settle(zsum.at[pl.ds(0, (PAIRS - 1) * BLK)], st_recv.at[9])
    zt[...] = zsum[...]

    for copy in (ra0, lb0, ra, lb, rb, la, fa, fb, *swaps, ra_b0, lb_b0, ra_b, lb_b, rb_b, la_b, fa_b, fb_b):
        copy.wait_send()
    for copy in outs:
        copy.wait()
    settle(pr, st_send.at[0])
    settle(gz.at[pl.ds(0, NZ - 1)], st_send.at[1])
    settle(gf.at[others], st_send.at[2])

    @pl.when(root)
    def _():
        for d in range(1, NY):
            settle(p1w, p1_send.at[d - 1])

    @pl.when(space == 0)
    def _():
        settle(gf.at[others], st_send.at[4])

    @pl.when(z == 0)
    def _():
        settle(gz.at[pl.ds(0, NZ - 1)], st_send.at[5])

    settle(gf.at[others], st_send.at[6])
    settle(pm, st_send.at[7])
    settle(mz.at[pl.ds(0, NZ - 1)], st_send.at[8])
    settle(zsum.at[pl.ds(0, (PAIRS - 1) * BLK)], st_send.at[9])
    settle(yr.at[pl.ds(0, NY - 1)], st_send.at[10])


def update_kernel(scale, p_ref, t_ref, zt_ref, upper_ref, up_ref, out_ref, up, new, out_sem):
    up[...] = upper_ref[...] * scale
    copies = [pltpu.make_async_copy(up, up_ref, out_sem.at[NY])]
    copies[0].start()
    zt = zt_ref[...]
    rows, width = zt.shape
    part = p_ref.shape[2]
    zh, zl = split2(zt)
    quad = jnp.concatenate([jnp.concatenate([zh, zh], axis=1),
                            jnp.concatenate([zl, zl], axis=1)], axis=0)
    for c in range(NY):
        cols = pl.ds(c * part, part)
        ph, pl_ = split2(p_ref[c])
        both = jnp.dot(quad, jnp.concatenate([ph, pl_], axis=0), preferred_element_type=F32)
        new[c] = t_ref[:, cols] - (both[:rows] + both[rows:])
        if c == 0:
            @pl.when(lax.axis_index("space") == 0)
            def _():
                new[0, :, 0:width] -= lax.dot_general(
                    zt, upper_ref[...], (((1,), (1,)), ((), ())), precision=HIGHEST,
                    preferred_element_type=F32)
        copy = pltpu.make_async_copy(new.at[c], out_ref.at[:, cols], out_sem.at[c])
        copy.start()
        copies.append(copy)
    for copy in copies:
        copy.wait()


def per_device(panel, trailing):
    width, part = panel.shape
    rows, block = trailing.shape
    tail = part // LANES * 2 // 5 * LANES
    rows_total = block * lax.axis_size("space")
    vmem = pl.BlockSpec(memory_space=pltpu.VMEM)
    hbm = pl.BlockSpec(memory_space=pltpu.HBM)
    anywhere = pl.BlockSpec(memory_space=pl.ANY)

    def buf(*shape):
        return pltpu.VMEM(shape, F32)

    gat, upper, zt = pl.pallas_call(
        main_kernel,
        out_shape=(
            jax.ShapeDtypeStruct((NY, width, part), F32),
            jax.ShapeDtypeStruct((width, width), F32),
            jax.ShapeDtypeStruct((rows, width), F32),
        ),
        in_specs=[hbm, hbm],
        out_specs=(anywhere, vmem, vmem),
        scratch_shapes=[
            buf(NY, width, part),
            buf(NY, rows, part),
            buf(NY, rows, tail),
            buf(width, width),
            buf(PAIRS - 1, PIECE, width),
            buf(NY, PIECE, width),
            buf(NZ, PIECE, width),
            buf(width, width),
            buf(width, width),
            buf(PIECE, width),
            buf(width, width),
            buf(NY, rows, width),
            buf(PLANE - 1, BLK, width),
            buf(NZ, BLK, width),
            buf(rows, width),
            buf(width, width),
            buf(width, width),
            pltpu.SemaphoreType.DMA((19,)),
            pltpu.SemaphoreType.DMA((19,)),
            pltpu.SemaphoreType.DMA((1 + NY,)),
            pltpu.SemaphoreType.DMA((2 * NY - 1,)),
            pltpu.SemaphoreType.DMA((11,)),
            pltpu.SemaphoreType.DMA((11,)),
            pltpu.SemaphoreType.DMA((NY - 1,)),
            pltpu.SemaphoreType.REGULAR((5,)),
        ],
        compiler_params=pltpu.CompilerParams(
            collective_id=0, has_side_effects=True, vmem_limit_bytes=40 * 2**20),
        name="reduce_factor",
    )(pltpu.with_memory_space_constraint(panel, pltpu.HBM),
      pltpu.with_memory_space_constraint(trailing, pltpu.HBM))

    upper_factor, updated = pl.pallas_call(
        functools.partial(update_kernel, -1.0 / math.sqrt(rows_total)),
        out_shape=(
            jax.ShapeDtypeStruct((width, width), F32),
            jax.ShapeDtypeStruct((rows, block), F32),
        ),
        in_specs=[vmem] * 4,
        out_specs=(hbm, hbm),
        scratch_shapes=[
            buf(width, width), buf(NY, rows, part), pltpu.SemaphoreType.DMA((NY + 1,))],
        compiler_params=pltpu.CompilerParams(vmem_limit_bytes=40 * 2**20),
        name="apply_update",
    )(gat, trailing, zt, upper)
    return (upper_factor, updated)


def solution(mesh):
    return jax.shard_map(
        per_device,
        mesh=mesh,
        in_specs=(P(None, ("space", "col")), P("col", "space")),
        out_specs=(P(), P("col", "space")),
        check_vma=False,
    )
```

```python
import functools
import math

import jax
import jax.numpy as jnp
from jax import lax
from jax.experimental import pallas as pl
from jax.experimental.pallas import tpu as pltpu
from jax.sharding import PartitionSpec as P

F32 = jnp.float32
BF16 = jnp.bfloat16
HIGHEST = lax.Precision.HIGHEST
MESH = pl.DeviceIdType.MESH
NX, NZ, NCORE, NY = 4, 16, 2, 4
PAIRS = NX * NCORE
BLK = 8
LANES = 128
PIECE = 16
MIDDLE = 8
PLANE = PAIRS * NY


def split2(x):
    high = x.astype(BF16)
    low = (x - high.astype(F32)).astype(BF16)
    return high, low


def split3(x):
    high = x.astype(BF16).astype(F32)
    rest = x - high
    mid = rest.astype(BF16).astype(F32)
    return high, mid, rest - mid


def stacks(a, b):
    ah, am, al = split3(a)
    bh, bm, bl = split3(b)
    left = jnp.concatenate([ah, ah, ah, am, am, al], axis=0).astype(BF16)
    right = jnp.concatenate([bh, bm, bl, bh, bm, bh], axis=0).astype(BF16)
    return left, right


def dot_tn(a, b):
    return lax.dot_general(a, b, (((0,), (0,)), ((), ())), preferred_element_type=F32)


def dot_nt(a, b):
    return lax.dot_general(a, b, (((1,), (1,)), ((), ())), preferred_element_type=F32)


def recip(x):
    y = pl.reciprocal(x, approx=True)
    return y * (2.0 - x * y)


def lane_splat(x, lane):
    return jnp.take_along_axis(x, jnp.full(x.shape, lane, jnp.int32), axis=1)


def merge(rows, row8):
    out = rows[0]
    for i in range(1, len(rows)):
        out = jnp.where(row8 == i, rows[i], out)
    return out


def block_rows(ref, base):
    width = ref.shape[1]
    return [jnp.broadcast_to(ref[pl.ds(base + i, 1), :], (BLK, width)) for i in range(BLK)]


def chol_step(k, work, upper):
    width = work.shape[1]
    row8 = lax.broadcasted_iota(jnp.int32, (BLK, width), 0)
    lane8 = lax.broadcasted_iota(jnp.int32, (BLK, width), 1)
    base = pl.multiple_of(k * BLK, BLK)
    rows = block_rows(work, base)
    s = {(i, j): lane_splat(rows[i], base + j) for i in range(BLK) for j in range(i, BLK)}
    for j in range(BLK):
        inv = recip(s[j, j])
        for i in range(j + 1, BLK):
            factor = s[j, i] * inv
            for l in range(i, BLK):
                s[i, l] = s[i, l] - factor * s[j, l]
            rows[i] = rows[i] - factor * rows[j]
    pivots = merge([s[j, j] for j in range(BLK)], row8)
    block = merge(rows, row8) * lax.rsqrt(pivots)
    block = jnp.where(lane8 >= row8 + base, block, 0.0)
    upper[pl.ds(base, BLK), :] = block
    left, right = stacks(block, block)
    work[...] -= dot_tn(left, right)


def inverse_step(k, mat, mat_t):
    width = mat.shape[1]
    row8 = lax.broadcasted_iota(jnp.int32, (BLK, width), 0)
    lane8 = lax.broadcasted_iota(jnp.int32, (BLK, width), 1)
    base = pl.multiple_of(k * BLK, BLK)
    rows = block_rows(mat, base)
    cols = mat_t[pl.ds(base, BLK), :]
    s = {(i, j): lane_splat(rows[i], base + j) for i in range(BLK) for j in range(BLK)}
    for j in range(BLK):
        inv = recip(s[j, j])
        at = lane8 == base + j
        scaled = jnp.where(at, 1.0, rows[j]) * inv
        for l in range(j + 1, BLK):
            s[j, l] = s[j, l] * inv
        for i in range(BLK):
            if i == j:
                continue
            for l in range(j + 1, BLK):
                s[i, l] = s[i, l] - s[i, j] * s[j, l]
            rows[i] = jnp.where(at, 0.0, rows[i]) - s[i, j] * scaled
        rows[j] = scaled
    block = merge(rows, row8)
    inside = (lane8 >= base) & (lane8 < base + BLK)
    cols = jnp.where(inside, jnp.where(lane8 == row8 + base, -1.0, 0.0), cols)
    left, right = stacks(cols, block)
    row_id = lax.broadcasted_iota(jnp.int32, (width, width), 0)
    lane_id = lax.broadcasted_iota(jnp.int32, (width, width), 1)
    row_out = (row_id < base) | (row_id >= base + BLK)
    lane_out = (lane_id < base) | (lane_id >= base + BLK)
    keep = row_out & lane_out
    mat[...] = jnp.where(keep, mat[...], 0.0) - dot_tn(left, right)
    mat_t[...] = jnp.where(keep, mat_t[...], 0.0) - dot_tn(right, left)


def main_kernel(p_hbm, t_hbm, gat_out, upper_out, zt,
                gat, tv, tb, g_loc, pr, yr, gz, gf, p1w, p1s, p1f, upper, m_loc, pm, mz, zsum, work, work_t,
                gp_send, gp_recv, loc, out_sem, st_send, st_recv, p1_send, ready):
    width, part = p_hbm.shape
    half = width // 2
    rows = t_hbm.shape[0]
    tail = tb.shape[2]
    main = part - tail
    space = lax.axis_index("space")
    y = lax.axis_index("col")
    core = space % NCORE
    z = (space // NCORE) % NZ
    x = space // (NCORE * NZ)
    pair = x * NCORE + core
    right, left, far = (y + 1) % NY, (y + NY - 1) % NY, (y + 2) % NY
    root = (space == 0) & (y == 0)

    z_order = sorted(range(1, NZ), key=lambda d: -min(d, NZ - d))
    plane_order = sorted(
        ((dx, dc, dy) for dx in range(NX) for dc in range(NCORE) for dy in range(NY)),
        key=lambda d: -(min(d[0], NX - d[0]) + d[1] + min(d[2], NY - d[2])))[:-1]
    pair_order = [(dx, dc) for dx, dc, dy in plane_order if dy == 0]

    def pair_at(dx, dc):
        return ((x + dx) % NX) * NCORE + (core + dc) % NCORE

    def to_pairs(src, dst, stage):
        for n, (dx, dc) in enumerate(pair_order):
            q = pair_at(dx, dc)
            send(src(q), dst(n), stage, at_pair(q))

    def to_z(ref, stage):
        for d in z_order:
            send(ref, ref, stage, at_z((z + d) % NZ))

    def at_z(zz):
        return (x * (NZ * NCORE) + zz * NCORE + core, y)

    def at_y(yy):
        return (space, yy)

    def at_pair(q):
        return ((q // NCORE) * (NZ * NCORE) + z * NCORE + q % NCORE, y)

    def loop(low, high, body):
        lax.fori_loop(low, high, lambda i, c: (body(i), c)[1], 0)

    def send(src, dst, stage, device):
        pltpu.make_async_remote_copy(
            src_ref=src, dst_ref=dst, send_sem=st_send.at[stage], recv_sem=st_recv.at[stage],
            device_id=device, device_id_type=MESH).start()

    def settle(ref, sem):
        pltpu.make_async_copy(ref, ref, sem).wait()

    def rows_of(i, size):
        return pl.ds(pl.multiple_of(i * size, size), size)

    barrier = pltpu.get_barrier_semaphore()

    def greet(device):
        pl.semaphore_signal(barrier, inc=1, device_id=device, device_id_type=MESH)

    own = pltpu.make_async_copy(p_hbm, gat.at[y], loc.at[0])
    own.start()
    greet(at_z((z + 1) % NZ))
    greet(at_z((z + NZ - 1) % NZ))
    for step in (1, NY - 1):
        greet(at_y((y + step) % NY))
    near = [(0, 1), (1, 0), (NX - 1, 0), (1, 1), (NX - 1, 1)]
    for dx, dc in near:
        greet(at_pair(pair_at(dx, dc)))
    pl.semaphore_wait(barrier, 4 + len(near))

    def announce(level, one, other):
        for device in (one, other):
            pl.semaphore_signal(ready.at[level], inc=1, device_id=device, device_id_type=MESH)

    def announce_z(level, step):
        announce(level, at_z((z + step) % NZ), at_z((z + NZ - step) % NZ))

    announce(3, at_pair(pair_at(1, 0)), at_pair(pair_at(NX - 1, 0)))
    announce(4, at_y(right), at_y(left))
    announce_z(0, 1)

    def gather_copy(src, dst, index, target):
        return pltpu.make_async_remote_copy(
            src_ref=src, dst_ref=dst, send_sem=gp_send.at[index], recv_sem=gp_recv.at[index],
            device_id=(space, target), device_id_type=MESH)

    def share(start, size, cols, index, target):
        lines = pl.ds(start, size)
        copy = gather_copy(p_hbm.at[lines, cols], gat.at[y, lines, cols], index, target)
        copy.start()
        return copy

    def forward(block, lines, cols, index, target):
        ref = gat.at[block, lines, cols]
        copy = gather_copy(ref, ref, index, target)
        copy.start()
        return copy

    first, second = pl.ds(0, half), pl.ds(half, half)
    cols_a, cols_b = pl.ds(0, main), pl.ds(main, tail)
    ra = share(0, half, cols_a, 0, right)
    lb = share(half, half, cols_a, 1, left)
    rb = share(half, half, cols_a, 2, right)
    la = share(0, half, cols_a, 3, left)
    own.wait()
    high, low = split2(gat[y])
    both = dot_nt(high, jnp.concatenate([high, low], axis=0))
    cross = both[:, width:]
    g_loc[...] = both[:, :width] + cross + cross.T
    pl.semaphore_wait(ready.at[3], 2)
    to_pairs(lambda q: g_loc.at[rows_of(q, PIECE)], lambda n: pr.at[n], 0)
    pl.semaphore_wait(ready.at[0], 2)
    announce_z(1, 2)
    pl.semaphore_wait(ready.at[4], 2)

    @pl.when(root)
    def _():
        for d in range(1, NY):
            pltpu.make_async_remote_copy(
                src_ref=gat.at[0, :, pl.ds(0, width)], dst_ref=p1w, send_sem=p1_send.at[d - 1],
                recv_sem=st_recv.at[3], device_id=at_y(d), device_id_type=MESH).start()
        p1w[...] = gat[0, :, 0:width]

    settle(pr, st_recv.at[0])
    total = g_loc[rows_of(pair, PIECE), :]
    for d in range(PAIRS - 1):
        total = total + pr[d]
    yr[y] = total
    loop(1, NY, lambda d: send(yr.at[y], yr.at[y], 10, at_y((y + d) % NY)))
    swaps = []
    for index, target in ((8, right), (9, left), (10, far)):
        cols = pl.ds(pl.multiple_of(target * part + main, LANES), tail)
        swaps.append(gather_copy(t_hbm.at[:, cols], tb.at[y], index, target))
        swaps[-1].start()
    loads = [pltpu.make_async_copy(t_hbm.at[:, pl.ds(c * part, part)], tv.at[c], loc.at[1 + c])
             for c in range(NY)]
    for load in loads:
        load.start()
    pl.semaphore_wait(ready.at[1], 2)
    announce_z(2, 4)
    settle(yr.at[pl.ds(0, NY - 1)], st_recv.at[10])
    total = yr[0]
    for q in range(1, NY):
        total = total + yr[q]
    gz[z] = total
    pl.semaphore_wait(ready.at[2], 2)
    to_z(gz.at[z], 1)

    @pl.when((space == 0) & (y > 0))
    def _():
        settle(p1w, st_recv.at[3])

    @pl.when(space == 0)
    def _():
        loop(1, PAIRS, lambda q: send(p1w.at[rows_of(q, PIECE)], p1s, 4, at_pair(q)))
        p1s[...] = p1w[0:PIECE, :]

    @pl.when((z == 0) & (pair > 0))
    def _():
        settle(p1s, st_recv.at[4])

    @pl.when(z == 0)
    def _():
        loop(1, NZ, lambda d: send(p1s, p1s, 5, at_z(d)))

    for load in loads:
        load.wait()

    def products(trail, block):
        ph, pl_ = split2(block)
        th, tl = split2(trail)
        four = dot_nt(jnp.concatenate([th, tl], axis=0), jnp.concatenate([ph, pl_], axis=0))
        n = th.shape[0]
        return (four[:n, :width] + four[n:, :width]) + (four[:n, width:] + four[n:, width:])

    outs = []

    def put_out(c, cols):
        copy = pltpu.make_async_copy(gat.at[c, :, cols], gat_out.at[c, :, cols],
                                     out_sem.at[len(outs)])
        copy.start()
        outs.append(copy)

    def add_main(c):
        m_loc[0] += products(tv[c, :, 0:main], gat[c, :, 0:main])
        put_out(c, cols_a)

    m_loc[0] = products(tv[y], gat[y])
    put_out(y, pl.ds(0, part))

    ra.wait_recv()
    fa = forward(left, first, cols_a, 4, right)
    lb.wait_recv()
    fb = forward(right, second, cols_a, 5, left)
    fill = 24
    ra_b0 = share(0, fill, cols_b, 6, right)
    lb_b0 = share(half, fill, cols_b, 7, left)

    settle(gz.at[pl.ds(0, NZ - 1)], st_recv.at[1])
    total = gz[0]
    for q in range(1, NZ):
        total = total + gz[q]
    mine = rows_of(pair, PIECE)
    gf[mine, :] = total
    to_pairs(lambda q: gf.at[mine], lambda n: gf.at[mine], 2)

    @pl.when(z > 0)
    def _():
        settle(p1s, st_recv.at[5])

    p1f[mine, :] = p1s[...]
    to_pairs(lambda q: p1f.at[mine], lambda n: p1f.at[mine], 6)

    others = pl.ds(0, (PAIRS - 1) * PIECE)
    settle(gf.at[others], st_recv.at[2])
    work[...] = gf[...]
    loop(0, width // BLK, lambda k: chol_step(k, work, upper))
    outs.append(pltpu.make_async_copy(upper, upper_out, out_sem.at[len(outs)]))
    outs[-1].start()
    rb.wait_recv()
    add_main(left)
    la.wait_recv()
    add_main(right)
    @pl.when(space == 0)
    def _():
        m_loc[0] += jnp.dot(tv[0, :, 0:width], upper[...], precision=HIGHEST,
                            preferred_element_type=F32)

    for swap in swaps:
        swap.wait_recv()
    others_t = jnp.concatenate([tb[right], tb[far], tb[left]], axis=0)
    swapped = products(others_t, gat[y, :, main:part])
    for r in range(1, NY):
        m_loc[r] = swapped[(r - 1) * rows:r * rows, :]
    fa.wait_recv()
    fb.wait_recv()
    add_main(far)

    for n, (dx, dc, dy) in enumerate(plane_order):
        q = pair_at(dx, dc)
        send(m_loc.at[dy, rows_of(q, BLK)], pm.at[n], 7, (at_pair(q)[0], (y + dy) % NY))
    ra_b = share(fill, half - fill, cols_b, 11, right)
    lb_b = share(half + fill, half - fill, cols_b, 12, left)
    rb_b = share(half, half, cols_b, 13, right)
    la_b = share(0, half, cols_b, 14, left)
    settle(p1f.at[others], st_recv.at[6])
    work[...] = gf[...] + jnp.dot(p1f[...], upper[...], precision=HIGHEST, preferred_element_type=F32)
    work_t[...] = work[...].T
    loop(0, MIDDLE, lambda k: inverse_step(k, work, work_t))
    settle(pm, st_recv.at[7])
    tile = rows_of(pair, BLK)
    total = m_loc[0, tile, :]
    for d in range(PLANE - 1):
        total = total + pm[d]
    mz[z] = total
    to_z(mz.at[z], 8)
    loop(MIDDLE, width // BLK, lambda k: inverse_step(k, work, work_t))
    ra_b0.wait_recv()
    ra_b.wait_recv()
    fa_b = forward(left, first, cols_b, 15, right)
    lb_b0.wait_recv()
    lb_b.wait_recv()
    fb_b = forward(right, second, cols_b, 16, left)
    settle(mz.at[pl.ds(0, NZ - 1)], st_recv.at[8])
    total = mz[0]
    for q in range(1, NZ):
        total = total + mz[q]
    zsum[tile, :] = jnp.dot(total, work[...], precision=HIGHEST, preferred_element_type=F32)
    to_pairs(lambda q: zsum.at[tile], lambda n: zsum.at[tile], 9)
    rb_b.wait_recv()
    put_out(left, cols_b)
    la_b.wait_recv()
    put_out(right, cols_b)
    fa_b.wait_recv()
    fb_b.wait_recv()
    put_out(far, cols_b)
    settle(zsum.at[pl.ds(0, (PAIRS - 1) * BLK)], st_recv.at[9])
    zt[...] = zsum[...]

    for copy in (ra, lb, rb, la, fa, fb, *swaps, ra_b0, lb_b0, ra_b, lb_b, rb_b, la_b, fa_b, fb_b):
        copy.wait_send()
    for copy in outs:
        copy.wait()
    settle(pr, st_send.at[0])
    settle(gz.at[pl.ds(0, NZ - 1)], st_send.at[1])
    settle(gf.at[others], st_send.at[2])

    @pl.when(root)
    def _():
        for d in range(1, NY):
            settle(p1w, p1_send.at[d - 1])

    @pl.when(space == 0)
    def _():
        settle(gf.at[others], st_send.at[4])

    @pl.when(z == 0)
    def _():
        settle(gz.at[pl.ds(0, NZ - 1)], st_send.at[5])

    settle(gf.at[others], st_send.at[6])
    settle(pm, st_send.at[7])
    settle(mz.at[pl.ds(0, NZ - 1)], st_send.at[8])
    settle(zsum.at[pl.ds(0, (PAIRS - 1) * BLK)], st_send.at[9])
    settle(yr.at[pl.ds(0, NY - 1)], st_send.at[10])


def update_kernel(scale, p_ref, t_ref, zt_ref, upper_ref, up_ref, out_ref, up, new, out_sem):
    up[...] = upper_ref[...] * scale
    copies = [pltpu.make_async_copy(up, up_ref, out_sem.at[NY])]
    copies[0].start()
    zt = zt_ref[...]
    rows, width = zt.shape
    part = p_ref.shape[2]
    zh, zl = split2(zt)
    quad = jnp.concatenate([jnp.concatenate([zh, zh], axis=1),
                            jnp.concatenate([zl, zl], axis=1)], axis=0)
    for c in range(NY):
        cols = pl.ds(c * part, part)
        ph, pl_ = split2(p_ref[c])
        both = jnp.dot(quad, jnp.concatenate([ph, pl_], axis=0), preferred_element_type=F32)
        new[c] = t_ref[:, cols] - (both[:rows] + both[rows:])
        if c == 0:
            @pl.when(lax.axis_index("space") == 0)
            def _():
                new[0, :, 0:width] -= lax.dot_general(
                    zt, upper_ref[...], (((1,), (1,)), ((), ())), precision=HIGHEST,
                    preferred_element_type=F32)
        copy = pltpu.make_async_copy(new.at[c], out_ref.at[:, cols], out_sem.at[c])
        copy.start()
        copies.append(copy)
    for copy in copies:
        copy.wait()


def per_device(panel, trailing):
    width, part = panel.shape
    rows, block = trailing.shape
    tail = part // LANES * 11 // 15 * LANES
    rows_total = block * lax.axis_size("space")
    vmem = pl.BlockSpec(memory_space=pltpu.VMEM)
    hbm = pl.BlockSpec(memory_space=pltpu.HBM)
    anywhere = pl.BlockSpec(memory_space=pl.ANY)

    def buf(*shape):
        return pltpu.VMEM(shape, F32)

    gat, upper, zt = pl.pallas_call(
        main_kernel,
        out_shape=(
            jax.ShapeDtypeStruct((NY, width, part), F32),
            jax.ShapeDtypeStruct((width, width), F32),
            jax.ShapeDtypeStruct((rows, width), F32),
        ),
        in_specs=[hbm, hbm],
        out_specs=(anywhere, anywhere, vmem),
        scratch_shapes=[
            buf(NY, width, part),
            buf(NY, rows, part),
            buf(NY, rows, tail),
            buf(width, width),
            buf(PAIRS - 1, PIECE, width),
            buf(NY, PIECE, width),
            buf(NZ, PIECE, width),
            buf(width, width),
            buf(width, width),
            buf(PIECE, width),
            buf(width, width),
            buf(width, width),
            buf(NY, rows, width),
            buf(PLANE - 1, BLK, width),
            buf(NZ, BLK, width),
            buf(rows, width),
            buf(width, width),
            buf(width, width),
            pltpu.SemaphoreType.DMA((17,)),
            pltpu.SemaphoreType.DMA((17,)),
            pltpu.SemaphoreType.DMA((1 + NY,)),
            pltpu.SemaphoreType.DMA((2 * NY,)),
            pltpu.SemaphoreType.DMA((11,)),
            pltpu.SemaphoreType.DMA((11,)),
            pltpu.SemaphoreType.DMA((NY - 1,)),
            pltpu.SemaphoreType.REGULAR((5,)),
        ],
        compiler_params=pltpu.CompilerParams(
            collective_id=0, has_side_effects=True, vmem_limit_bytes=40 * 2**20),
        name="reduce_factor",
    )(pltpu.with_memory_space_constraint(panel, pltpu.HBM),
      pltpu.with_memory_space_constraint(trailing, pltpu.HBM))

    upper_factor, updated = pl.pallas_call(
        functools.partial(update_kernel, -1.0 / math.sqrt(rows_total)),
        out_shape=(
            jax.ShapeDtypeStruct((width, width), F32),
            jax.ShapeDtypeStruct((rows, block), F32),
        ),
        in_specs=[vmem] * 4,
        out_specs=(hbm, hbm),
        scratch_shapes=[
            buf(width, width), buf(NY, rows, part), pltpu.SemaphoreType.DMA((NY + 1,))],
        compiler_params=pltpu.CompilerParams(vmem_limit_bytes=40 * 2**20),
        name="apply_update",
    )(gat, trailing, zt, upper)
    return (upper_factor, updated)


def solution(mesh):
    return jax.shard_map(
        per_device,
        mesh=mesh,
        in_specs=(P(None, ("space", "col")), P("col", "space")),
        out_specs=(P(), P("col", "space")),
        check_vma=False,
    )
```

```python
import functools
import math

import jax
import jax.numpy as jnp
from jax import lax
from jax.experimental import pallas as pl
from jax.experimental.pallas import tpu as pltpu
from jax.sharding import PartitionSpec as P

F32 = jnp.float32
BF16 = jnp.bfloat16
HIGHEST = lax.Precision.HIGHEST
MESH = pl.DeviceIdType.MESH
NX, NZ, NCORE, NY = 4, 16, 2, 4
PAIRS = NX * NCORE
BLK = 8
LANES = 128
PIECE = 16
MIDDLE = 8
EARLY_PLANES = 7
PLANE = PAIRS * NY


def split2(x):
    high = x.astype(BF16)
    low = (x - high.astype(F32)).astype(BF16)
    return high, low


def split3(x):
    high = x.astype(BF16).astype(F32)
    rest = x - high
    mid = rest.astype(BF16).astype(F32)
    return high, mid, rest - mid


def stacks(a, b):
    ah, am, al = split3(a)
    bh, bm, bl = split3(b)
    left = jnp.concatenate([ah, ah, ah, am, am, al], axis=0).astype(BF16)
    right = jnp.concatenate([bh, bm, bl, bh, bm, bh], axis=0).astype(BF16)
    return left, right


def dot_tn(a, b):
    return lax.dot_general(a, b, (((0,), (0,)), ((), ())), preferred_element_type=F32)


def dot_nt(a, b):
    return lax.dot_general(a, b, (((1,), (1,)), ((), ())), preferred_element_type=F32)


def recip(x):
    y = pl.reciprocal(x, approx=True)
    return y * (2.0 - x * y)


def lane_splat(x, lane):
    return jnp.take_along_axis(x, jnp.full(x.shape, lane, jnp.int32), axis=1)


def merge(rows, row8):
    out = rows[0]
    for i in range(1, len(rows)):
        out = jnp.where(row8 == i, rows[i], out)
    return out


def block_rows(ref, base):
    width = ref.shape[1]
    return [jnp.broadcast_to(ref[pl.ds(base + i, 1), :], (BLK, width)) for i in range(BLK)]


def chol_step(k, work, upper):
    width = work.shape[1]
    row8 = lax.broadcasted_iota(jnp.int32, (BLK, width), 0)
    lane8 = lax.broadcasted_iota(jnp.int32, (BLK, width), 1)
    base = pl.multiple_of(k * BLK, BLK)
    rows = block_rows(work, base)
    s = {(i, j): lane_splat(rows[i], base + j) for i in range(BLK) for j in range(i, BLK)}
    for j in range(BLK):
        inv = recip(s[j, j])
        for i in range(j + 1, BLK):
            factor = s[j, i] * inv
            for l in range(i, BLK):
                s[i, l] = s[i, l] - factor * s[j, l]
            rows[i] = rows[i] - factor * rows[j]
    pivots = merge([s[j, j] for j in range(BLK)], row8)
    block = merge(rows, row8) * lax.rsqrt(pivots)
    block = jnp.where(lane8 >= row8 + base, block, 0.0)
    upper[pl.ds(base, BLK), :] = block
    left, right = stacks(block, block)
    work[...] -= dot_tn(left, right)


def inverse_step(k, mat, mat_t):
    width = mat.shape[1]
    row8 = lax.broadcasted_iota(jnp.int32, (BLK, width), 0)
    lane8 = lax.broadcasted_iota(jnp.int32, (BLK, width), 1)
    base = pl.multiple_of(k * BLK, BLK)
    rows = block_rows(mat, base)
    cols = mat_t[pl.ds(base, BLK), :]
    s = {(i, j): lane_splat(rows[i], base + j) for i in range(BLK) for j in range(BLK)}
    for j in range(BLK):
        inv = recip(s[j, j])
        at = lane8 == base + j
        scaled = jnp.where(at, 1.0, rows[j]) * inv
        for l in range(j + 1, BLK):
            s[j, l] = s[j, l] * inv
        for i in range(BLK):
            if i == j:
                continue
            for l in range(j + 1, BLK):
                s[i, l] = s[i, l] - s[i, j] * s[j, l]
            rows[i] = jnp.where(at, 0.0, rows[i]) - s[i, j] * scaled
        rows[j] = scaled
    block = merge(rows, row8)
    inside = (lane8 >= base) & (lane8 < base + BLK)
    cols = jnp.where(inside, jnp.where(lane8 == row8 + base, -1.0, 0.0), cols)
    left, right = stacks(cols, block)
    row_id = lax.broadcasted_iota(jnp.int32, (width, width), 0)
    lane_id = lax.broadcasted_iota(jnp.int32, (width, width), 1)
    row_out = (row_id < base) | (row_id >= base + BLK)
    lane_out = (lane_id < base) | (lane_id >= base + BLK)
    keep = row_out & lane_out
    mat[...] = jnp.where(keep, mat[...], 0.0) - dot_tn(left, right)
    mat_t[...] = jnp.where(keep, mat_t[...], 0.0) - dot_tn(right, left)


def main_kernel(p_hbm, t_hbm, gat_out, upper_out, zt,
                gat, tv, tb, g_loc, pr, yr, gz, gf, p1w, p1s, p1f, t1, upper, m_loc, pm, mz, zsum, work, work_t,
                gp_send, gp_recv, loc, out_sem, st_send, st_recv, p1_send, ready):
    width, part = p_hbm.shape
    half = width // 2
    rows = t_hbm.shape[0]
    tail = tb.shape[2]
    main = part - tail
    space = lax.axis_index("space")
    y = lax.axis_index("col")
    core = space % NCORE
    z = (space // NCORE) % NZ
    x = space // (NCORE * NZ)
    pair = x * NCORE + core
    right, left, far = (y + 1) % NY, (y + NY - 1) % NY, (y + 2) % NY
    root = (space == 0) & (y == 0)

    z_order = sorted(range(1, NZ), key=lambda d: -min(d, NZ - d))
    plane_order = sorted(
        ((dx, dc, dy) for dx in range(NX) for dc in range(NCORE) for dy in range(NY)),
        key=lambda d: -(min(d[0], NX - d[0]) + d[1] + min(d[2], NY - d[2])))[:-1]
    pair_order = [(dx, dc) for dx, dc, dy in plane_order if dy == 0]

    def pair_at(dx, dc):
        return ((x + dx) % NX) * NCORE + (core + dc) % NCORE

    def to_pairs(src, dst, stage):
        for n, (dx, dc) in enumerate(pair_order):
            q = pair_at(dx, dc)
            send(src(q), dst(n), stage, at_pair(q))

    def to_z(ref, stage):
        for d in z_order:
            send(ref, ref, stage, at_z((z + d) % NZ))

    def at_z(zz):
        return (x * (NZ * NCORE) + zz * NCORE + core, y)

    def at_y(yy):
        return (space, yy)

    def at_pair(q):
        return ((q // NCORE) * (NZ * NCORE) + z * NCORE + q % NCORE, y)

    def loop(low, high, body):
        lax.fori_loop(low, high, lambda i, c: (body(i), c)[1], 0)

    def send(src, dst, stage, device):
        pltpu.make_async_remote_copy(
            src_ref=src, dst_ref=dst, send_sem=st_send.at[stage], recv_sem=st_recv.at[stage],
            device_id=device, device_id_type=MESH).start()

    def settle(ref, sem):
        pltpu.make_async_copy(ref, ref, sem).wait()

    def rows_of(i, size):
        return pl.ds(pl.multiple_of(i * size, size), size)

    barrier = pltpu.get_barrier_semaphore()

    def greet(device):
        pl.semaphore_signal(barrier, inc=1, device_id=device, device_id_type=MESH)

    own = pltpu.make_async_copy(p_hbm, gat.at[y], loc.at[0])
    own.start()
    greet(at_z((z + 1) % NZ))
    greet(at_z((z + NZ - 1) % NZ))
    for step in (1, NY - 1):
        greet(at_y((y + step) % NY))
    near = [(0, 1), (1, 0), (NX - 1, 0), (1, 1), (NX - 1, 1)]
    for dx, dc in near:
        greet(at_pair(pair_at(dx, dc)))
    pl.semaphore_wait(barrier, 4 + len(near))

    def announce(level, one, other):
        for device in (one, other):
            pl.semaphore_signal(ready.at[level], inc=1, device_id=device, device_id_type=MESH)

    def announce_z(level, step):
        announce(level, at_z((z + step) % NZ), at_z((z + NZ - step) % NZ))

    announce(3, at_pair(pair_at(1, 0)), at_pair(pair_at(NX - 1, 0)))
    announce(4, at_y(right), at_y(left))
    announce_z(0, 1)

    def gather_copy(src, dst, index, target):
        return pltpu.make_async_remote_copy(
            src_ref=src, dst_ref=dst, send_sem=gp_send.at[index], recv_sem=gp_recv.at[index],
            device_id=(space, target), device_id_type=MESH)

    def share(start, size, cols, index, target):
        lines = pl.ds(start, size)
        copy = gather_copy(p_hbm.at[lines, cols], gat.at[y, lines, cols], index, target)
        copy.start()
        return copy

    def forward(block, lines, cols, index, target):
        ref = gat.at[block, lines, cols]
        copy = gather_copy(ref, ref, index, target)
        copy.start()
        return copy

    top, bottom = pl.ds(0, half), pl.ds(half, half)
    cols_a, cols_b = pl.ds(0, main), pl.ds(main, tail)
    ra = share(0, half, cols_a, 0, right)
    lb = share(half, half, cols_a, 1, left)
    rb = share(half, half, cols_a, 2, right)
    la = share(0, half, cols_a, 3, left)
    own.wait()
    high, low = split2(gat[y])
    both = dot_nt(high, jnp.concatenate([high, low], axis=0))
    cross = both[:, width:]
    g_loc[...] = both[:, :width] + cross + cross.T
    pl.semaphore_wait(ready.at[3], 2)
    to_pairs(lambda q: g_loc.at[rows_of(q, PIECE)], lambda n: pr.at[n], 0)
    pl.semaphore_wait(ready.at[0], 2)
    announce_z(1, 2)
    pl.semaphore_wait(ready.at[4], 2)

    @pl.when(root)
    def _():
        for d in range(1, NY):
            pltpu.make_async_remote_copy(
                src_ref=gat.at[0, :, pl.ds(0, width)], dst_ref=p1w, send_sem=p1_send.at[d - 1],
                recv_sem=st_recv.at[3], device_id=at_y(d), device_id_type=MESH).start()
        p1w[...] = gat[0, :, 0:width]

    settle(pr, st_recv.at[0])
    total = g_loc[rows_of(pair, PIECE), :]
    for d in range(PAIRS - 1):
        total = total + pr[d]
    yr[y] = total
    loop(1, NY, lambda d: send(yr.at[y], yr.at[y], 10, at_y((y + d) % NY)))
    swaps = []
    for index, target in ((8, right), (9, left), (10, far)):
        cols = pl.ds(pl.multiple_of(target * part + main, LANES), tail)
        swaps.append(gather_copy(t_hbm.at[:, cols], tb.at[y], index, target))
        swaps[-1].start()
    loads = [pltpu.make_async_copy(t_hbm.at[:, pl.ds(c * part, part)], tv.at[c], loc.at[1 + c])
             for c in range(NY)]
    for load in loads:
        load.start()
    pl.semaphore_wait(ready.at[1], 2)
    announce_z(2, 4)
    settle(yr.at[pl.ds(0, NY - 1)], st_recv.at[10])
    total = yr[0]
    for q in range(1, NY):
        total = total + yr[q]
    gz[z] = total
    pl.semaphore_wait(ready.at[2], 2)
    to_z(gz.at[z], 1)

    @pl.when((space == 0) & (y > 0))
    def _():
        settle(p1w, st_recv.at[3])

    @pl.when(space == 0)
    def _():
        loop(1, PAIRS, lambda q: send(p1w.at[rows_of(q, PIECE)], p1s, 4, at_pair(q)))
        p1s[...] = p1w[0:PIECE, :]

    @pl.when((z == 0) & (pair > 0))
    def _():
        settle(p1s, st_recv.at[4])

    @pl.when(z == 0)
    def _():
        loop(1, NZ, lambda d: send(p1s, p1s, 5, at_z(d)))

    for load in loads:
        load.wait()

    @pl.when(space == 0)
    def _():
        to_pairs(lambda q: tv.at[0, rows_of(q, BLK), pl.ds(0, width)], lambda n: t1, 11)
        t1[...] = tv[0, 0:BLK, 0:width]

    def products(trail, block):
        ph, pl_ = split2(block)
        th, tl = split2(trail)
        four = dot_nt(jnp.concatenate([th, tl], axis=0), jnp.concatenate([ph, pl_], axis=0))
        n = th.shape[0]
        return (four[:n, :width] + four[n:, :width]) + (four[:n, width:] + four[n:, width:])

    outs = []

    def put_out(c, cols):
        copy = pltpu.make_async_copy(gat.at[c, :, cols], gat_out.at[c, :, cols],
                                     out_sem.at[len(outs)])
        copy.start()
        outs.append(copy)

    def add_main(c):
        m_loc[0] += products(tv[c, :, 0:main], gat[c, :, 0:main])

    m_loc[0] = products(tv[y], gat[y])
    put_out(y, pl.ds(0, part))

    ra.wait_recv()
    fa = forward(left, top, cols_a, 4, right)
    lb.wait_recv()
    fb = forward(right, bottom, cols_a, 5, left)
    fill = 24
    ra_b0 = share(0, fill, cols_b, 6, right)
    lb_b0 = share(half, fill, cols_b, 7, left)

    def second(start, size, index, target):
        lines = pl.ds(start, size)
        return gather_copy(p_hbm.at[lines, cols_b], gat.at[y, lines, cols_b], index, target)

    def relay(block, lines, index, target):
        ref = gat.at[block, lines, cols_b]
        return gather_copy(ref, ref, index, target)

    ra_b = second(fill, half - fill, 11, right)
    lb_b = second(half + fill, half - fill, 12, left)
    rb_b = second(half, half, 13, right)
    la_b = second(0, half, 14, left)
    fa_b = relay(left, top, 15, right)
    fb_b = relay(right, bottom, 16, left)

    def finish_first():
        rb.wait_recv()
        add_main(left)
        la.wait_recv()
        add_main(right)
        for swap in swaps:
            swap.wait_recv()
        others_t = jnp.concatenate([tb[right], tb[far], tb[left]], axis=0)
        swapped = products(others_t, gat[y, :, main:part])
        for r in range(1, NY):
            m_loc[r] = swapped[(r - 1) * rows:r * rows, :]
        fa.wait_recv()
        fb.wait_recv()
        add_main(far)
        for n, (dx, dc, dy) in enumerate(plane_order):
            q = pair_at(dx, dc)
            send(m_loc.at[dy, rows_of(q, BLK)], pm.at[n], 7, (at_pair(q)[0], (y + dy) % NY))
        for copy in (ra_b, lb_b, rb_b, la_b):
            copy.start()

    def forward_second():
        ra_b0.wait_recv()
        ra_b.wait_recv()
        fa_b.start()
        lb_b0.wait_recv()
        lb_b.wait_recv()
        fb_b.start()

    early = z < EARLY_PLANES

    @pl.when(early)
    def _():
        finish_first()


    settle(gz.at[pl.ds(0, NZ - 1)], st_recv.at[1])
    total = gz[0]
    for q in range(1, NZ):
        total = total + gz[q]
    mine = rows_of(pair, PIECE)
    gf[mine, :] = total
    to_pairs(lambda q: gf.at[mine], lambda n: gf.at[mine], 2)

    @pl.when(z > 0)
    def _():
        settle(p1s, st_recv.at[5])

    p1f[mine, :] = p1s[...]
    to_pairs(lambda q: p1f.at[mine], lambda n: p1f.at[mine], 6)

    others = pl.ds(0, (PAIRS - 1) * PIECE)
    settle(gf.at[others], st_recv.at[2])
    work[...] = gf[...]
    loop(0, width // BLK, lambda k: chol_step(k, work, upper))
    outs.append(pltpu.make_async_copy(upper, upper_out, out_sem.at[len(outs)]))
    outs[-1].start()

    @pl.when(early)
    def _():
        forward_second()

    @pl.when(jnp.logical_not(early))
    def _():
        finish_first()

    for block in (left, right, far):
        put_out(block, cols_a)
    settle(p1f.at[others], st_recv.at[6])
    work[...] = gf[...] + jnp.dot(p1f[...], upper[...], precision=HIGHEST, preferred_element_type=F32)
    work_t[...] = work[...].T
    loop(0, MIDDLE, lambda k: inverse_step(k, work, work_t))
    settle(pm, st_recv.at[7])
    tile = rows_of(pair, BLK)
    total = m_loc[0, tile, :]
    for d in range(PLANE - 1):
        total = total + pm[d]
    mz[z] = total

    @pl.when((z == 0) & (pair > 0))
    def _():
        settle(t1, st_recv.at[11])

    @pl.when(z == 0)
    def _():
        mz[0] += jnp.dot(t1[...], upper[...], precision=HIGHEST, preferred_element_type=F32)

    to_z(mz.at[z], 8)
    loop(MIDDLE, width // BLK, lambda k: inverse_step(k, work, work_t))

    @pl.when(jnp.logical_not(early))
    def _():
        forward_second()

    settle(mz.at[pl.ds(0, NZ - 1)], st_recv.at[8])
    total = mz[0]
    for q in range(1, NZ):
        total = total + mz[q]
    zsum[tile, :] = jnp.dot(total, work[...], precision=HIGHEST, preferred_element_type=F32)
    to_pairs(lambda q: zsum.at[tile], lambda n: zsum.at[tile], 9)
    rb_b.wait_recv()
    put_out(left, cols_b)
    la_b.wait_recv()
    put_out(right, cols_b)
    fa_b.wait_recv()
    fb_b.wait_recv()
    put_out(far, cols_b)
    settle(zsum.at[pl.ds(0, (PAIRS - 1) * BLK)], st_recv.at[9])
    zt[...] = zsum[...]

    for copy in (ra, lb, rb, la, fa, fb, *swaps, ra_b0, lb_b0, ra_b, lb_b, rb_b, la_b, fa_b, fb_b):
        copy.wait_send()
    for copy in outs:
        copy.wait()
    settle(pr, st_send.at[0])

    @pl.when(space == 0)
    def _():
        settle(pm.at[pl.ds(0, PAIRS - 1)], st_send.at[11])

    settle(gz.at[pl.ds(0, NZ - 1)], st_send.at[1])
    settle(gf.at[others], st_send.at[2])

    @pl.when(root)
    def _():
        for d in range(1, NY):
            settle(p1w, p1_send.at[d - 1])

    @pl.when(space == 0)
    def _():
        settle(gf.at[others], st_send.at[4])

    @pl.when(z == 0)
    def _():
        settle(gz.at[pl.ds(0, NZ - 1)], st_send.at[5])

    settle(gf.at[others], st_send.at[6])
    settle(pm, st_send.at[7])
    settle(mz.at[pl.ds(0, NZ - 1)], st_send.at[8])
    settle(zsum.at[pl.ds(0, (PAIRS - 1) * BLK)], st_send.at[9])
    settle(yr.at[pl.ds(0, NY - 1)], st_send.at[10])


def update_kernel(scale, p_ref, t_ref, zt_ref, upper_ref, up_ref, out_ref, up, new, out_sem):
    up[...] = upper_ref[...] * scale
    copies = [pltpu.make_async_copy(up, up_ref, out_sem.at[NY])]
    copies[0].start()
    zt = zt_ref[...]
    rows, width = zt.shape
    part = p_ref.shape[2]
    zh, zl = split2(zt)
    quad = jnp.concatenate([jnp.concatenate([zh, zh], axis=1),
                            jnp.concatenate([zl, zl], axis=1)], axis=0)
    for c in range(NY):
        cols = pl.ds(c * part, part)
        ph, pl_ = split2(p_ref[c])
        both = jnp.dot(quad, jnp.concatenate([ph, pl_], axis=0), preferred_element_type=F32)
        new[c] = t_ref[:, cols] - (both[:rows] + both[rows:])
        if c == 0:
            @pl.when(lax.axis_index("space") == 0)
            def _():
                new[0, :, 0:width] -= lax.dot_general(
                    zt, upper_ref[...], (((1,), (1,)), ((), ())), precision=HIGHEST,
                    preferred_element_type=F32)
        copy = pltpu.make_async_copy(new.at[c], out_ref.at[:, cols], out_sem.at[c])
        copy.start()
        copies.append(copy)
    for copy in copies:
        copy.wait()


def per_device(panel, trailing):
    width, part = panel.shape
    rows, block = trailing.shape
    tail = part // LANES * 11 // 15 * LANES
    rows_total = block * lax.axis_size("space")
    vmem = pl.BlockSpec(memory_space=pltpu.VMEM)
    hbm = pl.BlockSpec(memory_space=pltpu.HBM)
    anywhere = pl.BlockSpec(memory_space=pl.ANY)

    def buf(*shape):
        return pltpu.VMEM(shape, F32)

    gat, upper, zt = pl.pallas_call(
        main_kernel,
        out_shape=(
            jax.ShapeDtypeStruct((NY, width, part), F32),
            jax.ShapeDtypeStruct((width, width), F32),
            jax.ShapeDtypeStruct((rows, width), F32),
        ),
        in_specs=[hbm, hbm],
        out_specs=(anywhere, anywhere, vmem),
        scratch_shapes=[
            buf(NY, width, part),
            buf(NY, rows, part),
            buf(NY, rows, tail),
            buf(width, width),
            buf(PAIRS - 1, PIECE, width),
            buf(NY, PIECE, width),
            buf(NZ, PIECE, width),
            buf(width, width),
            buf(width, width),
            buf(PIECE, width),
            buf(width, width),
            buf(BLK, width),
            buf(width, width),
            buf(NY, rows, width),
            buf(PLANE - 1, BLK, width),
            buf(NZ, BLK, width),
            buf(rows, width),
            buf(width, width),
            buf(width, width),
            pltpu.SemaphoreType.DMA((17,)),
            pltpu.SemaphoreType.DMA((17,)),
            pltpu.SemaphoreType.DMA((1 + NY,)),
            pltpu.SemaphoreType.DMA((2 * NY,)),
            pltpu.SemaphoreType.DMA((12,)),
            pltpu.SemaphoreType.DMA((12,)),
            pltpu.SemaphoreType.DMA((NY - 1,)),
            pltpu.SemaphoreType.REGULAR((5,)),
        ],
        compiler_params=pltpu.CompilerParams(
            collective_id=0, has_side_effects=True, vmem_limit_bytes=40 * 2**20),
        name="reduce_factor",
    )(pltpu.with_memory_space_constraint(panel, pltpu.HBM),
      pltpu.with_memory_space_constraint(trailing, pltpu.HBM))

    upper_factor, updated = pl.pallas_call(
        functools.partial(update_kernel, -1.0 / math.sqrt(rows_total)),
        out_shape=(
            jax.ShapeDtypeStruct((width, width), F32),
            jax.ShapeDtypeStruct((rows, block), F32),
        ),
        in_specs=[vmem] * 4,
        out_specs=(hbm, hbm),
        scratch_shapes=[
            buf(width, width), buf(NY, rows, part), pltpu.SemaphoreType.DMA((NY + 1,))],
        compiler_params=pltpu.CompilerParams(vmem_limit_bytes=40 * 2**20),
        name="apply_update",
    )(gat, trailing, zt, upper)
    return (upper_factor, updated)


def solution(mesh):
    return jax.shard_map(
        per_device,
        mesh=mesh,
        in_specs=(P(None, ("space", "col")), P("col", "space")),
        out_specs=(P(), P("col", "space")),
        check_vma=False,
    )
```

```python
import functools
import math

import jax
import jax.numpy as jnp
from jax import lax
from jax.experimental import pallas as pl
from jax.experimental.pallas import tpu as pltpu
from jax.sharding import PartitionSpec as P

F32 = jnp.float32
BF16 = jnp.bfloat16
HIGHEST = lax.Precision.HIGHEST
MESH = pl.DeviceIdType.MESH
NX, NZ, NCORE, NY = 4, 16, 2, 4
PAIRS = NX * NCORE
BLK = 8
LANES = 128
PIECE = 16
MIDDLE = 8
EARLY_PLANES = 3
PLANE = PAIRS * NY


def split2(x):
    high = x.astype(BF16)
    low = (x - high.astype(F32)).astype(BF16)
    return high, low


def split3(x):
    high = x.astype(BF16).astype(F32)
    rest = x - high
    mid = rest.astype(BF16).astype(F32)
    return high, mid, rest - mid


def stacks(a, b):
    ah, am, al = split3(a)
    bh, bm, bl = split3(b)
    left = jnp.concatenate([ah, ah, ah, am, am, al], axis=0).astype(BF16)
    right = jnp.concatenate([bh, bm, bl, bh, bm, bh], axis=0).astype(BF16)
    return left, right


def dot_tn(a, b):
    return lax.dot_general(a, b, (((0,), (0,)), ((), ())), preferred_element_type=F32)


def dot_nt(a, b):
    return lax.dot_general(a, b, (((1,), (1,)), ((), ())), preferred_element_type=F32)


def recip(x):
    y = pl.reciprocal(x, approx=True)
    return y * (2.0 - x * y)


def lane_splat(x, lane):
    return jnp.take_along_axis(x, jnp.full(x.shape, lane, jnp.int32), axis=1)


def merge(rows, row8):
    out = rows[0]
    for i in range(1, len(rows)):
        out = jnp.where(row8 == i, rows[i], out)
    return out


def block_rows(ref, base):
    width = ref.shape[1]
    return [jnp.broadcast_to(ref[pl.ds(base + i, 1), :], (BLK, width)) for i in range(BLK)]


def chol_step(k, work, upper):
    width = work.shape[1]
    row8 = lax.broadcasted_iota(jnp.int32, (BLK, width), 0)
    lane8 = lax.broadcasted_iota(jnp.int32, (BLK, width), 1)
    base = pl.multiple_of(k * BLK, BLK)
    rows = block_rows(work, base)
    s = {(i, j): lane_splat(rows[i], base + j) for i in range(BLK) for j in range(i, BLK)}
    for j in range(BLK):
        inv = recip(s[j, j])
        for i in range(j + 1, BLK):
            factor = s[j, i] * inv
            for l in range(i, BLK):
                s[i, l] = s[i, l] - factor * s[j, l]
            rows[i] = rows[i] - factor * rows[j]
    pivots = merge([s[j, j] for j in range(BLK)], row8)
    block = merge(rows, row8) * lax.rsqrt(pivots)
    block = jnp.where(lane8 >= row8 + base, block, 0.0)
    upper[pl.ds(base, BLK), :] = block
    left, right = stacks(block, block)
    work[...] -= dot_tn(left, right)


def inverse_step(k, mat, mat_t):
    width = mat.shape[1]
    row8 = lax.broadcasted_iota(jnp.int32, (BLK, width), 0)
    lane8 = lax.broadcasted_iota(jnp.int32, (BLK, width), 1)
    base = pl.multiple_of(k * BLK, BLK)
    rows = block_rows(mat, base)
    cols = mat_t[pl.ds(base, BLK), :]
    s = {(i, j): lane_splat(rows[i], base + j) for i in range(BLK) for j in range(BLK)}
    for j in range(BLK):
        inv = recip(s[j, j])
        at = lane8 == base + j
        scaled = jnp.where(at, 1.0, rows[j]) * inv
        for l in range(j + 1, BLK):
            s[j, l] = s[j, l] * inv
        for i in range(BLK):
            if i == j:
                continue
            for l in range(j + 1, BLK):
                s[i, l] = s[i, l] - s[i, j] * s[j, l]
            rows[i] = jnp.where(at, 0.0, rows[i]) - s[i, j] * scaled
        rows[j] = scaled
    block = merge(rows, row8)
    inside = (lane8 >= base) & (lane8 < base + BLK)
    cols = jnp.where(inside, jnp.where(lane8 == row8 + base, -1.0, 0.0), cols)
    left, right = stacks(cols, block)
    row_id = lax.broadcasted_iota(jnp.int32, (width, width), 0)
    lane_id = lax.broadcasted_iota(jnp.int32, (width, width), 1)
    row_out = (row_id < base) | (row_id >= base + BLK)
    lane_out = (lane_id < base) | (lane_id >= base + BLK)
    keep = row_out & lane_out
    mat[...] = jnp.where(keep, mat[...], 0.0) - dot_tn(left, right)
    mat_t[...] = jnp.where(keep, mat_t[...], 0.0) - dot_tn(right, left)


def main_kernel(p_hbm, t_hbm, gat_out, upper_out, zt,
                gat, tv, tb, g_loc, pr, yr, gz, gf, p1w, p1s, p1f, t1, upper, m_loc, pm, mz, zsum, work, work_t,
                gp_send, gp_recv, loc, out_sem, st_send, st_recv, p1_send, ready):
    width, part = p_hbm.shape
    half = width // 2
    rows = t_hbm.shape[0]
    tail = tb.shape[2]
    main = part - tail
    space = lax.axis_index("space")
    y = lax.axis_index("col")
    core = space % NCORE
    z = (space // NCORE) % NZ
    x = space // (NCORE * NZ)
    pair = x * NCORE + core
    right, left, far = (y + 1) % NY, (y + NY - 1) % NY, (y + 2) % NY
    root = (space == 0) & (y == 0)

    z_order = sorted(range(1, NZ), key=lambda d: -min(d, NZ - d))
    plane_order = sorted(
        ((dx, dc, dy) for dx in range(NX) for dc in range(NCORE) for dy in range(NY)),
        key=lambda d: -(min(d[0], NX - d[0]) + d[1] + min(d[2], NY - d[2])))[:-1]
    pair_order = [(dx, dc) for dx, dc, dy in plane_order if dy == 0]

    def pair_at(dx, dc):
        return ((x + dx) % NX) * NCORE + (core + dc) % NCORE

    def to_pairs(src, dst, stage):
        for n, (dx, dc) in enumerate(pair_order):
            q = pair_at(dx, dc)
            send(src(q), dst(n), stage, at_pair(q))

    def to_z(ref, stage):
        for d in z_order:
            send(ref, ref, stage, at_z((z + d) % NZ))

    def at_z(zz):
        return (x * (NZ * NCORE) + zz * NCORE + core, y)

    def at_y(yy):
        return (space, yy)

    def at_pair(q):
        return ((q // NCORE) * (NZ * NCORE) + z * NCORE + q % NCORE, y)

    def loop(low, high, body):
        lax.fori_loop(low, high, lambda i, c: (body(i), c)[1], 0)

    def send(src, dst, stage, device):
        pltpu.make_async_remote_copy(
            src_ref=src, dst_ref=dst, send_sem=st_send.at[stage], recv_sem=st_recv.at[stage],
            device_id=device, device_id_type=MESH).start()

    def settle(ref, sem):
        pltpu.make_async_copy(ref, ref, sem).wait()

    def rows_of(i, size):
        return pl.ds(pl.multiple_of(i * size, size), size)

    barrier = pltpu.get_barrier_semaphore()

    def greet(device):
        pl.semaphore_signal(barrier, inc=1, device_id=device, device_id_type=MESH)

    own = pltpu.make_async_copy(p_hbm, gat.at[y], loc.at[0])
    own.start()
    greet(at_z((z + 1) % NZ))
    greet(at_z((z + NZ - 1) % NZ))
    for step in (1, NY - 1):
        greet(at_y((y + step) % NY))
    near = [(0, 1), (1, 0), (NX - 1, 0), (1, 1), (NX - 1, 1)]
    for dx, dc in near:
        greet(at_pair(pair_at(dx, dc)))
    pl.semaphore_wait(barrier, 4 + len(near))

    def announce(level, one, other):
        for device in (one, other):
            pl.semaphore_signal(ready.at[level], inc=1, device_id=device, device_id_type=MESH)

    def announce_z(level, step):
        announce(level, at_z((z + step) % NZ), at_z((z + NZ - step) % NZ))

    announce(3, at_pair(pair_at(1, 0)), at_pair(pair_at(NX - 1, 0)))
    announce(4, at_y(right), at_y(left))
    announce_z(0, 1)

    def gather_copy(src, dst, index, target):
        return pltpu.make_async_remote_copy(
            src_ref=src, dst_ref=dst, send_sem=gp_send.at[index], recv_sem=gp_recv.at[index],
            device_id=(space, target), device_id_type=MESH)

    def share(start, size, cols, index, target):
        lines = pl.ds(start, size)
        copy = gather_copy(p_hbm.at[lines, cols], gat.at[y, lines, cols], index, target)
        copy.start()
        return copy

    def forward(block, lines, cols, index, target):
        ref = gat.at[block, lines, cols]
        copy = gather_copy(ref, ref, index, target)
        copy.start()
        return copy

    top, bottom = pl.ds(0, half), pl.ds(half, half)
    cols_a, cols_b = pl.ds(0, main), pl.ds(main, tail)
    ra = share(0, half, cols_a, 0, right)
    lb = share(half, half, cols_a, 1, left)
    own.wait()
    high, low = split2(gat[y])
    both = dot_nt(high, jnp.concatenate([high, low], axis=0))
    cross = both[:, width:]
    g_loc[...] = both[:, :width] + cross + cross.T
    pl.semaphore_wait(ready.at[3], 2)
    to_pairs(lambda q: g_loc.at[rows_of(q, PIECE)], lambda n: pr.at[n], 0)
    pl.semaphore_wait(ready.at[0], 2)
    announce_z(1, 2)
    pl.semaphore_wait(ready.at[4], 2)

    @pl.when(root)
    def _():
        for d in range(1, NY):
            pltpu.make_async_remote_copy(
                src_ref=gat.at[0, :, pl.ds(0, width)], dst_ref=p1w, send_sem=p1_send.at[d - 1],
                recv_sem=st_recv.at[3], device_id=at_y(d), device_id_type=MESH).start()
        p1w[...] = gat[0, :, 0:width]

    settle(pr, st_recv.at[0])
    total = g_loc[rows_of(pair, PIECE), :]
    for d in range(PAIRS - 1):
        total = total + pr[d]
    yr[y] = total
    loop(1, NY, lambda d: send(yr.at[y], yr.at[y], 10, at_y((y + d) % NY)))
    rb = share(half, half, cols_a, 2, right)
    la = share(0, half, cols_a, 3, left)
    swaps = []
    for index, target in ((8, right), (9, left), (10, far)):
        cols = pl.ds(pl.multiple_of(target * part + main, LANES), tail)
        swaps.append(gather_copy(t_hbm.at[:, cols], tb.at[y], index, target))
        swaps[-1].start()
    loads = [pltpu.make_async_copy(t_hbm.at[:, pl.ds(c * part, part)], tv.at[c], loc.at[1 + c])
             for c in range(NY)]
    for load in loads:
        load.start()
    pl.semaphore_wait(ready.at[1], 2)
    announce_z(2, 4)
    settle(yr.at[pl.ds(0, NY - 1)], st_recv.at[10])
    total = yr[0]
    for q in range(1, NY):
        total = total + yr[q]
    gz[z] = total
    pl.semaphore_wait(ready.at[2], 2)
    to_z(gz.at[z], 1)

    @pl.when((space == 0) & (y > 0))
    def _():
        settle(p1w, st_recv.at[3])

    @pl.when(space == 0)
    def _():
        loop(1, PAIRS, lambda q: send(p1w.at[rows_of(q, PIECE)], p1s, 4, at_pair(q)))
        p1s[...] = p1w[0:PIECE, :]

    @pl.when((z == 0) & (pair > 0))
    def _():
        settle(p1s, st_recv.at[4])

    @pl.when(z == 0)
    def _():
        loop(1, NZ, lambda d: send(p1s, p1s, 5, at_z(d)))

    for load in loads:
        load.wait()

    @pl.when(space == 0)
    def _():
        to_pairs(lambda q: tv.at[0, rows_of(q, BLK), pl.ds(0, width)], lambda n: t1, 11)
        t1[...] = tv[0, 0:BLK, 0:width]

    def products(trail, block):
        ph, pl_ = split2(block)
        th, tl = split2(trail)
        four = dot_nt(jnp.concatenate([th, tl], axis=0), jnp.concatenate([ph, pl_], axis=0))
        n = th.shape[0]
        return (four[:n, :width] + four[n:, :width]) + (four[:n, width:] + four[n:, width:])

    outs = []

    def put_out(c, cols):
        copy = pltpu.make_async_copy(gat.at[c, :, cols], gat_out.at[c, :, cols],
                                     out_sem.at[len(outs)])
        copy.start()
        outs.append(copy)

    def add_main(c):
        m_loc[0] += products(tv[c, :, 0:main], gat[c, :, 0:main])

    m_loc[0] = products(tv[y], gat[y])
    put_out(y, pl.ds(0, part))

    ra.wait_recv()
    fa = forward(left, top, cols_a, 4, right)
    lb.wait_recv()
    fb = forward(right, bottom, cols_a, 5, left)
    fill = 24
    ra_b0 = share(0, fill, cols_b, 6, right)
    lb_b0 = share(half, fill, cols_b, 7, left)
    rb.wait_recv()
    add_main(left)
    la.wait_recv()
    add_main(right)

    def second(start, size, index, target):
        lines = pl.ds(start, size)
        return gather_copy(p_hbm.at[lines, cols_b], gat.at[y, lines, cols_b], index, target)

    def relay(block, lines, index, target):
        ref = gat.at[block, lines, cols_b]
        return gather_copy(ref, ref, index, target)

    ra_b = second(fill, half - fill, 11, right)
    lb_b = second(half + fill, half - fill, 12, left)
    rb_b = second(half, half, 13, right)
    la_b = second(0, half, 14, left)
    fa_b = relay(left, top, 15, right)
    fb_b = relay(right, bottom, 16, left)

    def finish_first():
        for swap in swaps:
            swap.wait_recv()
        others_t = jnp.concatenate([tb[right], tb[far], tb[left]], axis=0)
        swapped = products(others_t, gat[y, :, main:part])
        for r in range(1, NY):
            m_loc[r] = swapped[(r - 1) * rows:r * rows, :]
        fa.wait_recv()
        fb.wait_recv()
        add_main(far)
        for n, (dx, dc, dy) in enumerate(plane_order):
            q = pair_at(dx, dc)
            send(m_loc.at[dy, rows_of(q, BLK)], pm.at[n], 7, (at_pair(q)[0], (y + dy) % NY))
        for copy in (ra_b, lb_b, rb_b, la_b):
            copy.start()

    def forward_second():
        ra_b0.wait_recv()
        ra_b.wait_recv()
        fa_b.start()
        lb_b0.wait_recv()
        lb_b.wait_recv()
        fb_b.start()

    def reduce_plane():
        settle(pm, st_recv.at[7])
        total = m_loc[0, tile, :]
        for d in range(PLANE - 1):
            total = total + pm[d]
        mz[z] = total
        to_z(mz.at[z], 8)

    tile = rows_of(pair, BLK)
    early = z < EARLY_PLANES

    @pl.when(early)
    def _():
        finish_first()


    settle(gz.at[pl.ds(0, NZ - 1)], st_recv.at[1])
    total = gz[0]
    for q in range(1, NZ):
        total = total + gz[q]
    mine = rows_of(pair, PIECE)
    gf[mine, :] = total
    to_pairs(lambda q: gf.at[mine], lambda n: gf.at[mine], 2)

    @pl.when(z > 0)
    def _():
        settle(p1s, st_recv.at[5])

    p1f[mine, :] = p1s[...]
    to_pairs(lambda q: p1f.at[mine], lambda n: p1f.at[mine], 6)

    @pl.when((z == 0) & (pair > 0))
    def _():
        settle(t1, st_recv.at[11])

    @pl.when(z == 0)
    def _():
        to_z(t1, 12)

    @pl.when(early)
    def _():
        reduce_plane()

    others = pl.ds(0, (PAIRS - 1) * PIECE)
    settle(gf.at[others], st_recv.at[2])
    work[...] = gf[...]
    loop(0, width // BLK, lambda k: chol_step(k, work, upper))
    outs.append(pltpu.make_async_copy(upper, upper_out, out_sem.at[len(outs)]))
    outs[-1].start()

    @pl.when(early)
    def _():
        forward_second()

    @pl.when(jnp.logical_not(early))
    def _():
        finish_first()

    for block in (left, right, far):
        put_out(block, cols_a)
    settle(p1f.at[others], st_recv.at[6])
    work[...] = gf[...] + jnp.dot(p1f[...], upper[...], precision=HIGHEST, preferred_element_type=F32)
    work_t[...] = work[...].T
    loop(0, MIDDLE, lambda k: inverse_step(k, work, work_t))

    @pl.when(jnp.logical_not(early))
    def _():
        reduce_plane()

    loop(MIDDLE, width // BLK, lambda k: inverse_step(k, work, work_t))

    @pl.when(jnp.logical_not(early))
    def _():
        forward_second()

    @pl.when(z > 0)
    def _():
        settle(t1, st_recv.at[12])

    total = jnp.dot(t1[...], upper[...], precision=HIGHEST, preferred_element_type=F32)
    settle(mz.at[pl.ds(0, NZ - 1)], st_recv.at[8])
    total = total + mz[0]
    for q in range(1, NZ):
        total = total + mz[q]
    zsum[tile, :] = jnp.dot(total, work[...], precision=HIGHEST, preferred_element_type=F32)
    to_pairs(lambda q: zsum.at[tile], lambda n: zsum.at[tile], 9)
    rb_b.wait_recv()
    put_out(left, cols_b)
    la_b.wait_recv()
    put_out(right, cols_b)
    fa_b.wait_recv()
    fb_b.wait_recv()
    put_out(far, cols_b)
    settle(zsum.at[pl.ds(0, (PAIRS - 1) * BLK)], st_recv.at[9])
    zt[...] = zsum[...]

    for copy in (ra, lb, rb, la, fa, fb, *swaps, ra_b0, lb_b0, ra_b, lb_b, rb_b, la_b, fa_b, fb_b):
        copy.wait_send()
    for copy in outs:
        copy.wait()
    settle(pr, st_send.at[0])

    @pl.when(space == 0)
    def _():
        settle(pm.at[pl.ds(0, PAIRS - 1)], st_send.at[11])

    @pl.when(z == 0)
    def _():
        settle(mz.at[pl.ds(0, NZ - 1)], st_send.at[12])

    settle(gz.at[pl.ds(0, NZ - 1)], st_send.at[1])
    settle(gf.at[others], st_send.at[2])

    @pl.when(root)
    def _():
        for d in range(1, NY):
            settle(p1w, p1_send.at[d - 1])

    @pl.when(space == 0)
    def _():
        settle(gf.at[others], st_send.at[4])

    @pl.when(z == 0)
    def _():
        settle(gz.at[pl.ds(0, NZ - 1)], st_send.at[5])

    settle(gf.at[others], st_send.at[6])
    settle(pm, st_send.at[7])
    settle(mz.at[pl.ds(0, NZ - 1)], st_send.at[8])
    settle(zsum.at[pl.ds(0, (PAIRS - 1) * BLK)], st_send.at[9])
    settle(yr.at[pl.ds(0, NY - 1)], st_send.at[10])


def update_kernel(scale, p_ref, t_ref, zt_ref, upper_ref, up_ref, out_ref, up, new, out_sem):
    up[...] = upper_ref[...] * scale
    copies = [pltpu.make_async_copy(up, up_ref, out_sem.at[NY])]
    copies[0].start()
    zt = zt_ref[...]
    rows, width = zt.shape
    part = p_ref.shape[2]
    zh, zl = split2(zt)
    quad = jnp.concatenate([jnp.concatenate([zh, zh], axis=1),
                            jnp.concatenate([zl, zl], axis=1)], axis=0)
    for c in range(NY):
        cols = pl.ds(c * part, part)
        ph, pl_ = split2(p_ref[c])
        both = jnp.dot(quad, jnp.concatenate([ph, pl_], axis=0), preferred_element_type=F32)
        new[c] = t_ref[:, cols] - (both[:rows] + both[rows:])
        if c == 0:
            @pl.when(lax.axis_index("space") == 0)
            def _():
                new[0, :, 0:width] -= lax.dot_general(
                    zt, upper_ref[...], (((1,), (1,)), ((), ())), precision=HIGHEST,
                    preferred_element_type=F32)
        copy = pltpu.make_async_copy(new.at[c], out_ref.at[:, cols], out_sem.at[c])
        copy.start()
        copies.append(copy)
    for copy in copies:
        copy.wait()


def per_device(panel, trailing):
    width, part = panel.shape
    rows, block = trailing.shape
    tail = part // LANES * 8 // 15 * LANES
    rows_total = block * lax.axis_size("space")
    vmem = pl.BlockSpec(memory_space=pltpu.VMEM)
    hbm = pl.BlockSpec(memory_space=pltpu.HBM)
    anywhere = pl.BlockSpec(memory_space=pl.ANY)

    def buf(*shape):
        return pltpu.VMEM(shape, F32)

    gat, upper, zt = pl.pallas_call(
        main_kernel,
        out_shape=(
            jax.ShapeDtypeStruct((NY, width, part), F32),
            jax.ShapeDtypeStruct((width, width), F32),
            jax.ShapeDtypeStruct((rows, width), F32),
        ),
        in_specs=[hbm, hbm],
        out_specs=(anywhere, anywhere, vmem),
        scratch_shapes=[
            buf(NY, width, part),
            buf(NY, rows, part),
            buf(NY, rows, tail),
            buf(width, width),
            buf(PAIRS - 1, PIECE, width),
            buf(NY, PIECE, width),
            buf(NZ, PIECE, width),
            buf(width, width),
            buf(width, width),
            buf(PIECE, width),
            buf(width, width),
            buf(BLK, width),
            buf(width, width),
            buf(NY, rows, width),
            buf(PLANE - 1, BLK, width),
            buf(NZ, BLK, width),
            buf(rows, width),
            buf(width, width),
            buf(width, width),
            pltpu.SemaphoreType.DMA((17,)),
            pltpu.SemaphoreType.DMA((17,)),
            pltpu.SemaphoreType.DMA((1 + NY,)),
            pltpu.SemaphoreType.DMA((2 * NY,)),
            pltpu.SemaphoreType.DMA((13,)),
            pltpu.SemaphoreType.DMA((13,)),
            pltpu.SemaphoreType.DMA((NY - 1,)),
            pltpu.SemaphoreType.REGULAR((5,)),
        ],
        compiler_params=pltpu.CompilerParams(
            collective_id=0, has_side_effects=True, vmem_limit_bytes=40 * 2**20),
        name="reduce_factor",
    )(pltpu.with_memory_space_constraint(panel, pltpu.HBM),
      pltpu.with_memory_space_constraint(trailing, pltpu.HBM))

    upper_factor, updated = pl.pallas_call(
        functools.partial(update_kernel, -1.0 / math.sqrt(rows_total)),
        out_shape=(
            jax.ShapeDtypeStruct((width, width), F32),
            jax.ShapeDtypeStruct((rows, block), F32),
        ),
        in_specs=[vmem] * 4,
        out_specs=(hbm, hbm),
        scratch_shapes=[
            buf(width, width), buf(NY, rows, part), pltpu.SemaphoreType.DMA((NY + 1,))],
        compiler_params=pltpu.CompilerParams(vmem_limit_bytes=40 * 2**20),
        name="apply_update",
    )(gat, trailing, zt, upper)
    return (upper_factor, updated)


def solution(mesh):
    return jax.shard_map(
        per_device,
        mesh=mesh,
        in_specs=(P(None, ("space", "col")), P("col", "space")),
        out_specs=(P(), P("col", "space")),
        check_vma=False,
    )
```

```python
import functools
import math

import jax
import jax.numpy as jnp
from jax import lax
from jax.experimental import pallas as pl
from jax.experimental.pallas import tpu as pltpu
from jax.sharding import PartitionSpec as P

F32 = jnp.float32
BF16 = jnp.bfloat16
HIGHEST = lax.Precision.HIGHEST
MESH = pl.DeviceIdType.MESH
NX, NZ, NCORE, NY = 4, 16, 2, 4
PAIRS = NX * NCORE
BLK = 8
LANES = 128
PIECE = 16
MIDDLE = 8
EARLY_PLANES = 3
PLANE = PAIRS * NY


def split2(x):
    high = x.astype(BF16)
    low = (x - high.astype(F32)).astype(BF16)
    return high, low


def split3(x):
    high = x.astype(BF16).astype(F32)
    rest = x - high
    mid = rest.astype(BF16).astype(F32)
    return high, mid, rest - mid


def stacks(a, b):
    ah, am, al = split3(a)
    bh, bm, bl = split3(b)
    left = jnp.concatenate([ah, ah, ah, am, am, al], axis=0).astype(BF16)
    right = jnp.concatenate([bh, bm, bl, bh, bm, bh], axis=0).astype(BF16)
    return left, right


def dot_tn(a, b):
    return lax.dot_general(a, b, (((0,), (0,)), ((), ())), preferred_element_type=F32)


def dot_nt(a, b):
    return lax.dot_general(a, b, (((1,), (1,)), ((), ())), preferred_element_type=F32)


def recip(x):
    y = pl.reciprocal(x, approx=True)
    return y * (2.0 - x * y)


def lane_splat(x, lane):
    return jnp.take_along_axis(x, jnp.full(x.shape, lane, jnp.int32), axis=1)


def merge(rows, row8):
    out = rows[0]
    for i in range(1, len(rows)):
        out = jnp.where(row8 == i, rows[i], out)
    return out


def block_rows(ref, base):
    width = ref.shape[1]
    return [jnp.broadcast_to(ref[pl.ds(base + i, 1), :], (BLK, width)) for i in range(BLK)]


def chol_step(k, work, upper):
    width = work.shape[1]
    row8 = lax.broadcasted_iota(jnp.int32, (BLK, width), 0)
    lane8 = lax.broadcasted_iota(jnp.int32, (BLK, width), 1)
    base = pl.multiple_of(k * BLK, BLK)
    rows = block_rows(work, base)
    s = {(i, j): lane_splat(rows[i], base + j) for i in range(BLK) for j in range(i, BLK)}
    for j in range(BLK):
        inv = recip(s[j, j])
        for i in range(j + 1, BLK):
            factor = s[j, i] * inv
            for l in range(i, BLK):
                s[i, l] = s[i, l] - factor * s[j, l]
            rows[i] = rows[i] - factor * rows[j]
    pivots = merge([s[j, j] for j in range(BLK)], row8)
    block = merge(rows, row8) * lax.rsqrt(pivots)
    block = jnp.where(lane8 >= row8 + base, block, 0.0)
    upper[pl.ds(base, BLK), :] = block
    left, right = stacks(block, block)
    work[...] -= dot_tn(left, right)


def inverse_step(k, mat, mat_t):
    width = mat.shape[1]
    row8 = lax.broadcasted_iota(jnp.int32, (BLK, width), 0)
    lane8 = lax.broadcasted_iota(jnp.int32, (BLK, width), 1)
    base = pl.multiple_of(k * BLK, BLK)
    rows = block_rows(mat, base)
    cols = mat_t[pl.ds(base, BLK), :]
    s = {(i, j): lane_splat(rows[i], base + j) for i in range(BLK) for j in range(BLK)}
    for j in range(BLK):
        inv = recip(s[j, j])
        at = lane8 == base + j
        scaled = jnp.where(at, 1.0, rows[j]) * inv
        for l in range(j + 1, BLK):
            s[j, l] = s[j, l] * inv
        for i in range(BLK):
            if i == j:
                continue
            for l in range(j + 1, BLK):
                s[i, l] = s[i, l] - s[i, j] * s[j, l]
            rows[i] = jnp.where(at, 0.0, rows[i]) - s[i, j] * scaled
        rows[j] = scaled
    block = merge(rows, row8)
    inside = (lane8 >= base) & (lane8 < base + BLK)
    cols = jnp.where(inside, jnp.where(lane8 == row8 + base, -1.0, 0.0), cols)
    left, right = stacks(cols, block)
    row_id = lax.broadcasted_iota(jnp.int32, (width, width), 0)
    lane_id = lax.broadcasted_iota(jnp.int32, (width, width), 1)
    row_out = (row_id < base) | (row_id >= base + BLK)
    lane_out = (lane_id < base) | (lane_id >= base + BLK)
    keep = row_out & lane_out
    mat[...] = jnp.where(keep, mat[...], 0.0) - dot_tn(left, right)
    mat_t[...] = jnp.where(keep, mat_t[...], 0.0) - dot_tn(right, left)


def main_kernel(p_hbm, t_hbm, gat_out, upper_out, zt,
                gat, tv, tb, g_loc, pr, yr, gz, gf, p1w, p1s, p1f, upper, m_loc, pm, mz, zsum, work, work_t,
                gp_send, gp_recv, loc, out_sem, st_send, st_recv, p1_send, ready):
    width, part = p_hbm.shape
    half = width // 2
    rows = t_hbm.shape[0]
    tail = tb.shape[2]
    main = part - tail
    space = lax.axis_index("space")
    y = lax.axis_index("col")
    core = space % NCORE
    z = (space // NCORE) % NZ
    x = space // (NCORE * NZ)
    pair = x * NCORE + core
    right, left, far = (y + 1) % NY, (y + NY - 1) % NY, (y + 2) % NY
    root = (space == 0) & (y == 0)

    z_order = sorted(range(1, NZ), key=lambda d: -min(d, NZ - d))
    plane_order = sorted(
        ((dx, dc, dy) for dx in range(NX) for dc in range(NCORE) for dy in range(NY)),
        key=lambda d: -(min(d[0], NX - d[0]) + d[1] + min(d[2], NY - d[2])))[:-1]
    pair_order = [(dx, dc) for dx, dc, dy in plane_order if dy == 0]

    def pair_at(dx, dc):
        return ((x + dx) % NX) * NCORE + (core + dc) % NCORE

    def to_pairs(src, dst, stage):
        for n, (dx, dc) in enumerate(pair_order):
            q = pair_at(dx, dc)
            send(src(q), dst(n), stage, at_pair(q))

    def to_z(ref, stage):
        for d in z_order:
            send(ref, ref, stage, at_z((z + d) % NZ))

    def at_z(zz):
        return (x * (NZ * NCORE) + zz * NCORE + core, y)

    def at_y(yy):
        return (space, yy)

    def at_pair(q):
        return ((q // NCORE) * (NZ * NCORE) + z * NCORE + q % NCORE, y)

    def loop(low, high, body):
        lax.fori_loop(low, high, lambda i, c: (body(i), c)[1], 0)

    def send(src, dst, stage, device):
        pltpu.make_async_remote_copy(
            src_ref=src, dst_ref=dst, send_sem=st_send.at[stage], recv_sem=st_recv.at[stage],
            device_id=device, device_id_type=MESH).start()

    def settle(ref, sem):
        pltpu.make_async_copy(ref, ref, sem).wait()

    def rows_of(i, size):
        return pl.ds(pl.multiple_of(i * size, size), size)

    barrier = pltpu.get_barrier_semaphore()

    def greet(device):
        pl.semaphore_signal(barrier, inc=1, device_id=device, device_id_type=MESH)

    own = pltpu.make_async_copy(p_hbm, gat.at[y], loc.at[0])
    own.start()
    greet(at_z((z + 1) % NZ))
    greet(at_z((z + NZ - 1) % NZ))
    for step in (1, NY - 1):
        greet(at_y((y + step) % NY))
    near = [(0, 1), (1, 0), (NX - 1, 0), (1, 1), (NX - 1, 1)]
    for dx, dc in near:
        greet(at_pair(pair_at(dx, dc)))
    pl.semaphore_wait(barrier, 4 + len(near))

    def announce(level, one, other):
        for device in (one, other):
            pl.semaphore_signal(ready.at[level], inc=1, device_id=device, device_id_type=MESH)

    def announce_z(level, step):
        announce(level, at_z((z + step) % NZ), at_z((z + NZ - step) % NZ))

    announce(3, at_pair(pair_at(1, 0)), at_pair(pair_at(NX - 1, 0)))
    announce(4, at_y(right), at_y(left))
    announce_z(0, 1)

    def gather_copy(src, dst, index, target):
        return pltpu.make_async_remote_copy(
            src_ref=src, dst_ref=dst, send_sem=gp_send.at[index], recv_sem=gp_recv.at[index],
            device_id=(space, target), device_id_type=MESH)

    def share(start, size, cols, index, target):
        lines = pl.ds(start, size)
        copy = gather_copy(p_hbm.at[lines, cols], gat.at[y, lines, cols], index, target)
        copy.start()
        return copy

    def forward(block, lines, cols, index, target):
        ref = gat.at[block, lines, cols]
        copy = gather_copy(ref, ref, index, target)
        copy.start()
        return copy

    first, second_half = pl.ds(0, half), pl.ds(half, half)
    cols_a, cols_b = pl.ds(0, main), pl.ds(main, tail)
    ra = share(0, half, cols_a, 0, right)
    lb = share(half, half, cols_a, 1, left)
    own.wait()
    high, low = split2(gat[y])
    both = dot_nt(high, jnp.concatenate([high, low], axis=0))
    cross = both[:, width:]
    g_loc[...] = both[:, :width] + cross + cross.T
    pl.semaphore_wait(ready.at[3], 2)
    to_pairs(lambda q: g_loc.at[rows_of(q, PIECE)], lambda n: pr.at[n], 0)
    pl.semaphore_wait(ready.at[0], 2)
    announce_z(1, 2)
    pl.semaphore_wait(ready.at[4], 2)

    @pl.when(root)
    def _():
        for d in range(1, NY):
            pltpu.make_async_remote_copy(
                src_ref=gat.at[0, :, pl.ds(0, width)], dst_ref=p1w, send_sem=p1_send.at[d - 1],
                recv_sem=st_recv.at[3], device_id=at_y(d), device_id_type=MESH).start()
        p1w[...] = gat[0, :, 0:width]

    settle(pr, st_recv.at[0])
    total = g_loc[rows_of(pair, PIECE), :]
    for d in range(PAIRS - 1):
        total = total + pr[d]
    yr[y] = total
    loop(1, NY, lambda d: send(yr.at[y], yr.at[y], 10, at_y((y + d) % NY)))
    rb = share(half, half, cols_a, 2, right)
    la = share(0, half, cols_a, 3, left)
    swaps = []
    for index, target in ((8, right), (9, left), (10, far)):
        cols = pl.ds(pl.multiple_of(target * part + main, LANES), tail)
        swaps.append(gather_copy(t_hbm.at[:, cols], tb.at[y], index, target))
        swaps[-1].start()
    loads = [pltpu.make_async_copy(t_hbm.at[:, pl.ds(c * part, part)], tv.at[c], loc.at[1 + c])
             for c in range(NY)]
    for load in loads:
        load.start()
    pl.semaphore_wait(ready.at[1], 2)
    announce_z(2, 4)
    settle(yr.at[pl.ds(0, NY - 1)], st_recv.at[10])
    total = yr[0]
    for q in range(1, NY):
        total = total + yr[q]
    gz[z] = total
    pl.semaphore_wait(ready.at[2], 2)
    to_z(gz.at[z], 1)

    @pl.when((space == 0) & (y > 0))
    def _():
        settle(p1w, st_recv.at[3])

    @pl.when(space == 0)
    def _():
        loop(1, PAIRS, lambda q: send(p1w.at[rows_of(q, PIECE)], p1s, 4, at_pair(q)))
        p1s[...] = p1w[0:PIECE, :]

    @pl.when((z == 0) & (pair > 0))
    def _():
        settle(p1s, st_recv.at[4])

    @pl.when(z == 0)
    def _():
        loop(1, NZ, lambda d: send(p1s, p1s, 5, at_z(d)))

    for load in loads:
        load.wait()

    def products(trail, block):
        ph, pl_ = split2(block)
        th, tl = split2(trail)
        four = dot_nt(jnp.concatenate([th, tl], axis=0), jnp.concatenate([ph, pl_], axis=0))
        n = th.shape[0]
        return (four[:n, :width] + four[n:, :width]) + (four[:n, width:] + four[n:, width:])

    outs = []

    def put_out(c, cols):
        copy = pltpu.make_async_copy(gat.at[c, :, cols], gat_out.at[c, :, cols],
                                     out_sem.at[len(outs)])
        copy.start()
        outs.append(copy)

    def add_main(c):
        m_loc[0] += products(tv[c, :, 0:main], gat[c, :, 0:main])
        put_out(c, cols_a)

    m_loc[0] = products(tv[y], gat[y])
    put_out(y, pl.ds(0, part))

    ra.wait_recv()
    fa = forward(left, first, cols_a, 4, right)
    lb.wait_recv()
    fb = forward(right, second_half, cols_a, 5, left)
    fill = 24
    ra_b0 = share(0, fill, cols_b, 6, right)
    lb_b0 = share(half, fill, cols_b, 7, left)

    def second(start, size, index, target):
        lines = pl.ds(start, size)
        return gather_copy(p_hbm.at[lines, cols_b], gat.at[y, lines, cols_b], index, target)

    def relay(block, lines, index, target):
        ref = gat.at[block, lines, cols_b]
        return gather_copy(ref, ref, index, target)

    ra_b = second(fill, half - fill, 11, right)
    lb_b = second(half + fill, half - fill, 12, left)
    rb_b = second(half, half, 13, right)
    la_b = second(0, half, 14, left)
    fa_b = relay(left, first, 15, right)
    fb_b = relay(right, second_half, 16, left)

    def start_second():
        for copy in (ra_b, lb_b, rb_b, la_b):
            copy.start()

    def forward_second():
        ra_b0.wait_recv()
        ra_b.wait_recv()
        fa_b.start()
        lb_b0.wait_recv()
        lb_b.wait_recv()
        fb_b.start()

    early = z < EARLY_PLANES

    @pl.when(early)
    def _():
        start_second()

    rb.wait_recv()
    add_main(left)
    la.wait_recv()
    add_main(right)

    settle(gz.at[pl.ds(0, NZ - 1)], st_recv.at[1])
    total = gz[0]
    for q in range(1, NZ):
        total = total + gz[q]
    mine = rows_of(pair, PIECE)
    gf[mine, :] = total
    to_pairs(lambda q: gf.at[mine], lambda n: gf.at[mine], 2)

    @pl.when(z > 0)
    def _():
        settle(p1s, st_recv.at[5])

    p1f[mine, :] = p1s[...]
    to_pairs(lambda q: p1f.at[mine], lambda n: p1f.at[mine], 6)

    others = pl.ds(0, (PAIRS - 1) * PIECE)
    settle(gf.at[others], st_recv.at[2])
    work[...] = gf[...]
    loop(0, width // BLK // 2, lambda k: chol_step(k, work, upper))

    @pl.when(early)
    def _():
        forward_second()

    loop(width // BLK // 2, width // BLK, lambda k: chol_step(k, work, upper))
    outs.append(pltpu.make_async_copy(upper, upper_out, out_sem.at[len(outs)]))
    outs[-1].start()
    @pl.when(space == 0)
    def _():
        m_loc[0] += jnp.dot(tv[0, :, 0:width], upper[...], precision=HIGHEST,
                            preferred_element_type=F32)

    for swap in swaps:
        swap.wait_recv()
    others_t = jnp.concatenate([tb[right], tb[far], tb[left]], axis=0)
    swapped = products(others_t, gat[y, :, main:part])
    for r in range(1, NY):
        m_loc[r] = swapped[(r - 1) * rows:r * rows, :]
    fa.wait_recv()
    fb.wait_recv()
    add_main(far)

    for n, (dx, dc, dy) in enumerate(plane_order):
        q = pair_at(dx, dc)
        send(m_loc.at[dy, rows_of(q, BLK)], pm.at[n], 7, (at_pair(q)[0], (y + dy) % NY))

    @pl.when(jnp.logical_not(early))
    def _():
        start_second()

    settle(p1f.at[others], st_recv.at[6])
    work[...] = gf[...] + jnp.dot(p1f[...], upper[...], precision=HIGHEST, preferred_element_type=F32)
    work_t[...] = work[...].T
    loop(0, MIDDLE, lambda k: inverse_step(k, work, work_t))
    settle(pm, st_recv.at[7])
    tile = rows_of(pair, BLK)
    total = m_loc[0, tile, :]
    for d in range(PLANE - 1):
        total = total + pm[d]
    mz[z] = total
    to_z(mz.at[z], 8)
    loop(MIDDLE, width // BLK, lambda k: inverse_step(k, work, work_t))

    @pl.when(jnp.logical_not(early))
    def _():
        forward_second()

    settle(mz.at[pl.ds(0, NZ - 1)], st_recv.at[8])
    total = mz[0]
    for q in range(1, NZ):
        total = total + mz[q]
    zsum[tile, :] = jnp.dot(total, work[...], precision=HIGHEST, preferred_element_type=F32)
    to_pairs(lambda q: zsum.at[tile], lambda n: zsum.at[tile], 9)
    rb_b.wait_recv()
    put_out(left, cols_b)
    la_b.wait_recv()
    put_out(right, cols_b)
    fa_b.wait_recv()
    fb_b.wait_recv()
    put_out(far, cols_b)
    settle(zsum.at[pl.ds(0, (PAIRS - 1) * BLK)], st_recv.at[9])
    zt[...] = zsum[...]

    for copy in (ra, lb, rb, la, fa, fb, *swaps, ra_b0, lb_b0, ra_b, lb_b, rb_b, la_b, fa_b, fb_b):
        copy.wait_send()
    for copy in outs:
        copy.wait()
    settle(pr, st_send.at[0])
    settle(gz.at[pl.ds(0, NZ - 1)], st_send.at[1])
    settle(gf.at[others], st_send.at[2])

    @pl.when(root)
    def _():
        for d in range(1, NY):
            settle(p1w, p1_send.at[d - 1])

    @pl.when(space == 0)
    def _():
        settle(gf.at[others], st_send.at[4])

    @pl.when(z == 0)
    def _():
        settle(gz.at[pl.ds(0, NZ - 1)], st_send.at[5])

    settle(gf.at[others], st_send.at[6])
    settle(pm, st_send.at[7])
    settle(mz.at[pl.ds(0, NZ - 1)], st_send.at[8])
    settle(zsum.at[pl.ds(0, (PAIRS - 1) * BLK)], st_send.at[9])
    settle(yr.at[pl.ds(0, NY - 1)], st_send.at[10])


def update_kernel(scale, p_ref, t_ref, zt_ref, upper_ref, up_ref, out_ref, up, new, out_sem):
    up[...] = upper_ref[...] * scale
    copies = [pltpu.make_async_copy(up, up_ref, out_sem.at[NY])]
    copies[0].start()
    zt = zt_ref[...]
    rows, width = zt.shape
    part = p_ref.shape[2]
    zh, zl = split2(zt)
    quad = jnp.concatenate([jnp.concatenate([zh, zh], axis=1),
                            jnp.concatenate([zl, zl], axis=1)], axis=0)
    for c in range(NY):
        cols = pl.ds(c * part, part)
        ph, pl_ = split2(p_ref[c])
        both = jnp.dot(quad, jnp.concatenate([ph, pl_], axis=0), preferred_element_type=F32)
        new[c] = t_ref[:, cols] - (both[:rows] + both[rows:])
        if c == 0:
            @pl.when(lax.axis_index("space") == 0)
            def _():
                new[0, :, 0:width] -= lax.dot_general(
                    zt, upper_ref[...], (((1,), (1,)), ((), ())), precision=HIGHEST,
                    preferred_element_type=F32)
        copy = pltpu.make_async_copy(new.at[c], out_ref.at[:, cols], out_sem.at[c])
        copy.start()
        copies.append(copy)
    for copy in copies:
        copy.wait()


def per_device(panel, trailing):
    width, part = panel.shape
    rows, block = trailing.shape
    tail = part // LANES * 7 // 15 * LANES
    rows_total = block * lax.axis_size("space")
    vmem = pl.BlockSpec(memory_space=pltpu.VMEM)
    hbm = pl.BlockSpec(memory_space=pltpu.HBM)
    anywhere = pl.BlockSpec(memory_space=pl.ANY)

    def buf(*shape):
        return pltpu.VMEM(shape, F32)

    gat, upper, zt = pl.pallas_call(
        main_kernel,
        out_shape=(
            jax.ShapeDtypeStruct((NY, width, part), F32),
            jax.ShapeDtypeStruct((width, width), F32),
            jax.ShapeDtypeStruct((rows, width), F32),
        ),
        in_specs=[hbm, hbm],
        out_specs=(anywhere, anywhere, vmem),
        scratch_shapes=[
            buf(NY, width, part),
            buf(NY, rows, part),
            buf(NY, rows, tail),
            buf(width, width),
            buf(PAIRS - 1, PIECE, width),
            buf(NY, PIECE, width),
            buf(NZ, PIECE, width),
            buf(width, width),
            buf(width, width),
            buf(PIECE, width),
            buf(width, width),
            buf(width, width),
            buf(NY, rows, width),
            buf(PLANE - 1, BLK, width),
            buf(NZ, BLK, width),
            buf(rows, width),
            buf(width, width),
            buf(width, width),
            pltpu.SemaphoreType.DMA((17,)),
            pltpu.SemaphoreType.DMA((17,)),
            pltpu.SemaphoreType.DMA((1 + NY,)),
            pltpu.SemaphoreType.DMA((2 * NY,)),
            pltpu.SemaphoreType.DMA((11,)),
            pltpu.SemaphoreType.DMA((11,)),
            pltpu.SemaphoreType.DMA((NY - 1,)),
            pltpu.SemaphoreType.REGULAR((5,)),
        ],
        compiler_params=pltpu.CompilerParams(
            collective_id=0, has_side_effects=True, vmem_limit_bytes=40 * 2**20),
        name="reduce_factor",
    )(pltpu.with_memory_space_constraint(panel, pltpu.HBM),
      pltpu.with_memory_space_constraint(trailing, pltpu.HBM))

    upper_factor, updated = pl.pallas_call(
        functools.partial(update_kernel, -1.0 / math.sqrt(rows_total)),
        out_shape=(
            jax.ShapeDtypeStruct((width, width), F32),
            jax.ShapeDtypeStruct((rows, block), F32),
        ),
        in_specs=[vmem] * 4,
        out_specs=(hbm, hbm),
        scratch_shapes=[
            buf(width, width), buf(NY, rows, part), pltpu.SemaphoreType.DMA((NY + 1,))],
        compiler_params=pltpu.CompilerParams(vmem_limit_bytes=40 * 2**20),
        name="apply_update",
    )(gat, trailing, zt, upper)
    return (upper_factor, updated)


def solution(mesh):
    return jax.shard_map(
        per_device,
        mesh=mesh,
        in_specs=(P(None, ("space", "col")), P("col", "space")),
        out_specs=(P(), P("col", "space")),
        check_vma=False,
    )
```

```python
import functools
import math

import jax
import jax.numpy as jnp
from jax import lax
from jax.experimental import pallas as pl
from jax.experimental.pallas import tpu as pltpu
from jax.sharding import PartitionSpec as P

F32 = jnp.float32
BF16 = jnp.bfloat16
HIGHEST = lax.Precision.HIGHEST
MESH = pl.DeviceIdType.MESH
NX, NZ, NCORE, NY = 4, 16, 2, 4
PAIRS = NX * NCORE
BLK = 8
LANES = 128
PIECE = 16
MIDDLE = 8
EARLY_PLANES = 3
PLANE = PAIRS * NY


def split2(x):
    high = x.astype(BF16)
    low = (x - high.astype(F32)).astype(BF16)
    return high, low


def split3(x):
    high = x.astype(BF16).astype(F32)
    rest = x - high
    mid = rest.astype(BF16).astype(F32)
    return high, mid, rest - mid


def stacks(a, b):
    ah, am, al = split3(a)
    bh, bm, bl = split3(b)
    left = jnp.concatenate([ah, ah, ah, am, am, al], axis=0).astype(BF16)
    right = jnp.concatenate([bh, bm, bl, bh, bm, bh], axis=0).astype(BF16)
    return left, right


def dot_tn(a, b):
    return lax.dot_general(a, b, (((0,), (0,)), ((), ())), preferred_element_type=F32)


def dot_nt(a, b):
    return lax.dot_general(a, b, (((1,), (1,)), ((), ())), preferred_element_type=F32)


def recip(x):
    y = pl.reciprocal(x, approx=True)
    return y * (2.0 - x * y)


def lane_splat(x, lane):
    return jnp.take_along_axis(x, jnp.full(x.shape, lane, jnp.int32), axis=1)


def merge(rows, row8):
    out = rows[0]
    for i in range(1, len(rows)):
        out = jnp.where(row8 == i, rows[i], out)
    return out


def block_rows(ref, base):
    width = ref.shape[1]
    return [jnp.broadcast_to(ref[pl.ds(base + i, 1), :], (BLK, width)) for i in range(BLK)]


def chol_step(k, work, upper):
    width = work.shape[1]
    row8 = lax.broadcasted_iota(jnp.int32, (BLK, width), 0)
    lane8 = lax.broadcasted_iota(jnp.int32, (BLK, width), 1)
    base = pl.multiple_of(k * BLK, BLK)
    rows = block_rows(work, base)
    s = {(i, j): lane_splat(rows[i], base + j) for i in range(BLK) for j in range(i, BLK)}
    for j in range(BLK):
        inv = recip(s[j, j])
        for i in range(j + 1, BLK):
            factor = s[j, i] * inv
            for l in range(i, BLK):
                s[i, l] = s[i, l] - factor * s[j, l]
            rows[i] = rows[i] - factor * rows[j]
    pivots = merge([s[j, j] for j in range(BLK)], row8)
    block = merge(rows, row8) * lax.rsqrt(pivots)
    block = jnp.where(lane8 >= row8 + base, block, 0.0)
    upper[pl.ds(base, BLK), :] = block
    left, right = stacks(block, block)
    work[...] -= dot_tn(left, right)


def inverse_step(k, mat, mat_t):
    width = mat.shape[1]
    row8 = lax.broadcasted_iota(jnp.int32, (BLK, width), 0)
    lane8 = lax.broadcasted_iota(jnp.int32, (BLK, width), 1)
    base = pl.multiple_of(k * BLK, BLK)
    rows = block_rows(mat, base)
    cols = mat_t[pl.ds(base, BLK), :]
    s = {(i, j): lane_splat(rows[i], base + j) for i in range(BLK) for j in range(BLK)}
    for j in range(BLK):
        inv = recip(s[j, j])
        at = lane8 == base + j
        scaled = jnp.where(at, 1.0, rows[j]) * inv
        for l in range(j + 1, BLK):
            s[j, l] = s[j, l] * inv
        for i in range(BLK):
            if i == j:
                continue
            for l in range(j + 1, BLK):
                s[i, l] = s[i, l] - s[i, j] * s[j, l]
            rows[i] = jnp.where(at, 0.0, rows[i]) - s[i, j] * scaled
        rows[j] = scaled
    block = merge(rows, row8)
    inside = (lane8 >= base) & (lane8 < base + BLK)
    cols = jnp.where(inside, jnp.where(lane8 == row8 + base, -1.0, 0.0), cols)
    left, right = stacks(cols, block)
    row_id = lax.broadcasted_iota(jnp.int32, (width, width), 0)
    lane_id = lax.broadcasted_iota(jnp.int32, (width, width), 1)
    row_out = (row_id < base) | (row_id >= base + BLK)
    lane_out = (lane_id < base) | (lane_id >= base + BLK)
    keep = row_out & lane_out
    mat[...] = jnp.where(keep, mat[...], 0.0) - dot_tn(left, right)
    mat_t[...] = jnp.where(keep, mat_t[...], 0.0) - dot_tn(right, left)


def main_kernel(p_hbm, t_hbm, gat_out, upper_out, zt,
                gat, tv, tb, g_loc, pr, yr, gz, gf, p1w, p1s, p1f, upper, m_loc, pm, mz, zsum, work, work_t,
                gp_send, gp_recv, loc, out_sem, st_send, st_recv, p1_send, ready):
    width, part = p_hbm.shape
    half = width // 2
    rows = t_hbm.shape[0]
    tail = tb.shape[2]
    main = part - tail
    space = lax.axis_index("space")
    y = lax.axis_index("col")
    core = space % NCORE
    z = (space // NCORE) % NZ
    x = space // (NCORE * NZ)
    pair = x * NCORE + core
    right, left, far = (y + 1) % NY, (y + NY - 1) % NY, (y + 2) % NY
    root = (space == 0) & (y == 0)

    z_order = sorted(range(1, NZ), key=lambda d: -min(d, NZ - d))
    plane_order = sorted(
        ((dx, dc, dy) for dx in range(NX) for dc in range(NCORE) for dy in range(NY)),
        key=lambda d: -(min(d[0], NX - d[0]) + d[1] + min(d[2], NY - d[2])))[:-1]
    pair_order = [(dx, dc) for dx, dc, dy in plane_order if dy == 0]

    def pair_at(dx, dc):
        return ((x + dx) % NX) * NCORE + (core + dc) % NCORE

    def to_pairs(src, dst, stage):
        for n, (dx, dc) in enumerate(pair_order):
            q = pair_at(dx, dc)
            send(src(q), dst(n), stage, at_pair(q))

    def to_z(ref, stage):
        for d in z_order:
            send(ref, ref, stage, at_z((z + d) % NZ))

    def at_z(zz):
        return (x * (NZ * NCORE) + zz * NCORE + core, y)

    def at_y(yy):
        return (space, yy)

    def at_pair(q):
        return ((q // NCORE) * (NZ * NCORE) + z * NCORE + q % NCORE, y)

    def loop(low, high, body):
        lax.fori_loop(low, high, lambda i, c: (body(i), c)[1], 0)

    def send(src, dst, stage, device):
        pltpu.make_async_remote_copy(
            src_ref=src, dst_ref=dst, send_sem=st_send.at[stage], recv_sem=st_recv.at[stage],
            device_id=device, device_id_type=MESH).start()

    def settle(ref, sem):
        pltpu.make_async_copy(ref, ref, sem).wait()

    def rows_of(i, size):
        return pl.ds(pl.multiple_of(i * size, size), size)

    barrier = pltpu.get_barrier_semaphore()

    def greet(device):
        pl.semaphore_signal(barrier, inc=1, device_id=device, device_id_type=MESH)

    own = pltpu.make_async_copy(p_hbm, gat.at[y], loc.at[0])
    own.start()
    greet(at_z((z + 1) % NZ))
    greet(at_z((z + NZ - 1) % NZ))
    for step in (1, NY - 1):
        greet(at_y((y + step) % NY))
    near = [(0, 1), (1, 0), (NX - 1, 0), (1, 1), (NX - 1, 1)]
    for dx, dc in near:
        greet(at_pair(pair_at(dx, dc)))
    pl.semaphore_wait(barrier, 4 + len(near))

    def announce(level, one, other):
        for device in (one, other):
            pl.semaphore_signal(ready.at[level], inc=1, device_id=device, device_id_type=MESH)

    def announce_z(level, step):
        announce(level, at_z((z + step) % NZ), at_z((z + NZ - step) % NZ))

    announce(3, at_pair(pair_at(1, 0)), at_pair(pair_at(NX - 1, 0)))
    announce(4, at_y(right), at_y(left))
    announce_z(0, 1)

    def gather_copy(src, dst, index, target):
        return pltpu.make_async_remote_copy(
            src_ref=src, dst_ref=dst, send_sem=gp_send.at[index], recv_sem=gp_recv.at[index],
            device_id=(space, target), device_id_type=MESH)

    def share(start, size, cols, index, target):
        lines = pl.ds(start, size)
        copy = gather_copy(p_hbm.at[lines, cols], gat.at[y, lines, cols], index, target)
        copy.start()
        return copy

    def forward(block, lines, cols, index, target):
        ref = gat.at[block, lines, cols]
        copy = gather_copy(ref, ref, index, target)
        copy.start()
        return copy

    first, second_half = pl.ds(0, half), pl.ds(half, half)
    cols_a, cols_b = pl.ds(0, main), pl.ds(main, tail)
    ra = share(0, half, cols_a, 0, right)
    lb = share(half, half, cols_a, 1, left)
    own.wait()
    high, low = split2(gat[y])
    both = dot_nt(high, jnp.concatenate([high, low], axis=0))
    cross = both[:, width:]
    g_loc[...] = both[:, :width] + cross + cross.T
    pl.semaphore_wait(ready.at[3], 2)
    to_pairs(lambda q: g_loc.at[rows_of(q, PIECE)], lambda n: pr.at[n], 0)
    pl.semaphore_wait(ready.at[0], 2)
    announce_z(1, 2)
    pl.semaphore_wait(ready.at[4], 2)

    @pl.when(root)
    def _():
        for d in range(1, NY):
            pltpu.make_async_remote_copy(
                src_ref=gat.at[0, :, pl.ds(0, width)], dst_ref=p1w, send_sem=p1_send.at[d - 1],
                recv_sem=st_recv.at[3], device_id=at_y(d), device_id_type=MESH).start()
        p1w[...] = gat[0, :, 0:width]

    settle(pr, st_recv.at[0])
    total = g_loc[rows_of(pair, PIECE), :]
    for d in range(PAIRS - 1):
        total = total + pr[d]
    yr[y] = total
    loop(1, NY, lambda d: send(yr.at[y], yr.at[y], 10, at_y((y + d) % NY)))
    rb = share(half, half, cols_a, 2, right)
    la = share(0, half, cols_a, 3, left)
    swaps = []
    for index, target in ((8, right), (9, left), (10, far)):
        cols = pl.ds(pl.multiple_of(target * part + main, LANES), tail)
        swaps.append(gather_copy(t_hbm.at[:, cols], tb.at[y], index, target))
        swaps[-1].start()
    loads = [pltpu.make_async_copy(t_hbm.at[:, pl.ds(c * part, part)], tv.at[c], loc.at[1 + c])
             for c in range(NY)]
    for load in loads:
        load.start()
    pl.semaphore_wait(ready.at[1], 2)
    announce_z(2, 4)
    settle(yr.at[pl.ds(0, NY - 1)], st_recv.at[10])
    total = yr[0]
    for q in range(1, NY):
        total = total + yr[q]
    gz[z] = total
    pl.semaphore_wait(ready.at[2], 2)
    to_z(gz.at[z], 1)

    @pl.when((space == 0) & (y > 0))
    def _():
        settle(p1w, st_recv.at[3])

    @pl.when(space == 0)
    def _():
        loop(1, PAIRS, lambda q: send(p1w.at[rows_of(q, PIECE)], p1s, 4, at_pair(q)))
        p1s[...] = p1w[0:PIECE, :]

    @pl.when((z == 0) & (pair > 0))
    def _():
        settle(p1s, st_recv.at[4])

    @pl.when(z == 0)
    def _():
        loop(1, NZ, lambda d: send(p1s, p1s, 5, at_z(d)))

    for load in loads:
        load.wait()

    def products(trail, block):
        ph, pl_ = split2(block)
        th, tl = split2(trail)
        four = dot_nt(jnp.concatenate([th, tl], axis=0), jnp.concatenate([ph, pl_], axis=0))
        n = th.shape[0]
        return (four[:n, :width] + four[n:, :width]) + (four[:n, width:] + four[n:, width:])

    outs = []

    def put_out(c, cols):
        copy = pltpu.make_async_copy(gat.at[c, :, cols], gat_out.at[c, :, cols],
                                     out_sem.at[len(outs)])
        copy.start()
        outs.append(copy)

    def add_main(c):
        m_loc[0] += products(tv[c, :, 0:main], gat[c, :, 0:main])
        put_out(c, cols_a)

    m_loc[0] = products(tv[y], gat[y])
    put_out(y, pl.ds(0, part))

    ra.wait_recv()
    fa = forward(left, first, cols_a, 4, right)
    lb.wait_recv()
    fb = forward(right, second_half, cols_a, 5, left)
    fill = 24
    ra_b0 = share(0, fill, cols_b, 6, right)
    lb_b0 = share(half, fill, cols_b, 7, left)

    def second(start, size, index, target):
        lines = pl.ds(start, size)
        return gather_copy(p_hbm.at[lines, cols_b], gat.at[y, lines, cols_b], index, target)

    def relay(block, lines, index, target):
        ref = gat.at[block, lines, cols_b]
        return gather_copy(ref, ref, index, target)

    ra_b = second(fill, half - fill, 11, right)
    lb_b = second(half + fill, half - fill, 12, left)
    rb_b = second(half, half, 13, right)
    la_b = second(0, half, 14, left)
    fa_b = relay(left, first, 15, right)
    fb_b = relay(right, second_half, 16, left)

    def start_second():
        for copy in (ra_b, lb_b, rb_b, la_b):
            copy.start()

    def forward_second():
        ra_b0.wait_recv()
        ra_b.wait_recv()
        fa_b.start()
        lb_b0.wait_recv()
        lb_b.wait_recv()
        fb_b.start()

    early = z < EARLY_PLANES

    @pl.when(early)
    def _():
        start_second()

    rb.wait_recv()
    add_main(left)
    la.wait_recv()
    add_main(right)

    settle(gz.at[pl.ds(0, NZ - 1)], st_recv.at[1])
    total = gz[0]
    for q in range(1, NZ):
        total = total + gz[q]
    mine = rows_of(pair, PIECE)
    gf[mine, :] = total
    to_pairs(lambda q: gf.at[mine], lambda n: gf.at[mine], 2)

    @pl.when(z > 0)
    def _():
        settle(p1s, st_recv.at[5])

    p1f[mine, :] = p1s[...]
    to_pairs(lambda q: p1f.at[mine], lambda n: p1f.at[mine], 6)

    others = pl.ds(0, (PAIRS - 1) * PIECE)
    settle(gf.at[others], st_recv.at[2])
    work[...] = gf[...]
    loop(0, width // BLK, lambda k: chol_step(k, work, upper))
    outs.append(pltpu.make_async_copy(upper, upper_out, out_sem.at[len(outs)]))
    outs[-1].start()
    @pl.when(space == 0)
    def _():
        m_loc[0] += jnp.dot(tv[0, :, 0:width], upper[...], precision=HIGHEST,
                            preferred_element_type=F32)

    for swap in swaps:
        swap.wait_recv()
    others_t = jnp.concatenate([tb[right], tb[far], tb[left]], axis=0)
    swapped = products(others_t, gat[y, :, main:part])
    for r in range(1, NY):
        m_loc[r] = swapped[(r - 1) * rows:r * rows, :]
    fa.wait_recv()
    fb.wait_recv()
    add_main(far)

    for n, (dx, dc, dy) in enumerate(plane_order):
        q = pair_at(dx, dc)
        send(m_loc.at[dy, rows_of(q, BLK)], pm.at[n], 7, (at_pair(q)[0], (y + dy) % NY))

    @pl.when(early)
    def _():
        forward_second()

    @pl.when(jnp.logical_not(early))
    def _():
        start_second()

    settle(p1f.at[others], st_recv.at[6])
    work[...] = gf[...] + jnp.dot(p1f[...], upper[...], precision=HIGHEST, preferred_element_type=F32)
    work_t[...] = work[...].T
    loop(0, MIDDLE, lambda k: inverse_step(k, work, work_t))
    settle(pm, st_recv.at[7])
    tile = rows_of(pair, BLK)
    total = m_loc[0, tile, :]
    for d in range(PLANE - 1):
        total = total + pm[d]
    mz[z] = total
    to_z(mz.at[z], 8)
    loop(MIDDLE, width // BLK, lambda k: inverse_step(k, work, work_t))

    @pl.when(jnp.logical_not(early))
    def _():
        forward_second()

    settle(mz.at[pl.ds(0, NZ - 1)], st_recv.at[8])
    total = mz[0]
    for q in range(1, NZ):
        total = total + mz[q]
    zsum[tile, :] = jnp.dot(total, work[...], precision=HIGHEST, preferred_element_type=F32)
    to_pairs(lambda q: zsum.at[tile], lambda n: zsum.at[tile], 9)
    rb_b.wait_recv()
    put_out(left, cols_b)
    la_b.wait_recv()
    put_out(right, cols_b)
    fa_b.wait_recv()
    fb_b.wait_recv()
    put_out(far, cols_b)
    settle(zsum.at[pl.ds(0, (PAIRS - 1) * BLK)], st_recv.at[9])
    zt[...] = zsum[...]

    for copy in (ra, lb, rb, la, fa, fb, *swaps, ra_b0, lb_b0, ra_b, lb_b, rb_b, la_b, fa_b, fb_b):
        copy.wait_send()
    for copy in outs:
        copy.wait()
    settle(pr, st_send.at[0])
    settle(gz.at[pl.ds(0, NZ - 1)], st_send.at[1])
    settle(gf.at[others], st_send.at[2])

    @pl.when(root)
    def _():
        for d in range(1, NY):
            settle(p1w, p1_send.at[d - 1])

    @pl.when(space == 0)
    def _():
        settle(gf.at[others], st_send.at[4])

    @pl.when(z == 0)
    def _():
        settle(gz.at[pl.ds(0, NZ - 1)], st_send.at[5])

    settle(gf.at[others], st_send.at[6])
    settle(pm, st_send.at[7])
    settle(mz.at[pl.ds(0, NZ - 1)], st_send.at[8])
    settle(zsum.at[pl.ds(0, (PAIRS - 1) * BLK)], st_send.at[9])
    settle(yr.at[pl.ds(0, NY - 1)], st_send.at[10])


def update_kernel(scale, p_ref, t_ref, zt_ref, upper_ref, up_ref, out_ref, up, new, out_sem):
    up[...] = upper_ref[...] * scale
    copies = [pltpu.make_async_copy(up, up_ref, out_sem.at[NY])]
    copies[0].start()
    zt = zt_ref[...]
    rows, width = zt.shape
    part = p_ref.shape[2]
    zh, zl = split2(zt)
    quad = jnp.concatenate([jnp.concatenate([zh, zh], axis=1),
                            jnp.concatenate([zl, zl], axis=1)], axis=0)
    for c in range(NY):
        cols = pl.ds(c * part, part)
        ph, pl_ = split2(p_ref[c])
        both = jnp.dot(quad, jnp.concatenate([ph, pl_], axis=0), preferred_element_type=F32)
        new[c] = t_ref[:, cols] - (both[:rows] + both[rows:])
        if c == 0:
            @pl.when(lax.axis_index("space") == 0)
            def _():
                new[0, :, 0:width] -= lax.dot_general(
                    zt, upper_ref[...], (((1,), (1,)), ((), ())), precision=HIGHEST,
                    preferred_element_type=F32)
        copy = pltpu.make_async_copy(new.at[c], out_ref.at[:, cols], out_sem.at[c])
        copy.start()
        copies.append(copy)
    for copy in copies:
        copy.wait()


def per_device(panel, trailing):
    width, part = panel.shape
    rows, block = trailing.shape
    tail = part // LANES * 7 // 15 * LANES
    rows_total = block * lax.axis_size("space")
    vmem = pl.BlockSpec(memory_space=pltpu.VMEM)
    hbm = pl.BlockSpec(memory_space=pltpu.HBM)
    anywhere = pl.BlockSpec(memory_space=pl.ANY)

    def buf(*shape):
        return pltpu.VMEM(shape, F32)

    gat, upper, zt = pl.pallas_call(
        main_kernel,
        out_shape=(
            jax.ShapeDtypeStruct((NY, width, part), F32),
            jax.ShapeDtypeStruct((width, width), F32),
            jax.ShapeDtypeStruct((rows, width), F32),
        ),
        in_specs=[hbm, hbm],
        out_specs=(anywhere, anywhere, vmem),
        scratch_shapes=[
            buf(NY, width, part),
            buf(NY, rows, part),
            buf(NY, rows, tail),
            buf(width, width),
            buf(PAIRS - 1, PIECE, width),
            buf(NY, PIECE, width),
            buf(NZ, PIECE, width),
            buf(width, width),
            buf(width, width),
            buf(PIECE, width),
            buf(width, width),
            buf(width, width),
            buf(NY, rows, width),
            buf(PLANE - 1, BLK, width),
            buf(NZ, BLK, width),
            buf(rows, width),
            buf(width, width),
            buf(width, width),
            pltpu.SemaphoreType.DMA((17,)),
            pltpu.SemaphoreType.DMA((17,)),
            pltpu.SemaphoreType.DMA((1 + NY,)),
            pltpu.SemaphoreType.DMA((2 * NY,)),
            pltpu.SemaphoreType.DMA((11,)),
            pltpu.SemaphoreType.DMA((11,)),
            pltpu.SemaphoreType.DMA((NY - 1,)),
            pltpu.SemaphoreType.REGULAR((5,)),
        ],
        compiler_params=pltpu.CompilerParams(
            collective_id=0, has_side_effects=True, vmem_limit_bytes=40 * 2**20),
        name="reduce_factor",
    )(pltpu.with_memory_space_constraint(panel, pltpu.HBM),
      pltpu.with_memory_space_constraint(trailing, pltpu.HBM))

    upper_factor, updated = pl.pallas_call(
        functools.partial(update_kernel, -1.0 / math.sqrt(rows_total)),
        out_shape=(
            jax.ShapeDtypeStruct((width, width), F32),
            jax.ShapeDtypeStruct((rows, block), F32),
        ),
        in_specs=[vmem] * 4,
        out_specs=(hbm, hbm),
        scratch_shapes=[
            buf(width, width), buf(NY, rows, part), pltpu.SemaphoreType.DMA((NY + 1,))],
        compiler_params=pltpu.CompilerParams(vmem_limit_bytes=40 * 2**20),
        name="apply_update",
    )(gat, trailing, zt, upper)
    return (upper_factor, updated)


def solution(mesh):
    return jax.shard_map(
        per_device,
        mesh=mesh,
        in_specs=(P(None, ("space", "col")), P("col", "space")),
        out_specs=(P(), P("col", "space")),
        check_vma=False,
    )
```

```python
import functools
import math

import jax
import jax.numpy as jnp
from jax import lax
from jax.experimental import pallas as pl
from jax.experimental.pallas import tpu as pltpu
from jax.sharding import PartitionSpec as P

F32 = jnp.float32
BF16 = jnp.bfloat16
HIGHEST = lax.Precision.HIGHEST
MESH = pl.DeviceIdType.MESH
NX, NZ, NCORE, NY = 4, 16, 2, 4
PAIRS = NX * NCORE
BLK = 8
LANES = 128
PIECE = 16
EARLY, MIDDLE = 5, 12
PLANE = PAIRS * NY


def split2(x):
    high = x.astype(BF16)
    low = (x - high.astype(F32)).astype(BF16)
    return high, low


def split3(x):
    high = x.astype(BF16).astype(F32)
    rest = x - high
    mid = rest.astype(BF16).astype(F32)
    return high, mid, rest - mid


def stacks(a, b):
    ah, am, al = split3(a)
    bh, bm, bl = split3(b)
    left = jnp.concatenate([ah, ah, ah, am, am, al], axis=0).astype(BF16)
    right = jnp.concatenate([bh, bm, bl, bh, bm, bh], axis=0).astype(BF16)
    return left, right


def dot_tn(a, b):
    return lax.dot_general(a, b, (((0,), (0,)), ((), ())), preferred_element_type=F32)


def dot_nt(a, b):
    return lax.dot_general(a, b, (((1,), (1,)), ((), ())), preferred_element_type=F32)


def recip(x):
    y = pl.reciprocal(x, approx=True)
    return y * (2.0 - x * y)


def lane_splat(x, lane):
    return jnp.take_along_axis(x, jnp.full(x.shape, lane, jnp.int32), axis=1)


def merge(rows, row8):
    out = rows[0]
    for i in range(1, len(rows)):
        out = jnp.where(row8 == i, rows[i], out)
    return out


def block_rows(ref, base):
    width = ref.shape[1]
    return [jnp.broadcast_to(ref[pl.ds(base + i, 1), :], (BLK, width)) for i in range(BLK)]


def chol_step(k, work, upper):
    width = work.shape[1]
    row8 = lax.broadcasted_iota(jnp.int32, (BLK, width), 0)
    lane8 = lax.broadcasted_iota(jnp.int32, (BLK, width), 1)
    base = pl.multiple_of(k * BLK, BLK)
    rows = block_rows(work, base)
    s = {(i, j): lane_splat(rows[i], base + j) for i in range(BLK) for j in range(i, BLK)}
    for j in range(BLK):
        inv = recip(s[j, j])
        for i in range(j + 1, BLK):
            factor = s[j, i] * inv
            for l in range(i, BLK):
                s[i, l] = s[i, l] - factor * s[j, l]
            rows[i] = rows[i] - factor * rows[j]
    pivots = merge([s[j, j] for j in range(BLK)], row8)
    block = merge(rows, row8) * lax.rsqrt(pivots)
    block = jnp.where(lane8 >= row8 + base, block, 0.0)
    upper[pl.ds(base, BLK), :] = block
    left, right = stacks(block, block)
    work[...] -= dot_tn(left, right)


def inverse_step(k, mat, mat_t):
    width = mat.shape[1]
    row8 = lax.broadcasted_iota(jnp.int32, (BLK, width), 0)
    lane8 = lax.broadcasted_iota(jnp.int32, (BLK, width), 1)
    base = pl.multiple_of(k * BLK, BLK)
    rows = block_rows(mat, base)
    cols = mat_t[pl.ds(base, BLK), :]
    s = {(i, j): lane_splat(rows[i], base + j) for i in range(BLK) for j in range(BLK)}
    for j in range(BLK):
        inv = recip(s[j, j])
        at = lane8 == base + j
        scaled = jnp.where(at, 1.0, rows[j]) * inv
        for l in range(j + 1, BLK):
            s[j, l] = s[j, l] * inv
        for i in range(BLK):
            if i == j:
                continue
            for l in range(j + 1, BLK):
                s[i, l] = s[i, l] - s[i, j] * s[j, l]
            rows[i] = jnp.where(at, 0.0, rows[i]) - s[i, j] * scaled
        rows[j] = scaled
    block = merge(rows, row8)
    inside = (lane8 >= base) & (lane8 < base + BLK)
    cols = jnp.where(inside, jnp.where(lane8 == row8 + base, -1.0, 0.0), cols)
    left, right = stacks(cols, block)
    row_id = lax.broadcasted_iota(jnp.int32, (width, width), 0)
    lane_id = lax.broadcasted_iota(jnp.int32, (width, width), 1)
    row_out = (row_id < base) | (row_id >= base + BLK)
    lane_out = (lane_id < base) | (lane_id >= base + BLK)
    keep = row_out & lane_out
    mat[...] = jnp.where(keep, mat[...], 0.0) - dot_tn(left, right)
    mat_t[...] = jnp.where(keep, mat_t[...], 0.0) - dot_tn(right, left)


def main_kernel(p_hbm, t_hbm, gat_out, upper_out, zt,
                gat, tv, tb, g_loc, pr, yr, gz, gf, p1w, p1s, p1f, upper, m_loc, pm, mz, zsum, work, work_t,
                gp_send, gp_recv, loc, out_sem, st_send, st_recv, p1_send, ready):
    width, part = p_hbm.shape
    half = width // 2
    rows = t_hbm.shape[0]
    tail = tb.shape[2]
    main = part - tail
    space = lax.axis_index("space")
    y = lax.axis_index("col")
    core = space % NCORE
    z = (space // NCORE) % NZ
    x = space // (NCORE * NZ)
    pair = x * NCORE + core
    right, left, far = (y + 1) % NY, (y + NY - 1) % NY, (y + 2) % NY
    root = (space == 0) & (y == 0)

    z_order = sorted(range(1, NZ), key=lambda d: -min(d, NZ - d))
    plane_order = sorted(
        ((dx, dc, dy) for dx in range(NX) for dc in range(NCORE) for dy in range(NY)),
        key=lambda d: -(min(d[0], NX - d[0]) + d[1] + min(d[2], NY - d[2])))[:-1]
    pair_order = [(dx, dc) for dx, dc, dy in plane_order if dy == 0]

    def pair_at(dx, dc):
        return ((x + dx) % NX) * NCORE + (core + dc) % NCORE

    def to_pairs(src, dst, stage):
        for n, (dx, dc) in enumerate(pair_order):
            q = pair_at(dx, dc)
            send(src(q), dst(n), stage, at_pair(q))

    def to_z(ref, stage):
        for d in z_order:
            send(ref, ref, stage, at_z((z + d) % NZ))

    def at_z(zz):
        return (x * (NZ * NCORE) + zz * NCORE + core, y)

    def at_y(yy):
        return (space, yy)

    def at_pair(q):
        return ((q // NCORE) * (NZ * NCORE) + z * NCORE + q % NCORE, y)

    def loop(low, high, body):
        lax.fori_loop(low, high, lambda i, c: (body(i), c)[1], 0)

    def send(src, dst, stage, device):
        pltpu.make_async_remote_copy(
            src_ref=src, dst_ref=dst, send_sem=st_send.at[stage], recv_sem=st_recv.at[stage],
            device_id=device, device_id_type=MESH).start()

    def settle(ref, sem):
        pltpu.make_async_copy(ref, ref, sem).wait()

    def rows_of(i, size):
        return pl.ds(pl.multiple_of(i * size, size), size)

    barrier = pltpu.get_barrier_semaphore()

    def greet(device):
        pl.semaphore_signal(barrier, inc=1, device_id=device, device_id_type=MESH)

    own = pltpu.make_async_copy(p_hbm, gat.at[y], loc.at[0])
    own.start()
    greet(at_z((z + 1) % NZ))
    greet(at_z((z + NZ - 1) % NZ))
    for step in (1, NY - 1):
        greet(at_y((y + step) % NY))
    near = [(0, 1), (1, 0), (NX - 1, 0), (1, 1), (NX - 1, 1)]
    for dx, dc in near:
        greet(at_pair(pair_at(dx, dc)))
    pl.semaphore_wait(barrier, 4 + len(near))

    def announce(level, one, other):
        for device in (one, other):
            pl.semaphore_signal(ready.at[level], inc=1, device_id=device, device_id_type=MESH)

    def announce_z(level, step):
        announce(level, at_z((z + step) % NZ), at_z((z + NZ - step) % NZ))

    announce(3, at_pair(pair_at(1, 0)), at_pair(pair_at(NX - 1, 0)))
    announce(4, at_y(right), at_y(left))
    announce_z(0, 1)

    def gather_copy(src, dst, index, target):
        return pltpu.make_async_remote_copy(
            src_ref=src, dst_ref=dst, send_sem=gp_send.at[index], recv_sem=gp_recv.at[index],
            device_id=(space, target), device_id_type=MESH)

    def share(start, size, cols, index, target):
        lines = pl.ds(start, size)
        copy = gather_copy(p_hbm.at[lines, cols], gat.at[y, lines, cols], index, target)
        copy.start()
        return copy

    def forward(block, lines, cols, index, target):
        ref = gat.at[block, lines, cols]
        copy = gather_copy(ref, ref, index, target)
        copy.start()
        return copy

    first, second = pl.ds(0, half), pl.ds(half, half)
    cols_a, cols_b = pl.ds(0, main), pl.ds(main, tail)
    ra = share(0, half, cols_a, 0, right)
    lb = share(half, half, cols_a, 1, left)
    own.wait()
    high, low = split2(gat[y])
    both = dot_nt(high, jnp.concatenate([high, low], axis=0))
    cross = both[:, width:]
    g_loc[...] = both[:, :width] + cross + cross.T
    pl.semaphore_wait(ready.at[3], 2)
    to_pairs(lambda q: g_loc.at[rows_of(q, PIECE)], lambda n: pr.at[n], 0)
    pl.semaphore_wait(ready.at[0], 2)
    announce_z(1, 2)
    pl.semaphore_wait(ready.at[4], 2)

    @pl.when(root)
    def _():
        for d in range(1, NY):
            pltpu.make_async_remote_copy(
                src_ref=gat.at[0, :, pl.ds(0, width)], dst_ref=p1w, send_sem=p1_send.at[d - 1],
                recv_sem=st_recv.at[3], device_id=at_y(d), device_id_type=MESH).start()
        p1w[...] = gat[0, :, 0:width]

    settle(pr, st_recv.at[0])
    total = g_loc[rows_of(pair, PIECE), :]
    for d in range(PAIRS - 1):
        total = total + pr[d]
    yr[y] = total
    loop(1, NY, lambda d: send(yr.at[y], yr.at[y], 10, at_y((y + d) % NY)))
    rb = share(half, half, cols_a, 2, right)
    la = share(0, half, cols_a, 3, left)
    swaps = []
    for index, target in ((8, right), (9, left), (10, far)):
        cols = pl.ds(pl.multiple_of(target * part + main, LANES), tail)
        swaps.append(gather_copy(t_hbm.at[:, cols], tb.at[y], index, target))
        swaps[-1].start()
    loads = [pltpu.make_async_copy(t_hbm.at[:, pl.ds(c * part, part)], tv.at[c], loc.at[1 + c])
             for c in range(NY)]
    for load in loads:
        load.start()
    pl.semaphore_wait(ready.at[1], 2)
    announce_z(2, 4)
    settle(yr.at[pl.ds(0, NY - 1)], st_recv.at[10])
    total = yr[0]
    for q in range(1, NY):
        total = total + yr[q]
    gz[z] = total
    pl.semaphore_wait(ready.at[2], 2)
    to_z(gz.at[z], 1)

    @pl.when((space == 0) & (y > 0))
    def _():
        settle(p1w, st_recv.at[3])

    @pl.when(space == 0)
    def _():
        loop(1, PAIRS, lambda q: send(p1w.at[rows_of(q, PIECE)], p1s, 4, at_pair(q)))
        p1s[...] = p1w[0:PIECE, :]

    @pl.when((z == 0) & (pair > 0))
    def _():
        settle(p1s, st_recv.at[4])

    @pl.when(z == 0)
    def _():
        loop(1, NZ, lambda d: send(p1s, p1s, 5, at_z(d)))

    for load in loads:
        load.wait()

    def products(trail, block):
        ph, pl_ = split2(block)
        th, tl = split2(trail)
        four = dot_nt(jnp.concatenate([th, tl], axis=0), jnp.concatenate([ph, pl_], axis=0))
        n = th.shape[0]
        return (four[:n, :width] + four[n:, :width]) + (four[:n, width:] + four[n:, width:])

    outs = []

    def put_out(c, cols):
        copy = pltpu.make_async_copy(gat.at[c, :, cols], gat_out.at[c, :, cols],
                                     out_sem.at[len(outs)])
        copy.start()
        outs.append(copy)

    def add_main(c):
        m_loc[0] += products(tv[c, :, 0:main], gat[c, :, 0:main])
        put_out(c, cols_a)

    m_loc[0] = products(tv[y], gat[y])
    put_out(y, pl.ds(0, part))

    ra.wait_recv()
    fa = forward(left, first, cols_a, 4, right)
    lb.wait_recv()
    fb = forward(right, second, cols_a, 5, left)
    fill = 32
    ra_b0 = share(0, fill, cols_b, 6, right)
    lb_b0 = share(half, fill, cols_b, 7, left)

    settle(gz.at[pl.ds(0, NZ - 1)], st_recv.at[1])
    total = gz[0]
    for q in range(1, NZ):
        total = total + gz[q]
    mine = rows_of(pair, PIECE)
    gf[mine, :] = total
    to_pairs(lambda q: gf.at[mine], lambda n: gf.at[mine], 2)

    @pl.when(z > 0)
    def _():
        settle(p1s, st_recv.at[5])

    p1f[mine, :] = p1s[...]
    to_pairs(lambda q: p1f.at[mine], lambda n: p1f.at[mine], 6)

    others = pl.ds(0, (PAIRS - 1) * PIECE)
    settle(gf.at[others], st_recv.at[2])
    work[...] = gf[...]
    loop(0, width // BLK, lambda k: chol_step(k, work, upper))
    outs.append(pltpu.make_async_copy(upper, upper_out, out_sem.at[len(outs)]))
    outs[-1].start()
    rb.wait_recv()
    add_main(left)
    la.wait_recv()
    add_main(right)
    settle(p1f.at[others], st_recv.at[6])
    work[...] = gf[...] + jnp.dot(p1f[...], upper[...], precision=HIGHEST, preferred_element_type=F32)
    work_t[...] = work[...].T
    loop(0, EARLY, lambda k: inverse_step(k, work, work_t))

    @pl.when(space == 0)
    def _():
        m_loc[0] += jnp.dot(tv[0, :, 0:width], upper[...], precision=HIGHEST,
                            preferred_element_type=F32)

    for swap in swaps:
        swap.wait_recv()
    others_t = jnp.concatenate([tb[right], tb[far], tb[left]], axis=0)
    swapped = products(others_t, gat[y, :, main:part])
    for r in range(1, NY):
        m_loc[r] = swapped[(r - 1) * rows:r * rows, :]
    fa.wait_recv()
    fb.wait_recv()
    add_main(far)

    for n, (dx, dc, dy) in enumerate(plane_order):
        q = pair_at(dx, dc)
        send(m_loc.at[dy, rows_of(q, BLK)], pm.at[n], 7, (at_pair(q)[0], (y + dy) % NY))
    ra_b = share(fill, half - fill, cols_b, 11, right)
    lb_b = share(half + fill, half - fill, cols_b, 12, left)
    rb_b = share(half, half, cols_b, 13, right)
    la_b = share(0, half, cols_b, 14, left)
    loop(EARLY, MIDDLE, lambda k: inverse_step(k, work, work_t))
    settle(pm, st_recv.at[7])
    tile = rows_of(pair, BLK)
    total = m_loc[0, tile, :]
    for d in range(PLANE - 1):
        total = total + pm[d]
    mz[z] = total
    to_z(mz.at[z], 8)
    loop(MIDDLE, width // BLK, lambda k: inverse_step(k, work, work_t))
    ra_b0.wait_recv()
    ra_b.wait_recv()
    fa_b = forward(left, first, cols_b, 15, right)
    lb_b0.wait_recv()
    lb_b.wait_recv()
    fb_b = forward(right, second, cols_b, 16, left)
    settle(mz.at[pl.ds(0, NZ - 1)], st_recv.at[8])
    total = mz[0]
    for q in range(1, NZ):
        total = total + mz[q]
    zsum[tile, :] = jnp.dot(total, work[...], precision=HIGHEST, preferred_element_type=F32)
    to_pairs(lambda q: zsum.at[tile], lambda n: zsum.at[tile], 9)
    rb_b.wait_recv()
    put_out(left, cols_b)
    la_b.wait_recv()
    put_out(right, cols_b)
    fa_b.wait_recv()
    fb_b.wait_recv()
    put_out(far, cols_b)
    settle(zsum.at[pl.ds(0, (PAIRS - 1) * BLK)], st_recv.at[9])
    zt[...] = zsum[...]

    for copy in (ra, lb, rb, la, fa, fb, *swaps, ra_b0, lb_b0, ra_b, lb_b, rb_b, la_b, fa_b, fb_b):
        copy.wait_send()
    for copy in outs:
        copy.wait()
    settle(pr, st_send.at[0])
    settle(gz.at[pl.ds(0, NZ - 1)], st_send.at[1])
    settle(gf.at[others], st_send.at[2])

    @pl.when(root)
    def _():
        for d in range(1, NY):
            settle(p1w, p1_send.at[d - 1])

    @pl.when(space == 0)
    def _():
        settle(gf.at[others], st_send.at[4])

    @pl.when(z == 0)
    def _():
        settle(gz.at[pl.ds(0, NZ - 1)], st_send.at[5])

    settle(gf.at[others], st_send.at[6])
    settle(pm, st_send.at[7])
    settle(mz.at[pl.ds(0, NZ - 1)], st_send.at[8])
    settle(zsum.at[pl.ds(0, (PAIRS - 1) * BLK)], st_send.at[9])
    settle(yr.at[pl.ds(0, NY - 1)], st_send.at[10])


def update_kernel(scale, p_ref, t_ref, zt_ref, upper_ref, up_ref, out_ref, up, new, out_sem):
    up[...] = upper_ref[...] * scale
    copies = [pltpu.make_async_copy(up, up_ref, out_sem.at[NY])]
    copies[0].start()
    zt = zt_ref[...]
    rows, width = zt.shape
    part = p_ref.shape[2]
    zh, zl = split2(zt)
    quad = jnp.concatenate([jnp.concatenate([zh, zh], axis=1),
                            jnp.concatenate([zl, zl], axis=1)], axis=0)
    for c in range(NY):
        cols = pl.ds(c * part, part)
        ph, pl_ = split2(p_ref[c])
        both = jnp.dot(quad, jnp.concatenate([ph, pl_], axis=0), preferred_element_type=F32)
        new[c] = t_ref[:, cols] - (both[:rows] + both[rows:])
        if c == 0:
            @pl.when(lax.axis_index("space") == 0)
            def _():
                new[0, :, 0:width] -= lax.dot_general(
                    zt, upper_ref[...], (((1,), (1,)), ((), ())), precision=HIGHEST,
                    preferred_element_type=F32)
        copy = pltpu.make_async_copy(new.at[c], out_ref.at[:, cols], out_sem.at[c])
        copy.start()
        copies.append(copy)
    for copy in copies:
        copy.wait()


def per_device(panel, trailing):
    width, part = panel.shape
    rows, block = trailing.shape
    tail = part // LANES * 2 // 5 * LANES
    rows_total = block * lax.axis_size("space")
    vmem = pl.BlockSpec(memory_space=pltpu.VMEM)
    hbm = pl.BlockSpec(memory_space=pltpu.HBM)
    anywhere = pl.BlockSpec(memory_space=pl.ANY)

    def buf(*shape):
        return pltpu.VMEM(shape, F32)

    gat, upper, zt = pl.pallas_call(
        main_kernel,
        out_shape=(
            jax.ShapeDtypeStruct((NY, width, part), F32),
            jax.ShapeDtypeStruct((width, width), F32),
            jax.ShapeDtypeStruct((rows, width), F32),
        ),
        in_specs=[hbm, hbm],
        out_specs=(anywhere, anywhere, vmem),
        scratch_shapes=[
            buf(NY, width, part),
            buf(NY, rows, part),
            buf(NY, rows, tail),
            buf(width, width),
            buf(PAIRS - 1, PIECE, width),
            buf(NY, PIECE, width),
            buf(NZ, PIECE, width),
            buf(width, width),
            buf(width, width),
            buf(PIECE, width),
            buf(width, width),
            buf(width, width),
            buf(NY, rows, width),
            buf(PLANE - 1, BLK, width),
            buf(NZ, BLK, width),
            buf(rows, width),
            buf(width, width),
            buf(width, width),
            pltpu.SemaphoreType.DMA((17,)),
            pltpu.SemaphoreType.DMA((17,)),
            pltpu.SemaphoreType.DMA((1 + NY,)),
            pltpu.SemaphoreType.DMA((2 * NY,)),
            pltpu.SemaphoreType.DMA((11,)),
            pltpu.SemaphoreType.DMA((11,)),
            pltpu.SemaphoreType.DMA((NY - 1,)),
            pltpu.SemaphoreType.REGULAR((5,)),
        ],
        compiler_params=pltpu.CompilerParams(
            collective_id=0, has_side_effects=True, vmem_limit_bytes=40 * 2**20),
        name="reduce_factor",
    )(pltpu.with_memory_space_constraint(panel, pltpu.HBM),
      pltpu.with_memory_space_constraint(trailing, pltpu.HBM))

    upper_factor, updated = pl.pallas_call(
        functools.partial(update_kernel, -1.0 / math.sqrt(rows_total)),
        out_shape=(
            jax.ShapeDtypeStruct((width, width), F32),
            jax.ShapeDtypeStruct((rows, block), F32),
        ),
        in_specs=[vmem] * 4,
        out_specs=(hbm, hbm),
        scratch_shapes=[
            buf(width, width), buf(NY, rows, part), pltpu.SemaphoreType.DMA((NY + 1,))],
        compiler_params=pltpu.CompilerParams(vmem_limit_bytes=40 * 2**20),
        name="apply_update",
    )(gat, trailing, zt, upper)
    return (upper_factor, updated)


def solution(mesh):
    return jax.shard_map(
        per_device,
        mesh=mesh,
        in_specs=(P(None, ("space", "col")), P("col", "space")),
        out_specs=(P(), P("col", "space")),
        check_vma=False,
    )
```
